128 devices in a mesh: sub: 32 (over x, z, core), crs: 4 (over y).
Axes of the slice: x: 4, y: 4, z: 4, core: 2. Of those that a mesh axis runs over, the one named last changes fastest.
Arguments:
- face_index: int32 [128, 4, 147], P(('sub', 'crs')), may hold values from 0 to 1214, as said below
- kinv: float32 [128, 1215, 1215], P(('sub', 'crs')), as said below
- schur: float32 [128, 588, 588], P(('sub', 'crs'))
- corner: float32 [128, 1215, 24], P(('sub', 'crs')), may hold values from -0.3125 to 0.3125
- coarse_inverse: float32 [744, 744], P('crs')
- loads: float32 [128, 1215, 512], P(('sub', 'crs')), may hold values from -6 to 6
Outputs:
- multipliers: float32 [128, 4, 147, 512], P(('sub', 'crs'))
- residual: float32 [128, 4, 147, 512], P(('sub', 'crs'))
The draws below stay inside these ranges and needn't reach their ends.
Inputs may be any that keep to these rules, and one draw needn't show every extreme that they name: `face_index`: the 588 entries of one subdomain are distinct rows of its 1215 interface unknowns. kinv, schur and coarse_inverse are symmetric positive definite.
All inputs are finite; a program needn't handle non-finite values.
Results may differ from the reference program's by a relative error of at most 0.0003.
Values sent between devices are 32-bit elements; how exact they have to be, the bound alone decides.
A program may use at most 128 MiB of HBM per device.

```python
import math
import jax
import jax.numpy as jnp
from jax import lax

NR = 1215
FD = 147
CASES = 512
ITERS = 2
SUBS = 128
NC = 744
N_SUB = 32
N_CRS = 4


def symmetric_block(key, count, order, top):
    first, second, third = jax.random.split(key, 3)
    raw = jax.random.uniform(first, (count, order, order), jnp.float32, -1.0, 1.0)
    sym = (raw + jnp.swapaxes(raw, 1, 2)) * (0.3 / math.sqrt(order))
    diag = jax.random.uniform(second, (count, order), jnp.float32, 1.0, 1.5)
    scale = jnp.exp(jax.random.uniform(third, (count, order), jnp.float32, 0.0, math.log(top)))
    eye = jnp.eye(order, dtype=jnp.float32)
    mat = sym + diag[:, :, None] * eye[None]
    return mat * scale[:, :, None] * scale[:, None, :]


def draw_face_index(key, part):
    key = jax.random.fold_in(key, 5)
    keys = jax.random.split(key, SUBS)
    perms = jax.vmap(lambda k: jax.random.permutation(k, NR))(keys)
    return perms[:, :4 * FD].reshape(SUBS, 4, FD).astype(jnp.int32)


def draw_kinv(key, part):
    key = jax.random.fold_in(key, 1)
    return symmetric_block(key, SUBS, NR, 2.0)


def draw_schur(key, part):
    key = jax.random.fold_in(key, 2)
    return symmetric_block(key, SUBS, 4 * FD, 2.0)


def draw_coarse_inverse(key, part):
    key = jax.random.fold_in(key, 3)
    return symmetric_block(key, 1, NC, 2.0)[0]


def level_of(rng, dims, shards, low, top_value):
    factor_of, own = 1.0, jax.random.fold_in(rng, 6)
    for position, parts in shards:
        steps = jnp.exp(jax.random.uniform(jax.random.fold_in(own, position), (parts,), jnp.float32, low / len(shards), top_value / len(shards)))
        factor_of = factor_of * jnp.repeat(steps, dims[position] // parts).reshape([-1 if axis == position else 1 for axis in range(len(dims))])
    return factor_of


def centred(rng, extent, width, limit, pieces=(), kind=jnp.bfloat16):
    drawn = width * jax.random.normal(rng, extent, jnp.float32)
    if pieces:
        drawn = drawn * level_of(rng, extent, pieces, -0.22, 0.18)
    return jnp.clip(drawn, -limit, limit).astype(kind)


def setup_inputs(seed: int = 0) -> dict:
    arg_keys = jax.random.split(jax.random.key(seed), 7)
    return {
        "face_index": draw_face_index(jax.random.fold_in(arg_keys[6], 71), 0),
        "kinv": draw_kinv(jax.random.fold_in(arg_keys[6], 71), 0),
        "schur": draw_schur(jax.random.fold_in(arg_keys[6], 71), 0),
        "corner": centred(arg_keys[3], (SUBS, NR, 24), (NR // 4) ** -0.5, 0.3125, ((0, 128),), jnp.float32),
        "coarse_inverse": draw_coarse_inverse(jax.random.fold_in(arg_keys[6], 71), 0),
        "loads": centred(arg_keys[5], (SUBS, NR, CASES), 1.0, 6.0, ((0, 128),), jnp.float32),
    }


def signs():
    return jnp.array([-1.0, 1.0, -1.0, 1.0], jnp.float32)[None, :, None, None]


def keep_mask():
    arow = jnp.arange(SUBS, dtype=jnp.int32) // N_CRS
    first = jnp.where(arow > 0, 1.0, 0.0)
    second = jnp.where(arow < N_SUB - 1, 1.0, 0.0)
    ones = jnp.ones((SUBS,), jnp.float32)
    return jnp.stack([first, second, ones, ones], axis=1).astype(jnp.float32)[:, :, None, None]


def corner_map():
    sidx = jnp.arange(SUBS, dtype=jnp.int32)
    arow = sidx // N_CRS
    bcol = sidx % N_CRS
    local = jnp.arange(24, dtype=jnp.int32)
    which = local // 3
    comp = local % 3
    da = which // 4
    db = (which // 2) % 2
    dz = which % 2
    apos = arow[:, None] + da[None, :]
    bpos = (bcol[:, None] + db[None, :]) % N_CRS
    dof = 3 * (2 * ((apos - 1) * N_CRS + bpos) + dz[None, :]) + comp[None, :]
    valid = (apos >= 1) & (apos <= N_SUB - 1)
    cols = jnp.arange(NC, dtype=jnp.int32)
    hit = valid[:, :, None] & (dof[:, :, None] == cols[None, None, :])
    return jnp.where(hit, 1.0, 0.0).astype(jnp.float32)


def pick(values, face_index):
    return jax.vmap(lambda v, i: v[i])(values, face_index)


def spread(faces, face_index):
    def one(x, i):
        return jnp.zeros((NR, CASES), jnp.float32).at[i.reshape(-1)].set(x.reshape(-1, CASES))
    return jax.vmap(one)(signs() * faces, face_index)


def jump(faces):
    grid = faces.reshape(N_SUB, N_CRS, 4, FD, CASES)
    zero = jnp.zeros_like(grid[:1])
    lower = jnp.concatenate([zero, grid[:-1]], axis=0)
    upper = jnp.concatenate([grid[1:], zero], axis=0)
    before = jnp.roll(grid, 1, axis=1)
    after = jnp.roll(grid, -1, axis=1)
    out = jnp.stack([-grid[:, :, 0] + lower[:, :, 1], grid[:, :, 1] - upper[:, :, 0],
                     -grid[:, :, 2] + before[:, :, 3], grid[:, :, 3] - after[:, :, 2]], axis=2)
    return out.reshape(SUBS, 4, FD, CASES) * keep_mask()


def coarse(values, corner, coarse_inverse, emap):
    hp = lax.Precision.HIGHEST
    local = jnp.einsum("snk,snc->skc", corner, values, precision=hp)
    total = jnp.einsum("skm,skc->mc", emap, local, precision=hp)
    solved = jnp.dot(coarse_inverse, total, precision=hp)
    back = jnp.einsum("skm,mc->skc", emap, solved, precision=hp)
    return jnp.einsum("snk,skc->snc", corner, back, precision=hp)


def reference(face_index, kinv, schur, corner, coarse_inverse, loads):
    hp = lax.Precision.HIGHEST
    emap = corner_map()

    def operator(values):
        inner_part = jnp.einsum("snm,smc->snc", kinv, values, precision=hp)
        return jump(pick(inner_part + coarse(values, corner, coarse_inverse, emap), face_index))

    def precond(resid):
        scaled = (0.5 * signs() * keep_mask() * resid).reshape(SUBS, 4 * FD, CASES)
        result = jnp.einsum("snm,smc->snc", schur, scaled, precision=hp)
        return 0.5 * jump(result.reshape(SUBS, 4, FD, CASES))

    def inner(left, right):
        return 0.5 * jnp.sum(left * right, axis=(0, 1, 2))

    residual = operator(loads)
    multipliers = jnp.zeros_like(residual)
    zvec = precond(residual)
    direction = zvec
    rz_now = inner(residual, zvec)
    for step in range(ITERS):
        image = operator(spread(direction, face_index))
        alpha = rz_now / inner(direction, image)
        multipliers = multipliers + alpha * direction
        residual = residual - alpha * image
        zvec = precond(residual)
        rz_next = inner(residual, zvec)
        direction = zvec + (rz_next / rz_now) * direction
        rz_now = rz_next
    return multipliers, residual
```

```python
import functools

import jax
import jax.numpy as jnp
from jax import lax
from jax.experimental import pallas as pl
from jax.experimental.pallas import tpu as pltpu
from jax.sharding import PartitionSpec as P

F32 = jnp.float32
BF16 = jnp.bfloat16
MESH = pl.DeviceIdType.MESH

FACE = 160
SENT = 152
NX = 4 * FACE
NA = NX + 32
ORDER = (2, 3, 0, 1)
LANES = 128


def dot(left, right):
    return jnp.dot(left, right, preferred_element_type=F32)


def dot_nt(left, right):
    return lax.dot_general(left, right, (((1,), (1,)), ((), ())), preferred_element_type=F32)


def split(value):
    high = value.astype(BF16)
    return high, (value - high.astype(F32)).astype(BF16)


def hot(cond, value=1.0):
    return jnp.where(cond, value, 0.0).astype(BF16)


def rows_of(shape):
    return lax.broadcasted_iota(jnp.int32, shape, 0)


def cols_of(shape):
    return lax.broadcasted_iota(jnp.int32, shape, 1)


def div(value, by):
    return (value * (65536 // by + 1)) >> 16


def kernel(dims, idxc, idxr, kinv, schur, corner, cinv, loads, mo, ro,
           kv, lv, cv, sv, civ, khi, klo, tail, bmat, bmt, a0hi, a0lo, lhi, llo, a3, m3, w3, x3,
           cpad, chi, clo, cip, sp, tmat, tmt, ws, wo, wr, dall, dphi, dplo,
           tb, rb, rv, dv, pbuf, p0, p1, gb, sibs, sibr, hk, hb, h3,
           rs, rr, es, er, fr,
           dsem, fsend, frecv, wsend, wrecv, csend, crecv,
           s1as, s1ar, s1bs, s1br, s2s, s2r, bs, br, s3s, s3r,
           r1s, r1r, r2s, r2r, r3s, r3r):
    nsub, ncrs, nrows, fdof, cases, ncoarse = dims
    chips = nsub // 2
    nrp = khi.shape[1]
    cblock = ncoarse // ncrs
    cbp, ncp = cip.shape
    a = lax.axis_index("sub")
    b = lax.axis_index("crs")
    k = lax.div(a, 2)
    c = lax.rem(a, 2)
    sib = 2 * k + 1 - c
    up = lax.rem(a + 1, nsub)
    down = lax.rem(a + nsub - 1, nsub)
    left = lax.rem(b + ncrs - 1, ncrs)
    right = lax.rem(b + 1, ncrs)
    dests = ((a, left), (a, right), (down, b), (up, b))
    keeps = (None, None, a > 0, a < nsub - 1)
    drains = []

    def local(src, dst, n):
        return pltpu.make_async_copy(src, dst, dsem.at[n])

    def remote(src, dst, ssem, rsem, dev):
        return pltpu.make_async_remote_copy(
            src_ref=src, dst_ref=dst, send_sem=ssem, recv_sem=rsem, device_id=dev, device_id_type=MESH)

    def settle(ref, sem):
        pltpu.make_async_copy(ref, ref, sem).wait()

    in_copies = [local(corner.at[0], cv, 0), local(cinv, civ, 1), local(loads.at[0], lv, 2),
                 local(kinv.at[0], kv, 3), local(schur.at[0], sv, 4)]
    for copy in in_copies:
        copy.start()

    barrier = pltpu.get_barrier_semaphore()
    for j in range(1, ncrs):
        pl.semaphore_signal(barrier, inc=1, device_id=(a, lax.rem(b + j, ncrs)), device_id_type=MESH)
    for j in range(ncrs):
        pl.semaphore_signal(barrier, inc=1, device_id=(up, j), device_id_type=MESH)
        pl.semaphore_signal(barrier, inc=1, device_id=(down, j), device_id_type=MESH)

    def greet(j, carry):
        pl.semaphore_signal(barrier, inc=1, device_id=(2 * lax.rem(k + j, chips) + c, b), device_id_type=MESH)
        return carry

    lax.fori_loop(1, chips, greet, 0)

    for pos in range(4):
        sign = 1.0 if pos % 2 else -1.0
        band = slice(pos * FACE, (pos + 1) * FACE)
        bmat[band, :] = hot(idxc[band, :] == cols_of((FACE, nrp)), sign)
    lane = cols_of((1, NX))
    signs = jnp.where(((lane >= FACE) & (lane < 2 * FACE)) | (lane >= 3 * FACE), 1.0, -1.0)

    def build_bmt(i, carry):
        at = pl.multiple_of(i * LANES, LANES)
        rows = rows_of((LANES, NX)) + at
        bmt[pl.ds(at, LANES), :] = jnp.where(idxr[...] == rows, signs, 0.0).astype(BF16)
        return carry

    lax.fori_loop(0, nrp // LANES, build_bmt, 0)

    for n in range(2):
        for pos in range(4):
            rb[n, pos, SENT:FACE, :] = jnp.zeros((FACE - SENT, cases), F32)
    hb[:, 96:LANES, :] = jnp.zeros((3, 32, cases), F32)
    cpad[...] = jnp.zeros(cpad.shape, F32)
    cip[...] = jnp.zeros(cip.shape, F32)
    sp[...] = jnp.zeros(sp.shape, F32)
    edge = nrp - LANES
    khi[:, edge:] = jnp.zeros((nrp, LANES), BF16)
    klo[:, edge:] = jnp.zeros((nrp, LANES), BF16)
    whole = nrows // 16 * 16
    for ref in (khi, klo, lhi, llo):
        ref[whole:, :] = jnp.zeros((nrp - whole, ref.shape[1]), BF16)
    tail[...] = jnp.zeros(tail.shape, F32)

    in_copies[0].wait()
    ncl = cv.shape[1]
    cpad[0:nrows, 0:ncl] = cv[...]
    high, low = split(cpad[...])
    chi[...] = high
    clo[...] = low
    w = rows_of((32, 1))
    pick_l = jnp.where(w < 12, w, jnp.where((w >= 16) & (w < 28), w - 4, -1))
    sel = hot(pick_l == cols_of((32, LANES)))
    a0hi[0:32, :] = dot_nt(sel, chi[...]).astype(BF16)
    a0lo[0:32, :] = dot_nt(sel, clo[...]).astype(BF16)
    bch = dot(bmat[...], chi[...]).astype(BF16)
    bcl = dot(bmat[...], clo[...]).astype(BF16)
    l = rows_of((LANES, 1))
    da = div(l, 12)
    rem12 = l - 12 * da
    db = div(rem12, 6)
    where_l = 24 * (1 + da) + 6 * lax.rem(b + db, ncrs) + rem12 - 6 * db
    where_l = jnp.where(l < 24, where_l, -1000)
    lanes = cols_of((LANES, LANES))
    emaps = [hot(where_l + off == lanes) for off in (0, 24, -24)]
    wo[...] = dot(bch, emaps[0]) + dot(bcl, emaps[0])
    ws[0:2 * FACE, :] = wo[0:2 * FACE, :]
    for pos in (2, 3):
        band = slice(pos * FACE, (pos + 1) * FACE)
        ws[band, :] = dot(bch[band], emaps[pos - 1]) + dot(bcl[band], emaps[pos - 1])
    pl.semaphore_wait(barrier, ncrs - 1 + 2 * ncrs + chips - 1)
    wcopies = [remote(ws.at[pl.ds(pos * FACE, FACE)], wr.at[pl.ds((pos ^ 1) * FACE, FACE)],
                      wsend.at[pos], wrecv.at[pos ^ 1], dests[pos]) for pos in range(4)]
    for copy in wcopies:
        copy.start()

    in_copies[1].wait()
    cip[0:cblock, 0:ncoarse] = civ[...]
    high, low = split(cip[...])
    i = cols_of((1, cbp))
    r = cblock * b + i
    plane = div(r, 24)
    base = lax.div(lax.div(cblock * b, 24), 2)
    target = 24 * ((plane >> 1) - base) + r - 24 * plane
    target = jnp.where((((plane + 1) & 1) == c) & (i < cblock), target, -1)
    pct = hot(target == rows_of((LANES, cbp)))
    x1h = dot(pct, high).astype(BF16)
    x1l = dot(pct, low).astype(BF16)
    i = rows_of((LANES, 1))
    r = 48 * k - 48 + i
    r = jnp.where((i < 120) & (r < ncoarse), r, -1)
    sel = hot(r == cols_of((LANES, ncp)))
    dall[b] = dot_nt(sel, x1h) + dot_nt(sel, x1l)
    for j in range(1, ncrs):
        remote(dall.at[b], dall.at[b], csend.at[j], crecv.at[j], (a, lax.rem(b + j, ncrs))).start()

    in_copies[2].wait()
    step = 16 * 5

    def split_loads(i, carry):
        at = pl.multiple_of(i * step, step)
        high, low = split(lv[pl.ds(at, step), :])
        lhi[pl.ds(at, step), :] = high
        llo[pl.ds(at, step), :] = low
        return carry

    lax.fori_loop(0, whole // step, split_loads, 0)
    left_rows = nrows - whole
    tail[0:left_rows, 0:cases] = lv[whole:nrows, :]
    high, low = split(tail[:, 0:cases])
    lhi[whole:whole + 16, :] = high
    llo[whole:whole + 16, :] = low

    def apply_loads(lo, hi):
        high, low = a0hi[lo:hi, :], a0lo[lo:hi, :]
        return dot(high, lhi[...]) + dot(high, llo[...]) + dot(low, lhi[...])

    t = cols_of((1, LANES))
    blk = jnp.where(t >= 64, t - 64, t)
    src_b = blk >> 4
    w = blk & 15
    db = jnp.where(w >= 6, 1, 0)
    plane_row = jnp.where(w < 12, 6 * ((src_b + db) & (ncrs - 1)) + w - 6 * db, -1)
    gather_hot = hot(plane_row == rows_of((32, LANES)))

    def coarse_begin(f):
        for j in range(1, ncrs):
            to = lax.rem(b + j, ncrs)
            at = pl.ds(pl.multiple_of(to * LANES, LANES), LANES)
            remote(pbuf.at[f, pl.ds(0, 16), at], p0.at[f, b], s1as.at[f], s1ar.at[f], (a, to)).start()
        for j in range(ncrs):
            to = lax.rem(b + j, ncrs)
            at = pl.ds(pl.multiple_of(to * LANES, LANES), LANES)
            remote(pbuf.at[f, pl.ds(16, 16), at], p1.at[f, b], s1bs.at[f], s1br.at[f], (up, to)).start()
        at = pl.ds(pl.multiple_of(b * LANES, LANES), LANES)
        p0[f, b] = pbuf[f, 0:16, at]

        def drain():
            settle(p0.at[f, pl.ds(0, ncrs - 1)], s1as.at[f])
            settle(p1.at[f], s1bs.at[f])

        drains.append(drain)

    def coarse_gather(f):
        settle(p0.at[f, pl.ds(0, ncrs - 1)], s1ar.at[f])
        settle(p1.at[f], s1br.at[f])
        pieces = jnp.concatenate([p0[f].reshape(16 * ncrs, LANES), p1[f].reshape(16 * ncrs, LANES)], axis=0)
        high, low = split(pieces)
        gb[f, k] = (dot(gather_hot, high) + dot(gather_hot, low))[0:24]

        def send(j, carry):
            to = 2 * lax.rem(k + j, chips) + c
            remote(gb.at[f, k], gb.at[f, k], s2s.at[f], s2r.at[f], (to, b)).start()
            return carry

        lax.fori_loop(1, chips, send, 0)
        drains.append(lambda: settle(gb.at[f, pl.ds(0, chips - 1)], s2s.at[f]))

    def coarse_solve(f):
        settle(gb.at[f, pl.ds(0, chips - 1)], s2r.at[f])
        high, low = split(gb[f].reshape(chips * 24, LANES))
        sibs[f, 0:LANES] = dot(dphi[...], high) + dot(dphi[...], low) + dot(dplo[...], high)
        sibs[f, LANES:LANES + 24] = gb[f, k]
        copy = remote(sibs.at[f], sibr.at[f], bs.at[f], br.at[f], (sib, b))
        copy.start()
        return copy

    def coarse_spread(f, copy):
        copy.wait()
        hk[...] = sibs[f, 0:LANES] + sibr[f, 0:LANES]
        at = pl.ds(pl.multiple_of(b * LANES, LANES), LANES)
        hb[f, 0:96, at] = hk[pl.ds(pl.multiple_of(24 * c, 8), 96), :]
        for j in range(1, ncrs):
            remote(hb.at[f, pl.ds(0, 96), at], hb.at[f, pl.ds(0, 96), at], s3s.at[f], s3r.at[f],
                   (a, lax.rem(b + j, ncrs))).start()
        drains.append(lambda: settle(hb.at[f, pl.ds(0, 96), pl.ds(0, (ncrs - 1) * LANES)], s3s.at[f]))
        mine = hk[pl.ds(pl.multiple_of(24 + 24 * c, 8), 24), :] * sibs[f, LANES:LANES + 24]
        other = hk[pl.ds(pl.multiple_of(48 - 24 * c, 8), 24), :] * sibr[f, LANES:LANES + 24]
        return jnp.sum(mine + other, axis=0, keepdims=True)

    def coarse_end(f):
        settle(hb.at[f, pl.ds(0, 96), pl.ds(0, (ncrs - 1) * LANES)], s3r.at[f])
        high, low = split(hb[f])
        h3[0:LANES, :] = high
        h3[LANES:2 * LANES, :] = low
        h3[2 * LANES:, :] = high

    def sum_begin(n):
        for cc in range(2):
            for j in range(ncrs):
                to = lax.rem(b + j, ncrs)
                at = pl.ds(pl.multiple_of(to * LANES, LANES), LANES)
                if cc == 0 and j == 0:
                    rr[n, c * ncrs + b] = rs[n, :, at]
                    continue
                dev = (a if cc == 0 else sib, to)
                remote(rs.at[n, :, at], rr.at[n, c * ncrs + b], r1s.at[n], r1r.at[n], dev).start()
        drains.append(lambda: settle(rr.at[n, pl.ds(0, 2 * ncrs - 1)], r1s.at[n]))

    def sum_chip(n):
        settle(rr.at[n, pl.ds(0, 2 * ncrs - 1)], r1r.at[n])
        return jnp.sum(rr[n], axis=0)

    def sum_gather(n, block):
        er[n, k] = block

        def send(j, carry):
            to = 2 * lax.rem(k + j, chips) + c
            remote(er.at[n, k], er.at[n, k], r2s.at[n], r2r.at[n], (to, b)).start()
            return carry

        lax.fori_loop(1, chips, send, 0)
        drains.append(lambda: settle(er.at[n, pl.ds(0, chips - 1)], r2s.at[n]))

    def sum_spread(n):
        settle(er.at[n, pl.ds(0, chips - 1)], r2r.at[n])
        at = pl.ds(pl.multiple_of(b * LANES, LANES), LANES)
        fr[n, :, at] = jnp.sum(er[n], axis=0)
        for j in range(1, ncrs):
            remote(fr.at[n, :, at], fr.at[n, :, at], r3s.at[n], r3r.at[n], (a, lax.rem(b + j, ncrs))).start()
        drains.append(lambda: settle(fr.at[n, :, pl.ds(0, (ncrs - 1) * LANES)], r3s.at[n]))

    def sum_end(n):
        settle(fr.at[n, :, pl.ds(0, (ncrs - 1) * LANES)], r3r.at[n])
        return fr[n, 0:1, :], fr[n, 1:2, :]

    def faces_start(n, which):
        copies = []
        for pos in which:
            copy = remote(tb.at[n % 2, pl.ds(pos * FACE, SENT)], rb.at[n % 2, pos ^ 1, pl.ds(0, SENT)],
                          fsend.at[n % 2, pos], frecv.at[n % 2, pos ^ 1], dests[pos])
            copy.start()
            copies.append(copy)
        return copies

    def faces_wait(copies):
        for copy in copies:
            copy.wait()

    def jumped(n, pos, extra=None):
        band = slice(pos * FACE, (pos + 1) * FACE)
        value = tb[n % 2, band, :] + rb[n % 2, pos]
        if extra is not None:
            value = value + extra
        if keeps[pos] is not None:
            value = jnp.where(keeps[pos], value, 0.0)
        return value

    def put_x(pos, value):
        high, low = split(value)
        lo = pos * FACE
        x3[lo:lo + FACE, :] = high
        x3[NX + lo:NX + lo + FACE, :] = low
        x3[2 * NX + lo:2 * NX + lo + FACE, :] = high

    pbuf[0] = apply_loads(0, 32)
    coarse_begin(0)
    in_copies[3].wait()

    def split_k(i, carry):
        at = pl.multiple_of(i * step, step)
        high, low = split(kv[pl.ds(at, step), :])
        khi[pl.ds(at, step), 0:nrows] = high
        klo[pl.ds(at, step), 0:nrows] = low
        return carry

    lax.fori_loop(0, whole // step, split_k, 0)
    tail[0:left_rows, 0:nrows] = kv[whole:nrows, :]
    high, low = split(tail[...])
    khi[whole:whole + 16, :] = high
    klo[whole:whole + 16, :] = low

    def face_rows(lo, hi):
        def tile(i, carry):
            at = pl.ds(pl.multiple_of(i * 256, 256), 256)
            a0hi[32 + lo:32 + hi, at] = dot(bmat[lo:hi, :], khi[:, at]).astype(BF16)
            a0lo[32 + lo:32 + hi, at] = dot(bmat[lo:hi, :], klo[:, at]).astype(BF16)
            return carry

        lax.fori_loop(0, nrp // 256, tile, 0)

    half = 2 * FACE
    face_rows(0, half)
    tb[0, 0:half, :] = apply_loads(32, 32 + half)
    copies = faces_start(0, (0, 1))
    coarse_gather(0)
    face_rows(half, NX)
    tb[0, half:NX, :] = apply_loads(32 + half, 32 + NX)
    copies += faces_start(0, (2, 3))

    for j in range(1, ncrs):
        copy = remote(dall.at[b], dall.at[b], csend.at[j], crecv.at[j], (a, lax.rem(b + j, ncrs)))
        copy.wait()
    total_hi = total_lo = None
    for blk_b in range(ncrs):
        j = rows_of((LANES, 1))
        pair = div(j, 24)
        rem = j - 24 * pair
        pair = pair + (cblock * blk_b // 24) // 2
        r = 24 * (2 * pair + 1 - c) + rem
        target = jnp.where((j < 120) & (r >= cblock * blk_b) & (r < cblock * (blk_b + 1)),
                           24 * (pair + 1 - c) + rem, -1)
        perm = hot(target == cols_of((LANES, chips * 24)))
        high, low = split(dall[blk_b])
        ph, plo = dot(high, perm), dot(low, perm)
        total_hi = ph if total_hi is None else total_hi + ph
        total_lo = plo if total_lo is None else total_lo + plo
    dphi[...] = total_hi.astype(BF16)
    dplo[...] = total_lo.astype(BF16)

    coarse_copy = coarse_solve(0)

    def between(i, carry):
        at = pl.multiple_of(i * 224, 16)
        high = dot(a0hi[pl.ds(at, 224), :], bmt[...]).astype(BF16)
        a3[pl.ds(at, 224), 0:NX] = high
        a3[pl.ds(at, 224), NX:2 * NX] = high
        a3[pl.ds(at, 224), 2 * NX:] = dot(a0lo[pl.ds(at, 224), :], bmt[...]).astype(BF16)
        return carry

    lax.fori_loop(0, NA // 224, between, 0)
    coarse_spread(0, coarse_copy)

    in_copies[4].wait()
    nface = sv.shape[0]
    sp[0:nface, 0:nface] = sv[...]
    high, low = split(sp[...])
    khi[0:NX, 0:NX] = high
    klo[0:NX, 0:NX] = low
    for pos in range(4):
        face = ORDER[pos]
        sign = 0.5 if pos % 2 else -0.5
        j = rows_of((FACE, 1))
        target = jnp.where(j < fdof, j + face * fdof, -1)
        tmat[pos * FACE:(pos + 1) * FACE, :] = hot(target == cols_of((FACE, NX)), sign)
    pos_l = jnp.where(lane >= FACE, 1, 0) + jnp.where(lane >= 2 * FACE, 1, 0) + jnp.where(lane >= 3 * FACE, 1, 0)
    j = lane - FACE * pos_l
    target = jnp.where(j < fdof, j + fdof * ((pos_l + 2) & 3), -1)
    kept = jnp.where(pos_l == 2, jnp.where(a > 0, 0.5, 0.0), jnp.where(pos_l == 3, jnp.where(a < nsub - 1, 0.5, 0.0), 0.5))
    tmt[...] = jnp.where(target == rows_of((NX, NX)), signs * kept, 0.0).astype(BF16)

    def precond_rows(i, carry):
        at = pl.ds(pl.multiple_of(i * FACE, FACE), FACE)
        high = dot(tmat[at, :], khi[0:NX, 0:NX]).astype(BF16)
        low = dot(tmat[at, :], klo[0:NX, 0:NX]).astype(BF16)
        high = dot(high, tmt[...]).astype(BF16)
        m3[at, 0:NX] = high
        m3[at, NX:2 * NX] = high
        m3[at, 2 * NX:] = dot(low, tmt[...]).astype(BF16)
        return carry

    lax.fori_loop(0, 4, precond_rows, 0)

    for copy in wcopies:
        copy.wait()
    high, low = split(wo[...] + wr[...])
    w3[:, 0:LANES] = high
    w3[:, LANES:2 * LANES] = high
    w3[:, 2 * LANES:] = low

    def operator_end(n, f, copies, use):
        coarse_end(f)
        faces_wait(copies)
        for pos in range(4):
            use(pos, jumped(n, pos, dot(w3[pos * FACE:(pos + 1) * FACE, :], h3[...])))

    def first_use(pos, value):
        rv[pos * FACE:(pos + 1) * FACE, :] = value
        put_x(pos, value)

    operator_end(0, 0, copies, first_use)

    def precond(n):
        tb[n % 2, 0:half, :] = dot(m3[0:half, :], x3[...])
        copies = faces_start(n, (0, 1))
        tb[n % 2, half:, :] = dot(m3[half:, :], x3[...])
        copies += faces_start(n, (2, 3))
        return copies, jnp.sum(rv[...] * tb[n % 2], axis=0, keepdims=True)

    row8 = rows_of((8, cases))

    def operator(n, f, extra):
        block = dot(a3[0:32 + half, :], x3[...])
        pbuf[f] = block[0:32]
        coarse_begin(f)
        tb[n % 2, 0:half, :] = block[32:]
        copies = faces_start(n, (0, 1))
        tb[n % 2, half:, :] = dot(a3[32 + half:, :], x3[...])
        copies += faces_start(n, (2, 3))
        energy = jnp.sum(dv[...] * tb[n % 2], axis=0, keepdims=True)
        rs[f] = jnp.where(row8 == 0, extra, jnp.where(row8 == 1, energy, 0.0))
        sum_begin(f)
        coarse_gather(f)
        block = sum_chip(f)
        copy = coarse_solve(f)
        ce = coarse_spread(f, copy)
        sum_gather(f, block + jnp.where(rows_of((8, LANES)) == 1, ce, 0.0))
        return copies

    copies, rz_part = precond(1)
    faces_wait(copies)
    for pos in range(4):
        value = jumped(1, pos)
        dv[pos * FACE:(pos + 1) * FACE, :] = value
        put_x(pos, value)

    copies = operator(2, 1, rz_part)

    def keep_image(n):
        def use(pos, value):
            tb[n % 2, pos * FACE:(pos + 1) * FACE, :] = value
        return use

    operator_end(2, 1, copies, keep_image(2))
    sum_spread(1)
    rz_now, energy = sum_end(1)
    alpha = rz_now / energy
    for pos in range(4):
        band = slice(pos * FACE, (pos + 1) * FACE)
        value = rv[band, :] - alpha * tb[0, band, :]
        rv[band, :] = value
        put_x(pos, value)
        mo[0, ORDER[pos]] = (alpha * dv[band, :])[0:fdof]

    copies, rz_part = precond(3)
    rs[0] = jnp.where(row8 == 0, rz_part, 0.0)
    sum_begin(0)
    sum_gather(0, sum_chip(0))
    sum_spread(0)
    rz_next, _ = sum_end(0)
    beta = rz_next / rz_now
    faces_wait(copies)
    for pos in range(4):
        band = slice(pos * FACE, (pos + 1) * FACE)
        value = jumped(3, pos) + beta * dv[band, :]
        dv[band, :] = value
        put_x(pos, value)

    copies = operator(4, 2, rz_part)
    operator_end(4, 2, copies, keep_image(4))
    sum_spread(2)
    _, energy = sum_end(2)
    alpha = rz_next / energy
    for pos in range(4):
        band = slice(pos * FACE, (pos + 1) * FACE)
        ro[0, ORDER[pos]] = (rv[band, :] - alpha * tb[0, band, :])[0:fdof]
        mo[0, ORDER[pos]] = mo[0, ORDER[pos]] + (alpha * dv[band, :])[0:fdof]

    for drain in drains:
        drain()


def body(face_index, kinv, schur, corner, coarse_inverse, loads):
    nsub = lax.axis_size("sub")
    ncrs = lax.axis_size("crs")
    fdof = face_index.shape[2]
    nrows, cases = loads.shape[1:]
    ncoarse = coarse_inverse.shape[1]
    nface = schur.shape[1]
    ncl = corner.shape[2]
    chips = nsub // 2
    nrp = -(-nrows // 256) * 256
    cbp = -(-coarse_inverse.shape[0] // 16) * 16
    ncp = -(-ncoarse // LANES) * LANES
    idx = jnp.pad(face_index[0], ((0, 0), (0, FACE - fdof)), constant_values=-1)
    idx = jnp.concatenate([idx[2:4], idx[0:2]], axis=0)
    vm = pltpu.VMEM
    dma = pltpu.SemaphoreType.DMA
    scratch = [
        vm((nrows, nrows), F32), vm((nrows, cases), F32), vm((nrows, ncl), F32), vm((nface, nface), F32),
        vm(coarse_inverse.shape, F32),
        vm((nrp, nrp), BF16), vm((nrp, nrp), BF16), vm((16, nrp), F32),
        vm((NX, nrp), BF16), vm((nrp, NX), BF16), vm((NA, nrp), BF16), vm((NA, nrp), BF16),
        vm((nrp, cases), BF16), vm((nrp, cases), BF16),
        vm((NA, 3 * NX), BF16), vm((NX, 3 * NX), BF16), vm((NX, 3 * LANES), BF16), vm((3 * NX, cases), BF16),
        vm((nrp, LANES), F32), vm((nrp, LANES), BF16), vm((nrp, LANES), BF16), vm((cbp, ncp), F32),
        vm((NX, NX), F32), vm((NX, NX), BF16), vm((NX, NX), BF16),
        vm((NX, LANES), F32), vm((NX, LANES), F32), vm((NX, LANES), F32),
        vm((ncrs, LANES, LANES), F32), vm((LANES, chips * 24), BF16), vm((LANES, chips * 24), BF16),
        vm((2, NX, cases), F32), vm((2, 4, FACE, cases), F32), vm((NX, cases), F32), vm((NX, cases), F32),
        vm((3, 32, cases), F32), vm((3, ncrs, 16, LANES), F32), vm((3, ncrs, 16, LANES), F32),
        vm((3, chips, 24, LANES), F32),
        vm((3, LANES + 24, LANES), F32), vm((3, LANES + 24, LANES), F32), vm((LANES, LANES), F32),
        vm((3, LANES, cases), F32), vm((3 * LANES, cases), BF16),
        vm((3, 8, cases), F32), vm((3, 2 * ncrs, 8, LANES), F32), vm((3, 8, LANES), F32),
        vm((3, chips, 8, LANES), F32), vm((3, 8, cases), F32),
        dma((5,)), dma((2, 4)), dma((2, 4)), dma((4,)), dma((4,)), dma((ncrs,)), dma((ncrs,)),
    ] + [dma((3,)) for _ in range(16)]
    out = jax.ShapeDtypeStruct((1, 4, fdof, cases), F32)
    anyspace = pl.BlockSpec(memory_space=pl.ANY)
    inside = pl.BlockSpec(memory_space=pltpu.VMEM)
    dims = (nsub, ncrs, nrows, fdof, cases, ncoarse)
    return pl.pallas_call(
        functools.partial(kernel, dims),
        out_shape=(out, out),
        in_specs=[inside, inside] + [anyspace] * 5,
        out_specs=(inside, inside),
        scratch_shapes=scratch,
        compiler_params=pltpu.CompilerParams(
            collective_id=0, has_side_effects=True, vmem_limit_bytes=63 * 2**20),
    )(idx.reshape(NX, 1), idx.reshape(1, NX), kinv, schur, corner, coarse_inverse, loads)


def solution(mesh):
    subs = P(("sub", "crs"), None, None)
    out = P(("sub", "crs"), None, None, None)
    return jax.shard_map(
        body, mesh=mesh, in_specs=(subs, subs, subs, subs, P("crs", None), subs), out_specs=(out, out),
        check_vma=False)
```

```python
import functools

import jax
import jax.numpy as jnp
from jax import lax
from jax.experimental import pallas as pl
from jax.experimental.pallas import tpu as pltpu
from jax.sharding import PartitionSpec as P

F32 = jnp.float32
BF16 = jnp.bfloat16
MESH = pl.DeviceIdType.MESH

FACE = 160
SENT = 152
NX = 4 * FACE
NC = 48
NW = 96
NA = NX + NC
ORDER = (2, 3, 0, 1)
LANES = 128


def dot(left, right):
    return jnp.dot(left, right, preferred_element_type=F32)


def dot_nt(left, right):
    return lax.dot_general(left, right, (((1,), (1,)), ((), ())), preferred_element_type=F32)


def split(value):
    high = value.astype(BF16)
    return high, (value - high.astype(F32)).astype(BF16)


def hot(cond, value=1.0):
    return jnp.where(cond, value, 0.0).astype(BF16)


def rows_of(shape):
    return lax.broadcasted_iota(jnp.int32, shape, 0)


def cols_of(shape):
    return lax.broadcasted_iota(jnp.int32, shape, 1)


def div(value, by):
    return (value * (65536 // by + 1)) >> 16


def kernel(dims, faces, kinv, schur, corner, cinv, loads, mo, ro,
           kv, lv, cv, sv, civ, khi, klo, tail, idxr, idxc, bmat, bmt, a0hi, a0lo, lhi, llo, a3, m3, w3, x3,
           cpad, cip, sp, tmat, tmt, ws, wo, wr, dall, dphi, dplo,
           tb, rb, rv, dv, mv, pbuf, p0, gb, sibs, sibr, hk, qk, hb, h3,
           rs, rr, er, co, outs,
           dsem, osem, fsend, frecv, wsend, wrecv, csend, crecv,
           s1s, s1r, s2s, s2r, bs, br, s3s, s3r, r1s, r1r, r2s, r2r):
    nsub, ncrs, nrows, fdof, cases, ncoarse = dims
    chips = nsub // 2
    nrp = khi.shape[1]
    cblock = ncoarse // ncrs
    cbp, ncp = cip.shape
    a = lax.axis_index("sub")
    b = lax.axis_index("crs")
    k = lax.div(a, 2)
    c = lax.rem(a, 2)
    sib = 2 * k + 1 - c
    up = lax.rem(a + 1, nsub)
    down = lax.rem(a + nsub - 1, nsub)
    left = lax.rem(b + ncrs - 1, ncrs)
    right = lax.rem(b + 1, ncrs)
    dests = ((a, left), (a, right), (down, b), (up, b))
    keeps = (None, None, a > 0, a < nsub - 1)
    drains = []

    def local(src, dst, n):
        return pltpu.make_async_copy(src, dst, dsem.at[n])

    def remote(src, dst, ssem, rsem, dev):
        return pltpu.make_async_remote_copy(
            src_ref=src, dst_ref=dst, send_sem=ssem, recv_sem=rsem, device_id=dev, device_id_type=MESH)

    def settle(ref, sem):
        pltpu.make_async_copy(ref, ref, sem).wait()

    in_copies = [local(corner.at[0], cv, 0), local(cinv, civ, 1), local(loads.at[:, 0], lv, 2),
                 local(kinv.at[:, 0], kv, 3), local(schur.at[:, 0], sv, 4)]
    for copy in in_copies:
        copy.start()

    barrier = pltpu.get_barrier_semaphore()
    for j in range(1, ncrs):
        pl.semaphore_signal(barrier, inc=1, device_id=(a, lax.rem(b + j, ncrs)), device_id_type=MESH)
    for j in range(ncrs):
        pl.semaphore_signal(barrier, inc=1, device_id=(up, j), device_id_type=MESH)
        pl.semaphore_signal(barrier, inc=1, device_id=(down, j), device_id_type=MESH)
    for j in range(1, ncrs):
        to = lax.rem(b + j, ncrs)
        pl.semaphore_signal(barrier, inc=1, device_id=(lax.rem(a + 2, nsub), to), device_id_type=MESH)
        pl.semaphore_signal(barrier, inc=1, device_id=(lax.rem(a + nsub - 2, nsub), to), device_id_type=MESH)

    def greet(j, carry):
        pl.semaphore_signal(barrier, inc=1, device_id=(2 * lax.rem(k + j, chips) + c, b), device_id_type=MESH)
        return carry

    lax.fori_loop(1, chips, greet, 0)

    greeted = ncrs - 1 + 2 * ncrs + 2 * (ncrs - 1) + chips - 1

    idxr[...] = jnp.full(idxr.shape, -1, jnp.int32)
    for pos in range(4):
        face = ORDER[pos]
        idxr[0:1, pos * FACE:pos * FACE + fdof] = faces[0, face:face + 1, :]
    idxc[...] = jnp.transpose(idxr[...])
    for pos in range(4):
        sign = 1.0 if pos % 2 else -1.0
        band = slice(pos * FACE, (pos + 1) * FACE)
        bmat[band, :] = hot(idxc[band, 0:1] == cols_of((FACE, nrp)), sign)
    lane = cols_of((1, NX))
    signs = jnp.where(((lane >= FACE) & (lane < 2 * FACE)) | (lane >= 3 * FACE), 1.0, -1.0)

    def build_bmt(i, carry):
        at = pl.multiple_of(i * LANES, LANES)
        rows = rows_of((LANES, NX)) + at
        bmt[pl.ds(at, LANES), :] = jnp.where(idxr[0:1, :] == rows, signs, 0.0).astype(BF16)
        return carry

    lax.fori_loop(0, nrp // LANES, build_bmt, 0)

    for n in range(2):
        for pos in range(4):
            rb[n, pos, SENT:FACE, :] = jnp.zeros((FACE - SENT, cases), F32)
    hb[:, 96:LANES, :] = jnp.zeros((3, 32, cases), F32)
    cpad[...] = jnp.zeros(cpad.shape, F32)
    cip[...] = jnp.zeros(cip.shape, F32)
    sp[...] = jnp.zeros(sp.shape, F32)
    edge = nrp - LANES
    khi[:, edge:] = jnp.zeros((nrp, LANES), BF16)
    klo[:, edge:] = jnp.zeros((nrp, LANES), BF16)
    whole = nrows // 16 * 16
    for ref in (khi, klo, lhi, llo):
        ref[whole:, :] = jnp.zeros((nrp - whole, ref.shape[1]), BF16)
    tail[...] = jnp.zeros(tail.shape, F32)

    in_copies[0].wait()
    ncl = cv.shape[0]
    cpad[0:ncl, 0:nrows] = cv[...]
    chi, clo = split(cpad[...])
    l = cols_of((1, 32))
    da = div(l, 12)
    rem12 = l - 12 * da
    db = div(rem12, 6)
    where_l = jnp.where(l < 24, 24 * da + 6 * lax.rem(b + db, ncrs) + rem12 - 6 * db, -1000)
    sel = hot(where_l == rows_of((NC, 32)))
    a0hi[0:NC, :] = dot(sel, chi).astype(BF16)
    a0lo[0:NC, :] = dot(sel, clo).astype(BF16)
    in_copies[2].wait()
    step = 16 * 5

    def split_loads(i, carry):
        at = pl.multiple_of(i * step, step)
        high, low = split(lv[pl.ds(at, step), :])
        lhi[pl.ds(at, step), :] = high
        llo[pl.ds(at, step), :] = low
        return carry

    lax.fori_loop(0, whole // step, split_loads, 0)
    left_rows = nrows - whole
    tail[0:left_rows, 0:cases] = lv[whole:nrows, :]
    high, low = split(tail[:, 0:cases])
    lhi[whole:whole + 16, :] = high
    llo[whole:whole + 16, :] = low

    def apply_loads(lo, hi):
        high, low = a0hi[lo:hi, :], a0lo[lo:hi, :]
        return dot(high, lhi[...]) + dot(high, llo[...]) + dot(low, lhi[...])

    def coarse_begin(f, offs):
        for i, off in enumerate(offs):
            owner = lax.rem(a + off + nsub, nsub)
            for j in range(ncrs):
                to = lax.rem(b + j, ncrs)
                at = pl.ds(pl.multiple_of(to * LANES, LANES), LANES)
                band = pl.ds(24 * i, 24)
                if off == 0 and j == 0:
                    p0[f, i * ncrs + b] = pbuf[f, band, at]
                    continue
                remote(pbuf.at[f, band, at], p0.at[f, i * ncrs + b], s1s.at[f], s1r.at[f], (owner, to)).start()
        drains.append(lambda: settle(p0.at[f, pl.ds(0, ncrs * len(offs) - 1)], s1s.at[f]))

    def coarse_gather(f, offs):
        count = ncrs * len(offs)
        settle(p0.at[f, pl.ds(0, count - 1)], s1r.at[f])
        gb[f, k] = jnp.sum(p0[f, 0:count], axis=0)

        def send(j, carry):
            to = 2 * lax.rem(k + j, chips) + c
            remote(gb.at[f, k], gb.at[f, k], s2s.at[f], s2r.at[f], (to, b)).start()
            return carry

        lax.fori_loop(1, chips, send, 0)
        drains.append(lambda: settle(gb.at[f, pl.ds(0, chips - 1)], s2s.at[f]))

    def coarse_solve(f):
        settle(gb.at[f, pl.ds(0, chips - 1)], s2r.at[f])
        high, low = split(gb[f].reshape(chips * 24, LANES))
        sibs[f, 0:LANES] = dot(dphi[...], high) + dot(dphi[...], low) + dot(dplo[...], high)
        sibs[f, LANES:LANES + 24] = gb[f, k]
        copy = remote(sibs.at[f], sibr.at[f], bs.at[f], br.at[f], (sib, b))
        copy.start()
        return copy

    def coarse_spread(f, copy, scale=None):
        copy.wait()
        at = pl.ds(pl.multiple_of(b * LANES, LANES), LANES)
        total = sibs[f, 0:LANES] + sibr[f, 0:LANES]
        mine, other = sibs[f, LANES:LANES + 24], sibr[f, LANES:LANES + 24]
        if scale is not None:
            part = scale[0:1, at]
            total = total + part * hk[...]
            mine = mine + part * qk[0]
            other = other + part * qk[1]
        hk[...] = total
        qk[0] = mine
        qk[1] = other
        hb[f, 0:96, at] = hk[pl.ds(pl.multiple_of(24 * c, 8), 96), :]
        for j in range(1, ncrs):
            remote(hb.at[f, pl.ds(0, 96), at], hb.at[f, pl.ds(0, 96), at], s3s.at[f], s3r.at[f],
                   (a, lax.rem(b + j, ncrs))).start()
        drains.append(lambda: settle(hb.at[f, pl.ds(0, 96), pl.ds(0, (ncrs - 1) * LANES)], s3s.at[f]))
        mine = hk[pl.ds(pl.multiple_of(24 + 24 * c, 8), 24), :] * mine
        other = hk[pl.ds(pl.multiple_of(48 - 24 * c, 8), 24), :] * other
        return 0.5 * jnp.sum(mine + other, axis=0, keepdims=True)

    def coarse_end(f):
        settle(hb.at[f, pl.ds(0, 96), pl.ds(0, (ncrs - 1) * LANES)], s3r.at[f])
        high, low = split(hb[f])
        h3[0:LANES, :] = high
        h3[LANES:2 * LANES, :] = low
        h3[2 * LANES:, :] = high

    row8 = rows_of((8, LANES))

    def packed(value):
        return jnp.concatenate([value[:, i * LANES:(i + 1) * LANES] for i in range(ncrs)], axis=0)

    def unpacked(value):
        return jnp.concatenate([value[i:i + 1] for i in range(ncrs)], axis=1)

    def sum_begin(n, first, second):
        rs[n] = jnp.concatenate([first, second], axis=0)
        for cc in range(2):
            for j in range(ncrs):
                if cc == 0 and j == 0:
                    rr[n, c * ncrs + b] = rs[n]
                    continue
                dev = (a if cc == 0 else sib, lax.rem(b + j, ncrs))
                remote(rs.at[n], rr.at[n, c * ncrs + b], r1s.at[n], r1r.at[n], dev).start()
        drains.append(lambda: settle(rr.at[n, pl.ds(0, 2 * ncrs - 1)], r1s.at[n]))

    def sum_gather(n):
        settle(rr.at[n, pl.ds(0, 2 * ncrs - 1)], r1r.at[n])
        er[n, k] = jnp.sum(rr[n], axis=0)

        def send(j, carry):
            to = 2 * lax.rem(k + j, chips) + c
            remote(er.at[n, k], er.at[n, k], r2s.at[n], r2r.at[n], (to, b)).start()
            return carry

        lax.fori_loop(1, chips, send, 0)
        drains.append(lambda: settle(er.at[n, pl.ds(0, chips - 1)], r2s.at[n]))

    def sum_end(n):
        settle(er.at[n, pl.ds(0, chips - 1)], r2r.at[n])
        total = jnp.sum(er[n], axis=0)
        return total[0:ncrs], total[ncrs:]

    def faces_start(n, which):
        copies = []
        for pos in which:
            copy = remote(tb.at[n % 2, pl.ds(pos * FACE, SENT)], rb.at[n % 2, pos ^ 1, pl.ds(0, SENT)],
                          fsend.at[n % 2, pos], frecv.at[n % 2, pos ^ 1], dests[pos])
            copy.start()
            copies.append(copy)
        return copies

    def faces_wait(copies):
        for copy in copies:
            copy.wait()

    def jumped(n, pos, extra=None):
        band = slice(pos * FACE, (pos + 1) * FACE)
        value = tb[n % 2, band, :] + rb[n % 2, pos]
        if extra is not None:
            value = value + extra
        if keeps[pos] is not None:
            value = jnp.where(keeps[pos], value, 0.0)
        return value

    def put_x(pos, value):
        high, low = split(value)
        lo = pos * FACE
        x3[lo:lo + FACE, :] = high
        x3[NX + lo:NX + lo + FACE, :] = low
        x3[2 * NX + lo:2 * NX + lo + FACE, :] = high

    pbuf[0, 0:NC] = apply_loads(0, NC)
    pl.semaphore_wait(barrier, greeted)
    coarse_begin(0, (0, 1))

    bch = dot_nt(bmat[...], chi).astype(BF16)
    bcl = dot_nt(bmat[...], clo).astype(BF16)
    l = rows_of((32, 1))
    da = div(l, 12)
    rem12 = l - 12 * da
    db = div(rem12, 6)
    where_l = 24 * (1 + da) + 6 * lax.rem(b + db, ncrs) + rem12 - 6 * db
    where_l = jnp.where(l < 24, where_l, -1000)
    lanes = cols_of((32, LANES))
    emaps = [hot(where_l + off == lanes) for off in (0, 24, -24)]
    wo[...] = dot(bch, emaps[0]) + dot(bcl, emaps[0])
    ws[0:2 * FACE, :] = wo[0:2 * FACE, :]
    for pos in (2, 3):
        band = slice(pos * FACE, (pos + 1) * FACE)
        ws[band, :] = dot(bch[band], emaps[pos - 1]) + dot(bcl[band], emaps[pos - 1])
    wcopies = [remote(ws.at[pl.ds(pos * FACE, FACE)], wr.at[pl.ds((pos ^ 1) * FACE, FACE)],
                      wsend.at[pos], wrecv.at[pos ^ 1], dests[pos]) for pos in range(4)]
    for copy in wcopies:
        copy.start()

    in_copies[1].wait()
    cip[0:cblock, 0:ncoarse] = civ[...]
    high, low = split(cip[...])
    i = cols_of((1, cbp))
    r = cblock * b + i
    plane = div(r, 24)
    base = lax.div(lax.div(cblock * b, 24), 2)
    target = 24 * ((plane >> 1) - base) + r - 24 * plane
    target = jnp.where((((plane + 1) & 1) == c) & (i < cblock), target, -1)
    pct = hot(target == rows_of((LANES, cbp)))
    x1h = dot(pct, high).astype(BF16)
    x1l = dot(pct, low).astype(BF16)
    i = rows_of((LANES, 1))
    r = 48 * k - 48 + i
    r = jnp.where((i < 120) & (r < ncoarse), r, -1)
    sel = hot(r == cols_of((LANES, ncp)))
    dall[b] = dot_nt(sel, x1h) + dot_nt(sel, x1l)
    for j in range(1, ncrs):
        remote(dall.at[b], dall.at[b], csend.at[j], crecv.at[j], (a, lax.rem(b + j, ncrs))).start()

    in_copies[3].wait()

    def split_k(i, carry):
        at = pl.multiple_of(i * step, step)
        high, low = split(kv[pl.ds(at, step), :])
        khi[pl.ds(at, step), 0:nrows] = high
        klo[pl.ds(at, step), 0:nrows] = low
        return carry

    lax.fori_loop(0, whole // step, split_k, 0)
    tail[0:left_rows, 0:nrows] = kv[whole:nrows, :]
    high, low = split(tail[...])
    khi[whole:whole + 16, :] = high
    klo[whole:whole + 16, :] = low

    def face_rows(lo, hi):
        def tile(i, carry):
            at = pl.ds(pl.multiple_of(i * 256, 256), 256)
            a0hi[NC + lo:NC + hi, at] = dot(bmat[lo:hi, :], khi[:, at]).astype(BF16)
            a0lo[NC + lo:NC + hi, at] = dot(bmat[lo:hi, :], klo[:, at]).astype(BF16)
            return carry

        lax.fori_loop(0, nrp // 256, tile, 0)

    half = 2 * FACE
    face_rows(0, half)
    tb[0, 0:half, :] = apply_loads(NC, NC + half)
    copies = faces_start(0, (0, 1))
    coarse_gather(0, (0, 1))
    face_rows(half, NX)
    tb[0, half:NX, :] = apply_loads(NC + half, NC + NX)
    copies += faces_start(0, (2, 3))

    for j in range(1, ncrs):
        copy = remote(dall.at[b], dall.at[b], csend.at[j], crecv.at[j], (a, lax.rem(b + j, ncrs)))
        copy.wait()
    total_hi = total_lo = None
    for blk_b in range(ncrs):
        j = rows_of((LANES, 1))
        pair = div(j, 24)
        rem = j - 24 * pair
        pair = pair + (cblock * blk_b // 24) // 2
        r = 24 * (2 * pair + 1 - c) + rem
        target = jnp.where((j < 120) & (r >= cblock * blk_b) & (r < cblock * (blk_b + 1)),
                           24 * (pair + 1 - c) + rem, -1)
        perm = hot(target == cols_of((LANES, chips * 24)))
        high, low = split(dall[blk_b])
        ph, plo = dot(high, perm), dot(low, perm)
        total_hi = ph if total_hi is None else total_hi + ph
        total_lo = plo if total_lo is None else total_lo + plo
    dphi[...] = total_hi.astype(BF16)
    dplo[...] = total_lo.astype(BF16)

    coarse_copy = coarse_solve(0)

    def between(i, carry):
        at = pl.ds(pl.multiple_of(i * half, half), half)
        src = pl.ds(pl.multiple_of(NC + i * half, 16), half)
        high = dot(a0hi[src, :], bmt[...]).astype(BF16)
        a3[at, 0:NX] = high
        a3[at, NX:2 * NX] = high
        a3[at, 2 * NX:] = dot(a0lo[src, :], bmt[...]).astype(BF16)
        return carry

    lax.fori_loop(0, 2, between, 0)
    coarse_spread(0, coarse_copy)

    in_copies[4].wait()
    nface = sv.shape[0]
    sp[0:nface, 0:nface] = sv[...]
    high, low = split(sp[...])
    khi[0:NX, 0:NX] = high
    klo[0:NX, 0:NX] = low
    for pos in range(4):
        face = ORDER[pos]
        sign = 0.5 if pos % 2 else -0.5
        j = rows_of((FACE, 1))
        target = jnp.where(j < fdof, j + face * fdof, -1)
        tmat[pos * FACE:(pos + 1) * FACE, :] = hot(target == cols_of((FACE, NX)), sign)
    pos_l = jnp.where(lane >= FACE, 1, 0) + jnp.where(lane >= 2 * FACE, 1, 0) + jnp.where(lane >= 3 * FACE, 1, 0)
    j = lane - FACE * pos_l
    target = jnp.where(j < fdof, j + fdof * ((pos_l + 2) & 3), -1)
    kept = jnp.where(pos_l == 2, jnp.where(a > 0, 0.5, 0.0), jnp.where(pos_l == 3, jnp.where(a < nsub - 1, 0.5, 0.0), 0.5))
    tmt[...] = jnp.where(target == rows_of((NX, NX)), signs * kept, 0.0).astype(BF16)

    def precond_rows(i, carry):
        at = pl.ds(pl.multiple_of(i * FACE, FACE), FACE)
        high = dot(tmat[at, :], khi[0:NX, 0:NX]).astype(BF16)
        low = dot(tmat[at, :], klo[0:NX, 0:NX]).astype(BF16)
        high = dot(high, tmt[...]).astype(BF16)
        to = pl.ds(pl.multiple_of(NW + i * FACE, 16), FACE)
        m3[to, 0:NX] = high
        m3[to, NX:2 * NX] = high
        m3[to, 2 * NX:] = dot(low, tmt[...]).astype(BF16)
        return carry

    lax.fori_loop(0, 4, precond_rows, 0)

    for copy in wcopies:
        copy.wait()
    for pos in range(4):
        band = slice(pos * FACE, (pos + 1) * FACE)
        value = wo[band, :] + wr[band, :]
        if keeps[pos] is not None:
            value = jnp.where(keeps[pos], value, 0.0)
        wo[band, :] = value
    high, low = split(wo[...])
    w3[:, 0:LANES] = high
    w3[:, LANES:2 * LANES] = high
    w3[:, 2 * LANES:] = low
    high, low = split(jnp.transpose(wo[...]))
    mhi, mlo = m3[NW:, 0:NX], m3[NW:, 2 * NX:]
    high, low = split((dot(high, mhi) + dot(high, mlo) + dot(low, mhi))[0:NW])
    m3[0:NW, 0:NX] = high
    m3[0:NW, NX:2 * NX] = high
    m3[0:NW, 2 * NX:] = low

    def operator_end(n, f, copies, use):
        coarse_end(f)
        faces_wait(copies)
        for pos in range(4):
            use(pos, jumped(n, pos, dot(w3[pos * FACE:(pos + 1) * FACE, :], h3[...])))

    def first_use(pos, value):
        rv[pos * FACE:(pos + 1) * FACE, :] = value
        put_x(pos, value)

    operator_end(0, 0, copies, first_use)

    around = (-1, 0, 1, 2)

    def precond(n, f):
        block = dot(m3[0:NW + half, :], x3[...])
        pbuf[f] = block[0:NW]
        coarse_begin(f, around)
        tb[n % 2, 0:half, :] = block[NW:]
        copies = faces_start(n, (0, 1))
        tb[n % 2, half:, :] = dot(m3[NW + half:, :], x3[...])
        copies += faces_start(n, (2, 3))
        return copies, packed(jnp.sum(rv[...] * tb[n % 2], axis=0, keepdims=True))

    def operator(n, f, rz_part, scale):
        tb[n % 2, 0:half, :] = dot(a3[0:half, :], x3[...])
        copies = faces_start(n, (0, 1))
        coarse_copy = coarse_solve(f)
        tb[n % 2, half:, :] = dot(a3[half:, :], x3[...])
        copies += faces_start(n, (2, 3))
        energy = packed(jnp.sum(dv[...] * tb[n % 2], axis=0, keepdims=True))
        ce = coarse_spread(f, coarse_copy, scale)
        energy = energy + jnp.where(rows_of((ncrs, LANES)) == b, ce, 0.0)
        sum_begin(f, rz_part, energy)
        sum_gather(f)
        return copies

    def keep_image(n):
        def use(pos, value):
            tb[n % 2, pos * FACE:(pos + 1) * FACE, :] = value
        return use

    copies, rz_part = precond(1, 1)
    coarse_gather(1, around)
    faces_wait(copies)
    for pos in range(4):
        value = jumped(1, pos)
        dv[pos * FACE:(pos + 1) * FACE, :] = value
        put_x(pos, value)

    copies = operator(2, 1, rz_part, None)
    operator_end(2, 1, copies, keep_image(2))
    rz_now, energy = sum_end(1)
    alpha = unpacked(rz_now / energy)
    for pos in range(4):
        band = slice(pos * FACE, (pos + 1) * FACE)
        value = rv[band, :] - alpha * tb[0, band, :]
        rv[band, :] = value
        put_x(pos, value)

    copies, rz_part = precond(3, 2)
    sum_begin(0, rz_part, jnp.zeros((ncrs, LANES), F32))
    coarse_gather(2, around)
    sum_gather(0)
    for pos in range(4):
        band = slice(pos * FACE, (pos + 1) * FACE)
        mv[band, :] = alpha * dv[band, :]
    faces_wait(copies)
    rz_next, _ = sum_end(0)
    beta = unpacked(rz_next / rz_now)
    co[0:1, :] = beta
    for pos in range(4):
        band = slice(pos * FACE, (pos + 1) * FACE)
        value = jumped(3, pos) + beta * dv[band, :]
        dv[band, :] = value
        put_x(pos, value)

    copies = operator(4, 2, rz_next, co)
    operator_end(4, 2, copies, keep_image(4))
    _, energy = sum_end(2)
    alpha = unpacked(rz_next / energy)
    out_copies = []
    for pos in range(4):
        band = slice(pos * FACE, (pos + 1) * FACE)
        outs[pos] = (mv[band, :] + alpha * dv[band, :])[0:fdof]
        outs[4 + pos] = (rv[band, :] - alpha * tb[0, band, :])[0:fdof]
        for side, ref in enumerate((mo, ro)):
            copy = pltpu.make_async_copy(outs.at[4 * side + pos], ref.at[0, :, ORDER[pos]], osem.at[4 * side + pos])
            copy.start()
            out_copies.append(copy)
    for copy in out_copies:
        copy.wait()

    for drain in drains:
        drain()


def body(face_index, kinv, schur, corner, coarse_inverse, loads):
    nsub = lax.axis_size("sub")
    ncrs = lax.axis_size("crs")
    fdof = face_index.shape[2]
    nrows, cases = loads.shape[1:]
    ncoarse = coarse_inverse.shape[1]
    nface = schur.shape[1]
    ncl = corner.shape[2]
    chips = nsub // 2
    nrp = -(-nrows // 256) * 256
    cbp = -(-coarse_inverse.shape[0] // 16) * 16
    ncp = -(-ncoarse // LANES) * LANES
    vm = pltpu.VMEM
    dma = pltpu.SemaphoreType.DMA
    scratch = [
        vm((nrows, nrows), F32), vm((nrows, cases), F32), vm((ncl, nrows), F32), vm((nface, nface), F32),
        vm(coarse_inverse.shape, F32),
        vm((nrp, nrp), BF16), vm((nrp, nrp), BF16), vm((16, nrp), F32),
        vm((8, NX), jnp.int32), vm((NX, 8), jnp.int32),
        vm((NX, nrp), BF16), vm((nrp, NX), BF16), vm((NA, nrp), BF16), vm((NA, nrp), BF16),
        vm((nrp, cases), BF16), vm((nrp, cases), BF16),
        vm((NX, 3 * NX), BF16), vm((NW + NX, 3 * NX), BF16), vm((NX, 3 * LANES), BF16), vm((3 * NX, cases), BF16),
        vm((32, nrp), F32), vm((cbp, ncp), F32),
        vm((NX, NX), F32), vm((NX, NX), BF16), vm((NX, NX), BF16),
        vm((NX, LANES), F32), vm((NX, LANES), F32), vm((NX, LANES), F32),
        vm((ncrs, LANES, LANES), F32), vm((LANES, chips * 24), BF16), vm((LANES, chips * 24), BF16),
        vm((2, NX, cases), F32), vm((2, 4, FACE, cases), F32),
        vm((NX, cases), F32), vm((NX, cases), F32), vm((NX, cases), F32),
        vm((3, NW, cases), F32), vm((3, 4 * ncrs, 24, LANES), F32), vm((3, chips, 24, LANES), F32),
        vm((3, LANES + 24, LANES), F32), vm((3, LANES + 24, LANES), F32), vm((LANES, LANES), F32),
        vm((2, 24, LANES), F32), vm((3, LANES, cases), F32), vm((3 * LANES, cases), BF16),
        vm((3, 8, LANES), F32), vm((3, 2 * ncrs, 8, LANES), F32), vm((3, chips, 8, LANES), F32),
        vm((8, cases), F32), vm((8, fdof, cases), F32),
        dma((5,)), dma((8,)), dma((2, 4)), dma((2, 4)), dma((4,)), dma((4,)), dma((ncrs,)), dma((ncrs,)),
    ] + [dma((3,)) for _ in range(12)]
    out = jax.ShapeDtypeStruct((1, fdof, 4, cases), F32)
    anyspace = pl.BlockSpec(memory_space=pl.ANY)
    inside = pl.BlockSpec(memory_space=pltpu.VMEM)
    dims = (nsub, ncrs, nrows, fdof, cases, ncoarse)
    mult, resid = pl.pallas_call(
        functools.partial(kernel, dims),
        out_shape=(out, out),
        in_specs=[inside] + [anyspace] * 5,
        out_specs=(anyspace, anyspace),
        scratch_shapes=scratch,
        compiler_params=pltpu.CompilerParams(
            collective_id=0, has_side_effects=True, vmem_limit_bytes=63 * 2**20),
    )(face_index, jnp.swapaxes(kinv, 0, 1), jnp.swapaxes(schur, 0, 1),
      jnp.swapaxes(corner, 1, 2), coarse_inverse, jnp.swapaxes(loads, 0, 1))
    return jnp.swapaxes(mult, 1, 2), jnp.swapaxes(resid, 1, 2)


def solution(mesh):
    subs = P(("sub", "crs"), None, None)
    out = P(("sub", "crs"), None, None, None)
    return jax.shard_map(
        body, mesh=mesh, in_specs=(subs, subs, subs, subs, P("crs", None), subs), out_specs=(out, out),
        check_vma=False)
```

```python
import functools

import jax
import jax.numpy as jnp
from jax import lax
from jax.experimental import pallas as pl
from jax.experimental.pallas import tpu as pltpu
from jax.sharding import PartitionSpec as P

F32 = jnp.float32
BF16 = jnp.bfloat16
MESH = pl.DeviceIdType.MESH

FACE = 160
SENT = 152
NX = 4 * FACE
NC = 48
NW = 96
NA = NX + NC
ORDER = (2, 3, 0, 1)
LANES = 128


def dot(left, right):
    return jnp.dot(left, right, preferred_element_type=F32)


def dot_nt(left, right):
    return lax.dot_general(left, right, (((1,), (1,)), ((), ())), preferred_element_type=F32)


def split(value):
    high = value.astype(BF16)
    return high, (value - high.astype(F32)).astype(BF16)


def hot(cond, value=1.0):
    return jnp.where(cond, value, 0.0).astype(BF16)


def rows_of(shape):
    return lax.broadcasted_iota(jnp.int32, shape, 0)


def cols_of(shape):
    return lax.broadcasted_iota(jnp.int32, shape, 1)


def div(value, by):
    return (value * (65536 // by + 1)) >> 16


def kernel(dims, faces, kinv, schur, corner, cinv, loads, mo, ro,
           kv, lv, cv, sv, civ, khi, klo, tail, idxr, idxc, bmat, bmt, a0hi, a0lo, lhi, llo, a3, m3, w3, x3,
           cpad, cip, sp, tmat, tmt, ws, wo, wr, dall, dphi, dplo,
           tb, rb, rv, dv, mv, pbuf, p0, gb, sibs, sibr, hs, hk, qk, hb, h3,
           rs, rr, er, co, outs,
           dsem, osem, fsend, frecv, wsend, wrecv, csend, crecv,
           s1s, s1r, s2s, s2r, bs, br, s3s, s3r, r1s, r1r, r2s, r2r):
    nsub, ncrs, nrows, fdof, cases, ncoarse = dims
    chips = nsub // 2
    nrp = khi.shape[1]
    cblock = ncoarse // ncrs
    cbp, ncp = cip.shape
    a = lax.axis_index("sub")
    b = lax.axis_index("crs")
    k = lax.div(a, 2)
    c = lax.rem(a, 2)
    sib = 2 * k + 1 - c
    up = lax.rem(a + 1, nsub)
    down = lax.rem(a + nsub - 1, nsub)
    left = lax.rem(b + ncrs - 1, ncrs)
    right = lax.rem(b + 1, ncrs)
    dests = ((a, left), (a, right), (down, b), (up, b))
    keeps = (None, None, a > 0, a < nsub - 1)
    drains = []

    def local(src, dst, n):
        return pltpu.make_async_copy(src, dst, dsem.at[n])

    def remote(src, dst, ssem, rsem, dev):
        return pltpu.make_async_remote_copy(
            src_ref=src, dst_ref=dst, send_sem=ssem, recv_sem=rsem, device_id=dev, device_id_type=MESH)

    def settle(ref, sem):
        pltpu.make_async_copy(ref, ref, sem).wait()

    in_copies = [local(corner.at[0], cv, 0), local(cinv, civ, 1), local(loads.at[:, 0], lv, 2),
                 local(kinv.at[:, 0], kv, 3), local(schur.at[:, 0], sv, 4)]
    for copy in in_copies:
        copy.start()

    barrier = pltpu.get_barrier_semaphore()
    for j in range(1, ncrs):
        pl.semaphore_signal(barrier, inc=1, device_id=(a, lax.rem(b + j, ncrs)), device_id_type=MESH)
    for j in range(ncrs):
        pl.semaphore_signal(barrier, inc=1, device_id=(up, j), device_id_type=MESH)
        pl.semaphore_signal(barrier, inc=1, device_id=(down, j), device_id_type=MESH)
    for j in range(1, ncrs):
        to = lax.rem(b + j, ncrs)
        pl.semaphore_signal(barrier, inc=1, device_id=(lax.rem(a + 2, nsub), to), device_id_type=MESH)
        pl.semaphore_signal(barrier, inc=1, device_id=(lax.rem(a + nsub - 2, nsub), to), device_id_type=MESH)

    def greet(j, carry):
        pl.semaphore_signal(barrier, inc=1, device_id=(2 * lax.rem(k + j, chips) + c, b), device_id_type=MESH)
        return carry

    lax.fori_loop(1, chips, greet, 0)

    greeted = ncrs - 1 + 2 * ncrs + 2 * (ncrs - 1) + chips - 1

    idxr[...] = jnp.full(idxr.shape, -1, jnp.int32)
    for pos in range(4):
        face = ORDER[pos]
        idxr[0:1, pos * FACE:pos * FACE + fdof] = faces[0, face:face + 1, :]
    idxc[...] = jnp.transpose(idxr[...])
    for pos in range(4):
        sign = 1.0 if pos % 2 else -1.0
        band = slice(pos * FACE, (pos + 1) * FACE)
        bmat[band, :] = hot(idxc[band, 0:1] == cols_of((FACE, nrp)), sign)
    lane = cols_of((1, NX))
    signs = jnp.where(((lane >= FACE) & (lane < 2 * FACE)) | (lane >= 3 * FACE), 1.0, -1.0)

    def build_bmt(i, carry):
        at = pl.multiple_of(i * LANES, LANES)
        rows = rows_of((LANES, NX)) + at
        bmt[pl.ds(at, LANES), :] = jnp.where(idxr[0:1, :] == rows, signs, 0.0).astype(BF16)
        return carry

    lax.fori_loop(0, nrp // LANES, build_bmt, 0)

    for n in range(2):
        for pos in range(4):
            rb[n, pos, SENT:FACE, :] = jnp.zeros((FACE - SENT, cases), F32)
    hb[:, 96:LANES, :] = jnp.zeros((3, 32, cases), F32)
    cpad[...] = jnp.zeros(cpad.shape, F32)
    cip[...] = jnp.zeros(cip.shape, F32)
    sp[...] = jnp.zeros(sp.shape, F32)
    edge = nrp - LANES
    khi[:, edge:] = jnp.zeros((nrp, LANES), BF16)
    klo[:, edge:] = jnp.zeros((nrp, LANES), BF16)
    whole = nrows // 16 * 16
    for ref in (khi, klo, lhi, llo):
        ref[whole:, :] = jnp.zeros((nrp - whole, ref.shape[1]), BF16)
    tail[...] = jnp.zeros(tail.shape, F32)

    in_copies[0].wait()
    ncl = cv.shape[0]
    cpad[0:ncl, 0:nrows] = cv[...]
    chi, clo = split(cpad[...])
    l = cols_of((1, 32))
    da = div(l, 12)
    rem12 = l - 12 * da
    db = div(rem12, 6)
    where_l = jnp.where(l < 24, 24 * da + 6 * lax.rem(b + db, ncrs) + rem12 - 6 * db, -1000)
    sel = hot(where_l == rows_of((NC, 32)))
    a0hi[0:NC, :] = dot(sel, chi).astype(BF16)
    a0lo[0:NC, :] = dot(sel, clo).astype(BF16)
    in_copies[2].wait()
    step = 16 * 5

    def split_loads(i, carry):
        at = pl.multiple_of(i * step, step)
        high, low = split(lv[pl.ds(at, step), :])
        lhi[pl.ds(at, step), :] = high
        llo[pl.ds(at, step), :] = low
        return carry

    lax.fori_loop(0, whole // step, split_loads, 0)
    left_rows = nrows - whole
    tail[0:left_rows, 0:cases] = lv[whole:nrows, :]
    high, low = split(tail[:, 0:cases])
    lhi[whole:whole + 16, :] = high
    llo[whole:whole + 16, :] = low

    def apply_loads(lo, hi):
        high, low = a0hi[lo:hi, :], a0lo[lo:hi, :]
        return dot(high, lhi[...]) + dot(high, llo[...]) + dot(low, lhi[...])

    def coarse_begin(f, offs):
        for i, off in enumerate(offs):
            owner = lax.rem(a + off + nsub, nsub)
            for j in range(ncrs):
                to = lax.rem(b + j, ncrs)
                at = pl.ds(pl.multiple_of(to * LANES, LANES), LANES)
                band = pl.ds(24 * i, 24)
                if off == 0 and j == 0:
                    p0[f, i * ncrs + b] = pbuf[f, band, at]
                    continue
                remote(pbuf.at[f, band, at], p0.at[f, i * ncrs + b], s1s.at[f], s1r.at[f], (owner, to)).start()
        drains.append(lambda: settle(p0.at[f, pl.ds(0, ncrs * len(offs) - 1)], s1s.at[f]))

    def coarse_gather(f, offs):
        count = ncrs * len(offs)
        settle(p0.at[f, pl.ds(0, count - 1)], s1r.at[f])
        gb[f, k] = jnp.sum(p0[f, 0:count], axis=0)

        def send(j, carry):
            to = 2 * lax.rem(k + j, chips) + c
            remote(gb.at[f, k], gb.at[f, k], s2s.at[f], s2r.at[f], (to, b)).start()
            return carry

        lax.fori_loop(1, chips, send, 0)
        drains.append(lambda: settle(gb.at[f, pl.ds(0, chips - 1)], s2s.at[f]))

    def coarse_solve(f):
        settle(gb.at[f, pl.ds(0, chips - 1)], s2r.at[f])
        high, low = split(gb[f].reshape(chips * 24, LANES))
        sibs[f, 0:LANES] = dot(dphi[...], high) + dot(dphi[...], low) + dot(dplo[...], high)
        sibs[f, LANES:LANES + 24] = gb[f, k]
        copy = remote(sibs.at[f], sibr.at[f], bs.at[f], br.at[f], (sib, b))
        copy.start()
        return copy

    def coarse_spread(f, copy):
        copy.wait()
        at = pl.ds(pl.multiple_of(b * LANES, LANES), LANES)
        total = sibs[f, 0:LANES] + sibr[f, 0:LANES]
        hs[...] = total
        hb[f, 0:NW, at] = hs[pl.ds(pl.multiple_of(24 * c, 8), NW), :]
        for j in range(1, ncrs):
            remote(hb.at[f, pl.ds(0, NW), at], hb.at[f, pl.ds(0, NW), at], s3s.at[f], s3r.at[f],
                   (a, lax.rem(b + j, ncrs))).start()
        drains.append(lambda: settle(hb.at[f, pl.ds(0, NW), pl.ds(0, (ncrs - 1) * LANES)], s3s.at[f]))

    def coarse_energy(f, scale=None):
        at = pl.ds(pl.multiple_of(b * LANES, LANES), LANES)
        total, mine, other = hs[...], sibs[f, LANES:LANES + 24], sibr[f, LANES:LANES + 24]
        if scale is not None:
            part = scale[0:1, at]
            total = total + part * hk[...]
            mine = mine + part * qk[0]
            other = other + part * qk[1]
        hk[...] = total
        qk[0] = mine
        qk[1] = other
        mine = hk[pl.ds(pl.multiple_of(24 + 24 * c, 8), 24), :] * mine
        other = hk[pl.ds(pl.multiple_of(48 - 24 * c, 8), 24), :] * other
        return 0.5 * jnp.sum(mine + other, axis=0, keepdims=True)

    def coarse_end(f, scale=None):
        settle(hb.at[f, pl.ds(0, 96), pl.ds(0, (ncrs - 1) * LANES)], s3r.at[f])
        value = hb[f]
        if scale is not None:
            value = value + scale[0:1, :] * hb[f - 1]
        high, low = split(value)
        h3[0:LANES, :] = high
        h3[LANES:2 * LANES, :] = low
        h3[2 * LANES:, :] = high

    row8 = rows_of((8, LANES))

    def packed(value):
        return jnp.concatenate([value[:, i * LANES:(i + 1) * LANES] for i in range(ncrs)], axis=0)

    def unpacked(value):
        return jnp.concatenate([value[i:i + 1] for i in range(ncrs)], axis=1)

    def sum_begin(n, first, second):
        rs[n] = jnp.concatenate([first, second], axis=0)
        for cc in range(2):
            for j in range(ncrs):
                if cc == 0 and j == 0:
                    rr[n, c * ncrs + b] = rs[n]
                    continue
                dev = (a if cc == 0 else sib, lax.rem(b + j, ncrs))
                remote(rs.at[n], rr.at[n, c * ncrs + b], r1s.at[n], r1r.at[n], dev).start()
        drains.append(lambda: settle(rr.at[n, pl.ds(0, 2 * ncrs - 1)], r1s.at[n]))

    def sum_gather(n):
        settle(rr.at[n, pl.ds(0, 2 * ncrs - 1)], r1r.at[n])
        er[n, k] = jnp.sum(rr[n], axis=0)

        def send(j, carry):
            to = 2 * lax.rem(k + j, chips) + c
            remote(er.at[n, k], er.at[n, k], r2s.at[n], r2r.at[n], (to, b)).start()
            return carry

        lax.fori_loop(1, chips, send, 0)
        drains.append(lambda: settle(er.at[n, pl.ds(0, chips - 1)], r2s.at[n]))

    def sum_end(n):
        settle(er.at[n, pl.ds(0, chips - 1)], r2r.at[n])
        total = jnp.sum(er[n], axis=0)
        return total[0:ncrs], total[ncrs:]

    def faces_start(n, which):
        copies = []
        for pos in which:
            copy = remote(tb.at[n % 2, pl.ds(pos * FACE, SENT)], rb.at[n % 2, pos ^ 1, pl.ds(0, SENT)],
                          fsend.at[n % 2, pos], frecv.at[n % 2, pos ^ 1], dests[pos])
            copy.start()
            copies.append(copy)
        return copies

    def faces_wait(copies):
        for copy in copies:
            copy.wait()

    def jumped(n, pos, extra=None):
        band = slice(pos * FACE, (pos + 1) * FACE)
        value = tb[n % 2, band, :] + rb[n % 2, pos]
        if extra is not None:
            value = value + extra
        if keeps[pos] is not None:
            value = jnp.where(keeps[pos], value, 0.0)
        return value

    def put_x(pos, value):
        high, low = split(value)
        lo = pos * FACE
        x3[lo:lo + FACE, :] = high
        x3[NX + lo:NX + lo + FACE, :] = low
        x3[2 * NX + lo:2 * NX + lo + FACE, :] = high

    pbuf[0, 0:NC] = apply_loads(0, NC)
    bch = dot_nt(bmat[...], chi).astype(BF16)
    bcl = dot_nt(bmat[...], clo).astype(BF16)
    l = rows_of((32, 1))
    da = div(l, 12)
    rem12 = l - 12 * da
    db = div(rem12, 6)
    where_l = 24 * (1 + da) + 6 * lax.rem(b + db, ncrs) + rem12 - 6 * db
    where_l = jnp.where(l < 24, where_l, -1000)
    lanes = cols_of((32, LANES))
    emaps = [hot(where_l + off == lanes) for off in (0, 24, -24)]
    wo[...] = dot(bch, emaps[0]) + dot(bcl, emaps[0])
    ws[0:2 * FACE, :] = wo[0:2 * FACE, :]
    for pos in (2, 3):
        band = slice(pos * FACE, (pos + 1) * FACE)
        ws[band, :] = dot(bch[band], emaps[pos - 1]) + dot(bcl[band], emaps[pos - 1])
    wcopies = [remote(ws.at[pl.ds(pos * FACE, FACE)], wr.at[pl.ds((pos ^ 1) * FACE, FACE)],
                      wsend.at[pos], wrecv.at[pos ^ 1], dests[pos]) for pos in range(4)]

    in_copies[1].wait()
    cip[0:cblock, 0:ncoarse] = civ[...]
    high, low = split(cip[...])
    i = cols_of((1, cbp))
    r = cblock * b + i
    plane = div(r, 24)
    base = lax.div(lax.div(cblock * b, 24), 2)
    target = 24 * ((plane >> 1) - base) + r - 24 * plane
    target = jnp.where((((plane + 1) & 1) == c) & (i < cblock), target, -1)
    pct = hot(target == rows_of((LANES, cbp)))
    x1h = dot(pct, high).astype(BF16)
    x1l = dot(pct, low).astype(BF16)
    i = rows_of((LANES, 1))
    r = 48 * k - 48 + i
    r = jnp.where((i < 120) & (r < ncoarse), r, -1)
    sel = hot(r == cols_of((LANES, ncp)))
    dall[b] = dot_nt(sel, x1h) + dot_nt(sel, x1l)
    in_copies[3].wait()

    def split_k(i, carry):
        at = pl.multiple_of(i * step, step)
        high, low = split(kv[pl.ds(at, step), :])
        khi[pl.ds(at, step), 0:nrows] = high
        klo[pl.ds(at, step), 0:nrows] = low
        return carry

    lax.fori_loop(0, whole // step, split_k, 0)
    tail[0:left_rows, 0:nrows] = kv[whole:nrows, :]
    high, low = split(tail[...])
    khi[whole:whole + 16, :] = high
    klo[whole:whole + 16, :] = low

    def face_rows(lo, hi):
        def tile(i, carry):
            at = pl.ds(pl.multiple_of(i * 256, 256), 256)
            a0hi[NC + lo:NC + hi, at] = dot(bmat[lo:hi, :], khi[:, at]).astype(BF16)
            a0lo[NC + lo:NC + hi, at] = dot(bmat[lo:hi, :], klo[:, at]).astype(BF16)
            return carry

        lax.fori_loop(0, nrp // 256, tile, 0)

    half = 2 * FACE
    face_rows(0, half)
    pl.semaphore_wait(barrier, greeted)
    coarse_begin(0, (0, 1))
    for copy in wcopies:
        copy.start()
    for j in range(1, ncrs):
        remote(dall.at[b], dall.at[b], csend.at[j], crecv.at[j], (a, lax.rem(b + j, ncrs))).start()
    tb[0, 0:half, :] = apply_loads(NC, NC + half)
    copies = faces_start(0, (0, 1))
    face_rows(half, NX)
    coarse_gather(0, (0, 1))
    tb[0, half:NX, :] = apply_loads(NC + half, NC + NX)
    copies += faces_start(0, (2, 3))

    for j in range(1, ncrs):
        copy = remote(dall.at[b], dall.at[b], csend.at[j], crecv.at[j], (a, lax.rem(b + j, ncrs)))
        copy.wait()
    total_hi = total_lo = None
    for blk_b in range(ncrs):
        j = rows_of((LANES, 1))
        pair = div(j, 24)
        rem = j - 24 * pair
        pair = pair + (cblock * blk_b // 24) // 2
        r = 24 * (2 * pair + 1 - c) + rem
        target = jnp.where((j < 120) & (r >= cblock * blk_b) & (r < cblock * (blk_b + 1)),
                           24 * (pair + 1 - c) + rem, -1)
        perm = hot(target == cols_of((LANES, chips * 24)))
        high, low = split(dall[blk_b])
        ph, plo = dot(high, perm), dot(low, perm)
        total_hi = ph if total_hi is None else total_hi + ph
        total_lo = plo if total_lo is None else total_lo + plo
    dphi[...] = total_hi.astype(BF16)
    dplo[...] = total_lo.astype(BF16)

    def between(i, carry):
        at = pl.ds(pl.multiple_of(i * half, half), half)
        src = pl.ds(pl.multiple_of(NC + i * half, 16), half)
        high = dot(a0hi[src, :], bmt[...]).astype(BF16)
        a3[at, 0:NX] = high
        a3[at, NX:2 * NX] = high
        a3[at, 2 * NX:] = dot(a0lo[src, :], bmt[...]).astype(BF16)
        return carry

    lax.fori_loop(0, 2, between, 0)
    coarse_copy = coarse_solve(0)

    in_copies[4].wait()
    nface = sv.shape[0]
    sp[0:nface, 0:nface] = sv[...]
    high, low = split(sp[...])
    khi[0:NX, 0:NX] = high
    klo[0:NX, 0:NX] = low
    for pos in range(4):
        face = ORDER[pos]
        sign = 0.5 if pos % 2 else -0.5
        j = rows_of((FACE, 1))
        target = jnp.where(j < fdof, j + face * fdof, -1)
        tmat[pos * FACE:(pos + 1) * FACE, :] = hot(target == cols_of((FACE, NX)), sign)
    pos_l = jnp.where(lane >= FACE, 1, 0) + jnp.where(lane >= 2 * FACE, 1, 0) + jnp.where(lane >= 3 * FACE, 1, 0)
    j = lane - FACE * pos_l
    target = jnp.where(j < fdof, j + fdof * ((pos_l + 2) & 3), -1)
    kept = jnp.where(pos_l == 2, jnp.where(a > 0, 0.5, 0.0), jnp.where(pos_l == 3, jnp.where(a < nsub - 1, 0.5, 0.0), 0.5))
    tmt[...] = jnp.where(target == rows_of((NX, NX)), signs * kept, 0.0).astype(BF16)

    def precond_rows(i, carry):
        at = pl.ds(pl.multiple_of(i * FACE, FACE), FACE)
        high = dot(tmat[at, :], khi[0:NX, 0:NX]).astype(BF16)
        low = dot(tmat[at, :], klo[0:NX, 0:NX]).astype(BF16)
        high = dot(high, tmt[...]).astype(BF16)
        to = pl.ds(pl.multiple_of(NW + i * FACE, 16), FACE)
        m3[to, 0:NX] = high
        m3[to, NX:2 * NX] = high
        m3[to, 2 * NX:] = dot(low, tmt[...]).astype(BF16)
        return carry

    coarse_spread(0, coarse_copy)
    lax.fori_loop(0, 4, precond_rows, 0)

    for copy in wcopies:
        copy.wait()
    for pos in range(4):
        band = slice(pos * FACE, (pos + 1) * FACE)
        value = wo[band, :] + wr[band, :]
        if keeps[pos] is not None:
            value = jnp.where(keeps[pos], value, 0.0)
        wo[band, :] = value
    high, low = split(wo[...])
    w3[:, 0:LANES] = high
    w3[:, LANES:2 * LANES] = high
    w3[:, 2 * LANES:] = low
    high, low = split(jnp.transpose(wo[...]))
    mhi, mlo = m3[NW:, 0:NX], m3[NW:, 2 * NX:]
    high, low = split((dot(high, mhi) + dot(high, mlo) + dot(low, mhi))[0:NW])
    m3[0:NW, 0:NX] = high
    m3[0:NW, NX:2 * NX] = high
    m3[0:NW, 2 * NX:] = low

    def operator_end(n, f, copies, use, scale=None):
        coarse_end(f, scale)
        faces_wait(copies)
        for pos in range(4):
            use(pos, jumped(n, pos, dot(w3[pos * FACE:(pos + 1) * FACE, :], h3[...])))

    def first_use(pos, value):
        rv[pos * FACE:(pos + 1) * FACE, :] = value
        put_x(pos, value)

    operator_end(0, 0, copies, first_use)

    around = (-1, 0, 1, 2)

    def precond(n, f, total):
        block = dot(m3[0:NW + half, :], x3[...])
        pbuf[f] = block[0:NW]
        coarse_begin(f, around)
        tb[n % 2, 0:half, :] = block[NW:]
        copies = []
        if total is None:
            copies += faces_start(n, (0, 1))
        tb[n % 2, half:, :] = dot(m3[NW + half:, :], x3[...])
        if total is None:
            copies += faces_start(n, (2, 3))
        rz_part = packed(jnp.sum(rv[...] * tb[n % 2], axis=0, keepdims=True))
        if total is not None:
            sum_begin(total, rz_part, jnp.zeros((ncrs, LANES), F32))
            copies += faces_start(n, (0, 1, 2, 3))
        coarse_gather(f, around)
        if total is not None:
            sum_gather(total)
        coarse_copy = coarse_solve(f)
        faces_wait(copies)
        return coarse_copy, rz_part

    def operator(n, f, rz_part, scale):
        tb[n % 2, 0:half, :] = dot(a3[0:half, :], x3[...])
        tb[n % 2, half:, :] = dot(a3[half:, :], x3[...])
        energy = packed(jnp.sum(dv[...] * tb[n % 2], axis=0, keepdims=True))
        energy = energy + jnp.where(rows_of((ncrs, LANES)) == b, coarse_energy(f, scale), 0.0)
        sum_begin(f, rz_part, energy)
        copies = faces_start(n, (0, 1, 2, 3))
        sum_gather(f)
        return copies

    def keep_image(n):
        def use(pos, value):
            tb[n % 2, pos * FACE:(pos + 1) * FACE, :] = value
        return use

    coarse_copy, rz_part = precond(1, 1, None)
    for pos in range(4):
        value = jumped(1, pos)
        dv[pos * FACE:(pos + 1) * FACE, :] = value
        put_x(pos, value)

    coarse_spread(1, coarse_copy)
    copies = operator(2, 1, rz_part, None)
    operator_end(2, 1, copies, keep_image(2))
    rz_now, energy = sum_end(1)
    alpha = unpacked(rz_now / energy)
    for pos in range(4):
        band = slice(pos * FACE, (pos + 1) * FACE)
        value = rv[band, :] - alpha * tb[0, band, :]
        rv[band, :] = value
        put_x(pos, value)

    coarse_copy, rz_part = precond(3, 2, 0)
    coarse_spread(2, coarse_copy)
    for pos in range(4):
        band = slice(pos * FACE, (pos + 1) * FACE)
        mv[band, :] = alpha * dv[band, :]
    rz_next, _ = sum_end(0)
    beta = unpacked(rz_next / rz_now)
    co[0:1, :] = beta
    for pos in range(4):
        band = slice(pos * FACE, (pos + 1) * FACE)
        value = jumped(3, pos) + beta * dv[band, :]
        dv[band, :] = value
        put_x(pos, value)

    copies = operator(4, 2, rz_next, co)
    operator_end(4, 2, copies, keep_image(4), co)
    _, energy = sum_end(2)
    alpha = unpacked(rz_next / energy)
    out_copies = []
    for pos in range(4):
        band = slice(pos * FACE, (pos + 1) * FACE)
        outs[pos] = (mv[band, :] + alpha * dv[band, :])[0:fdof]
        outs[4 + pos] = (rv[band, :] - alpha * tb[0, band, :])[0:fdof]
        for side, ref in enumerate((mo, ro)):
            copy = pltpu.make_async_copy(outs.at[4 * side + pos], ref.at[0, :, ORDER[pos]], osem.at[4 * side + pos])
            copy.start()
            out_copies.append(copy)
    for copy in out_copies:
        copy.wait()

    for drain in drains:
        drain()


def body(face_index, kinv, schur, corner, coarse_inverse, loads):
    nsub = lax.axis_size("sub")
    ncrs = lax.axis_size("crs")
    fdof = face_index.shape[2]
    nrows, cases = loads.shape[1:]
    ncoarse = coarse_inverse.shape[1]
    nface = schur.shape[1]
    ncl = corner.shape[2]
    chips = nsub // 2
    nrp = -(-nrows // 256) * 256
    cbp = -(-coarse_inverse.shape[0] // 16) * 16
    ncp = -(-ncoarse // LANES) * LANES
    vm = pltpu.VMEM
    dma = pltpu.SemaphoreType.DMA
    scratch = [
        vm((nrows, nrows), F32), vm((nrows, cases), F32), vm((ncl, nrows), F32), vm((nface, nface), F32),
        vm(coarse_inverse.shape, F32),
        vm((nrp, nrp), BF16), vm((nrp, nrp), BF16), vm((16, nrp), F32),
        vm((8, NX), jnp.int32), vm((NX, 8), jnp.int32),
        vm((NX, nrp), BF16), vm((nrp, NX), BF16), vm((NA, nrp), BF16), vm((NA, nrp), BF16),
        vm((nrp, cases), BF16), vm((nrp, cases), BF16),
        vm((NX, 3 * NX), BF16), vm((NW + NX, 3 * NX), BF16), vm((NX, 3 * LANES), BF16), vm((3 * NX, cases), BF16),
        vm((32, nrp), F32), vm((cbp, ncp), F32),
        vm((NX, NX), F32), vm((NX, NX), BF16), vm((NX, NX), BF16),
        vm((NX, LANES), F32), vm((NX, LANES), F32), vm((NX, LANES), F32),
        vm((ncrs, LANES, LANES), F32), vm((LANES, chips * 24), BF16), vm((LANES, chips * 24), BF16),
        vm((2, NX, cases), F32), vm((2, 4, FACE, cases), F32),
        vm((NX, cases), F32), vm((NX, cases), F32), vm((NX, cases), F32),
        vm((3, NW, cases), F32), vm((3, 4 * ncrs, 24, LANES), F32), vm((3, chips, 24, LANES), F32),
        vm((3, LANES + 24, LANES), F32), vm((3, LANES + 24, LANES), F32), vm((LANES, LANES), F32), vm((LANES, LANES), F32),
        vm((2, 24, LANES), F32), vm((3, LANES, cases), F32), vm((3 * LANES, cases), BF16),
        vm((3, 8, LANES), F32), vm((3, 2 * ncrs, 8, LANES), F32), vm((3, chips, 8, LANES), F32),
        vm((8, cases), F32), vm((8, fdof, cases), F32),
        dma((5,)), dma((8,)), dma((2, 4)), dma((2, 4)), dma((4,)), dma((4,)), dma((ncrs,)), dma((ncrs,)),
    ] + [dma((3,)) for _ in range(12)]
    out = jax.ShapeDtypeStruct((1, fdof, 4, cases), F32)
    anyspace = pl.BlockSpec(memory_space=pl.ANY)
    inside = pl.BlockSpec(memory_space=pltpu.VMEM)
    dims = (nsub, ncrs, nrows, fdof, cases, ncoarse)
    mult, resid = pl.pallas_call(
        functools.partial(kernel, dims),
        out_shape=(out, out),
        in_specs=[inside] + [anyspace] * 5,
        out_specs=(anyspace, anyspace),
        scratch_shapes=scratch,
        compiler_params=pltpu.CompilerParams(
            collective_id=0, has_side_effects=True, vmem_limit_bytes=63 * 2**20),
    )(face_index, jnp.swapaxes(kinv, 0, 1), jnp.swapaxes(schur, 0, 1),
      jnp.swapaxes(corner, 1, 2), coarse_inverse, jnp.swapaxes(loads, 0, 1))
    return jnp.swapaxes(mult, 1, 2), jnp.swapaxes(resid, 1, 2)


def solution(mesh):
    subs = P(("sub", "crs"), None, None)
    out = P(("sub", "crs"), None, None, None)
    return jax.shard_map(
        body, mesh=mesh, in_specs=(subs, subs, subs, subs, P("crs", None), subs), out_specs=(out, out),
        check_vma=False)
```

```python
import functools

import jax
import jax.numpy as jnp
from jax import lax
from jax.experimental import pallas as pl
from jax.experimental.pallas import tpu as pltpu
from jax.sharding import PartitionSpec as P

F32 = jnp.float32
BF16 = jnp.bfloat16
MESH = pl.DeviceIdType.MESH

FACE = 160
SENT = 152
NX = 4 * FACE
NC = 48
NW = 96
NA = NX + NC
ORDER = (2, 3, 0, 1)
LANES = 128


def dot(left, right):
    return jnp.dot(left, right, preferred_element_type=F32)


def dot_nt(left, right):
    return lax.dot_general(left, right, (((1,), (1,)), ((), ())), preferred_element_type=F32)


def split(value):
    high = value.astype(BF16)
    return high, (value - high.astype(F32)).astype(BF16)


def hot(cond, value=1.0):
    return jnp.where(cond, value, 0.0).astype(BF16)


def rows_of(shape):
    return lax.broadcasted_iota(jnp.int32, shape, 0)


def cols_of(shape):
    return lax.broadcasted_iota(jnp.int32, shape, 1)


def div(value, by):
    return (value * (65536 // by + 1)) >> 16


def kernel(dims, faces, kinv, schur, corner, cinv, loads, mo, ro,
           kv, lv, cv, sv, civ, khi, klo, tail, idxr, idxc, bmat, bmt, a0hi, a0lo, lhi, llo, a3, m3, w3, x3,
           cpad, cip, sp, tmt, ws, wo, wr, dall, dphi, dplo,
           tb, rb, rv, dv, mv, pbuf, p0, gb, sibs, sibr, hs, hk, qk, hb, h3,
           rs, rr, er, co, outs,
           dsem, osem, fsend, frecv, wsend, wrecv, csend, crecv,
           s1s, s1r, s2s, s2r, bs, br, s3s, s3r, r1s, r1r, r2s, r2r):
    nsub, ncrs, nrows, fdof, cases, ncoarse = dims
    chips = nsub // 2
    nrp = khi.shape[1]
    cblock = ncoarse // ncrs
    cbp, ncp = cip.shape
    a = lax.axis_index("sub")
    b = lax.axis_index("crs")
    k = lax.div(a, 2)
    c = lax.rem(a, 2)
    sib = 2 * k + 1 - c
    up = lax.rem(a + 1, nsub)
    down = lax.rem(a + nsub - 1, nsub)
    left = lax.rem(b + ncrs - 1, ncrs)
    right = lax.rem(b + 1, ncrs)
    dests = ((a, left), (a, right), (down, b), (up, b))
    keeps = (None, None, a > 0, a < nsub - 1)
    drains = []

    def local(src, dst, n):
        return pltpu.make_async_copy(src, dst, dsem.at[n])

    def remote(src, dst, ssem, rsem, dev):
        return pltpu.make_async_remote_copy(
            src_ref=src, dst_ref=dst, send_sem=ssem, recv_sem=rsem, device_id=dev, device_id_type=MESH)

    def settle(ref, sem):
        pltpu.make_async_copy(ref, ref, sem).wait()

    in_copies = [local(corner.at[0], cv, 0), local(cinv, civ, 1), local(loads.at[:, 0], lv, 2),
                 local(kinv.at[:, 0], kv, 3)]
    in_copies += [local(schur.at[pl.ds(ORDER[pos] * fdof, fdof), 0], sv.at[pos], 4 + pos) for pos in range(4)]
    for copy in in_copies:
        copy.start()

    barrier = pltpu.get_barrier_semaphore()
    for j in range(1, ncrs):
        pl.semaphore_signal(barrier, inc=1, device_id=(a, lax.rem(b + j, ncrs)), device_id_type=MESH)
    for j in range(ncrs):
        pl.semaphore_signal(barrier, inc=1, device_id=(up, j), device_id_type=MESH)
        pl.semaphore_signal(barrier, inc=1, device_id=(down, j), device_id_type=MESH)
    for j in range(1, ncrs):
        to = lax.rem(b + j, ncrs)
        pl.semaphore_signal(barrier, inc=1, device_id=(lax.rem(a + 2, nsub), to), device_id_type=MESH)
        pl.semaphore_signal(barrier, inc=1, device_id=(lax.rem(a + nsub - 2, nsub), to), device_id_type=MESH)

    def greet(j, carry):
        pl.semaphore_signal(barrier, inc=1, device_id=(2 * lax.rem(k + j, chips) + c, b), device_id_type=MESH)
        return carry

    lax.fori_loop(1, chips, greet, 0)

    greeted = ncrs - 1 + 2 * ncrs + 2 * (ncrs - 1) + chips - 1

    idxr[...] = jnp.full(idxr.shape, -1, jnp.int32)
    for pos in range(4):
        face = ORDER[pos]
        idxr[0:1, pos * FACE:pos * FACE + fdof] = faces[0, face:face + 1, :]
    idxc[...] = jnp.transpose(idxr[...])
    for pos in range(4):
        sign = 1.0 if pos % 2 else -1.0
        band = slice(pos * FACE, (pos + 1) * FACE)
        bmat[band, :] = hot(idxc[band, 0:1] == cols_of((FACE, nrp)), sign)
    lane = cols_of((1, NX))
    signs = jnp.where(((lane >= FACE) & (lane < 2 * FACE)) | (lane >= 3 * FACE), 1.0, -1.0)

    def build_bmt(i, carry):
        at = pl.multiple_of(i * LANES, LANES)
        rows = rows_of((LANES, NX)) + at
        bmt[pl.ds(at, LANES), :] = jnp.where(idxr[0:1, :] == rows, signs, 0.0).astype(BF16)
        return carry

    lax.fori_loop(0, nrp // LANES, build_bmt, 0)

    for n in range(2):
        for pos in range(4):
            rb[n, pos, SENT:FACE, :] = jnp.zeros((FACE - SENT, cases), F32)
    hb[:, 96:LANES, :] = jnp.zeros((3, 32, cases), F32)
    cpad[...] = jnp.zeros(cpad.shape, F32)
    cip[...] = jnp.zeros(cip.shape, F32)
    sp[...] = jnp.zeros(sp.shape, F32)
    edge = nrp - LANES
    khi[:, edge:] = jnp.zeros((nrp, LANES), BF16)
    klo[:, edge:] = jnp.zeros((nrp, LANES), BF16)
    whole = nrows // 16 * 16
    for ref in (khi, klo, lhi, llo):
        ref[whole:, :] = jnp.zeros((nrp - whole, ref.shape[1]), BF16)
    tail[...] = jnp.zeros(tail.shape, F32)

    in_copies[0].wait()
    ncl = cv.shape[0]
    cpad[0:ncl, 0:nrows] = cv[...]
    chi, clo = split(cpad[...])
    l = cols_of((1, 32))
    da = div(l, 12)
    rem12 = l - 12 * da
    db = div(rem12, 6)
    where_l = jnp.where(l < 24, 24 * da + 6 * lax.rem(b + db, ncrs) + rem12 - 6 * db, -1000)
    sel = hot(where_l == rows_of((NC, 32)))
    a0hi[0:NC, :] = dot(sel, chi).astype(BF16)
    a0lo[0:NC, :] = dot(sel, clo).astype(BF16)
    in_copies[2].wait()
    step = 16 * 5

    def split_loads(i, carry):
        at = pl.multiple_of(i * step, step)
        high, low = split(lv[pl.ds(at, step), :])
        lhi[pl.ds(at, step), :] = high
        llo[pl.ds(at, step), :] = low
        return carry

    lax.fori_loop(0, whole // step, split_loads, 0)
    left_rows = nrows - whole
    tail[0:left_rows, 0:cases] = lv[whole:nrows, :]
    high, low = split(tail[:, 0:cases])
    lhi[whole:whole + 16, :] = high
    llo[whole:whole + 16, :] = low

    def apply_loads(lo, hi):
        high, low = a0hi[lo:hi, :], a0lo[lo:hi, :]
        return dot(high, lhi[...]) + dot(high, llo[...]) + dot(low, lhi[...])

    def coarse_begin(f, offs):
        for i, off in enumerate(offs):
            owner = lax.rem(a + off + nsub, nsub)
            for j in range(ncrs):
                to = lax.rem(b + j, ncrs)
                at = pl.ds(pl.multiple_of(to * LANES, LANES), LANES)
                band = pl.ds(24 * i, 24)
                if off == 0 and j == 0:
                    p0[f, i * ncrs + b] = pbuf[f, band, at]
                    continue
                remote(pbuf.at[f, band, at], p0.at[f, i * ncrs + b], s1s.at[f], s1r.at[f], (owner, to)).start()
        drains.append(lambda: settle(p0.at[f, pl.ds(0, ncrs * len(offs) - 1)], s1s.at[f]))

    def coarse_gather(f, offs):
        count = ncrs * len(offs)
        settle(p0.at[f, pl.ds(0, count - 1)], s1r.at[f])
        gb[f, k] = jnp.sum(p0[f, 0:count], axis=0)

        def send(j, carry):
            to = 2 * lax.rem(k + j, chips) + c
            remote(gb.at[f, k], gb.at[f, k], s2s.at[f], s2r.at[f], (to, b)).start()
            return carry

        lax.fori_loop(1, chips, send, 0)
        drains.append(lambda: settle(gb.at[f, pl.ds(0, chips - 1)], s2s.at[f]))

    def coarse_solve(f):
        settle(gb.at[f, pl.ds(0, chips - 1)], s2r.at[f])
        high, low = split(gb[f].reshape(chips * 24, LANES))
        sibs[f, 0:LANES] = dot(dphi[...], high) + dot(dphi[...], low) + dot(dplo[...], high)
        sibs[f, LANES:LANES + 24] = gb[f, k]
        copy = remote(sibs.at[f], sibr.at[f], bs.at[f], br.at[f], (sib, b))
        copy.start()
        return copy

    def coarse_spread(f, copy):
        copy.wait()
        at = pl.ds(pl.multiple_of(b * LANES, LANES), LANES)
        total = sibs[f, 0:LANES] + sibr[f, 0:LANES]
        hs[...] = total
        hb[f, 0:NW, at] = hs[pl.ds(pl.multiple_of(24 * c, 8), NW), :]
        for j in range(1, ncrs):
            remote(hb.at[f, pl.ds(0, NW), at], hb.at[f, pl.ds(0, NW), at], s3s.at[f], s3r.at[f],
                   (a, lax.rem(b + j, ncrs))).start()
        drains.append(lambda: settle(hb.at[f, pl.ds(0, NW), pl.ds(0, (ncrs - 1) * LANES)], s3s.at[f]))

    def coarse_energy(f, scale=None):
        at = pl.ds(pl.multiple_of(b * LANES, LANES), LANES)
        total, mine, other = hs[...], sibs[f, LANES:LANES + 24], sibr[f, LANES:LANES + 24]
        if scale is not None:
            part = scale[0:1, at]
            total = total + part * hk[...]
            mine = mine + part * qk[0]
            other = other + part * qk[1]
        hk[...] = total
        qk[0] = mine
        qk[1] = other
        mine = hk[pl.ds(pl.multiple_of(24 + 24 * c, 8), 24), :] * mine
        other = hk[pl.ds(pl.multiple_of(48 - 24 * c, 8), 24), :] * other
        return 0.5 * jnp.sum(mine + other, axis=0, keepdims=True)

    def coarse_end(f, scale=None):
        settle(hb.at[f, pl.ds(0, 96), pl.ds(0, (ncrs - 1) * LANES)], s3r.at[f])
        value = hb[f]
        if scale is not None:
            value = value + scale[0:1, :] * hb[f - 1]
        high, low = split(value)
        h3[0:LANES, :] = high
        h3[LANES:2 * LANES, :] = low
        h3[2 * LANES:, :] = high

    row8 = rows_of((8, LANES))

    def packed(value):
        return jnp.concatenate([value[:, i * LANES:(i + 1) * LANES] for i in range(ncrs)], axis=0)

    def unpacked(value):
        return jnp.concatenate([value[i:i + 1] for i in range(ncrs)], axis=1)

    def sum_begin(n, first, second):
        rs[n] = jnp.concatenate([first, second], axis=0)
        for cc in range(2):
            for j in range(ncrs):
                if cc == 0 and j == 0:
                    rr[n, c * ncrs + b] = rs[n]
                    continue
                dev = (a if cc == 0 else sib, lax.rem(b + j, ncrs))
                remote(rs.at[n], rr.at[n, c * ncrs + b], r1s.at[n], r1r.at[n], dev).start()
        drains.append(lambda: settle(rr.at[n, pl.ds(0, 2 * ncrs - 1)], r1s.at[n]))

    def sum_gather(n):
        settle(rr.at[n, pl.ds(0, 2 * ncrs - 1)], r1r.at[n])
        er[n, k] = jnp.sum(rr[n], axis=0)

        def send(j, carry):
            to = 2 * lax.rem(k + j, chips) + c
            remote(er.at[n, k], er.at[n, k], r2s.at[n], r2r.at[n], (to, b)).start()
            return carry

        lax.fori_loop(1, chips, send, 0)
        drains.append(lambda: settle(er.at[n, pl.ds(0, chips - 1)], r2s.at[n]))

    def sum_end(n):
        settle(er.at[n, pl.ds(0, chips - 1)], r2r.at[n])
        total = jnp.sum(er[n], axis=0)
        return total[0:ncrs], total[ncrs:]

    def late_begin(n, first, second):
        er[n, k] = jnp.concatenate([first, second], axis=0)

        def send(j, carry):
            to = 2 * lax.rem(k + j, chips) + c
            remote(er.at[n, k], er.at[n, k], r2s.at[n], r2r.at[n], (to, b)).start()
            return carry

        lax.fori_loop(1, chips, send, 0)
        drains.append(lambda: settle(er.at[n, pl.ds(0, chips - 1)], r2s.at[n]))

    def late_spread(n):
        settle(er.at[n, pl.ds(0, chips - 1)], r2r.at[n])
        mine = rr.at[n, c * ncrs + b]
        rr[n, c * ncrs + b] = jnp.sum(er[n], axis=0)
        for cc in range(2):
            for j in range(ncrs):
                if cc == 0 and j == 0:
                    continue
                dev = (a if cc == 0 else sib, lax.rem(b + j, ncrs))
                remote(mine, mine, r1s.at[n], r1r.at[n], dev).start()
        drains.append(lambda: settle(rr.at[n, pl.ds(0, 2 * ncrs - 1)], r1s.at[n]))

    def late_end(n):
        settle(rr.at[n, pl.ds(0, 2 * ncrs - 1)], r1r.at[n])
        total = jnp.sum(rr[n], axis=0)
        return total[0:ncrs], total[ncrs:]

    def faces_start(n, which):
        copies = []
        for pos in which:
            copy = remote(tb.at[n % 2, pl.ds(pos * FACE, SENT)], rb.at[n % 2, pos ^ 1, pl.ds(0, SENT)],
                          fsend.at[n % 2, pos], frecv.at[n % 2, pos ^ 1], dests[pos])
            copy.start()
            copies.append(copy)
        return copies

    def faces_wait(copies):
        for copy in copies:
            copy.wait()

    def jumped(n, pos, extra=None):
        band = slice(pos * FACE, (pos + 1) * FACE)
        value = tb[n % 2, band, :] + rb[n % 2, pos]
        if extra is not None:
            value = value + extra
        if keeps[pos] is not None:
            value = jnp.where(keeps[pos], value, 0.0)
        return value

    def put_x(pos, value):
        high, low = split(value)
        lo = pos * FACE
        x3[lo:lo + FACE, :] = high
        x3[NX + lo:NX + lo + FACE, :] = low
        x3[2 * NX + lo:2 * NX + lo + FACE, :] = high

    both = dot(jnp.concatenate([a0hi[0:NC, :], a0lo[0:NC, :]], axis=0), lhi[...])
    pbuf[0, 0:NC] = both[0:NC] + both[NC:] + dot(a0hi[0:NC, :], llo[...])
    pl.semaphore_wait(barrier, greeted)
    coarse_begin(0, (0, 1))

    in_copies[1].wait()
    cip[0:cblock, 0:ncoarse] = civ[...]
    high, low = split(cip[...])
    i = cols_of((1, cbp))
    r = cblock * b + i
    plane = div(r, 24)
    base = lax.div(lax.div(cblock * b, 24), 2)
    target = 24 * ((plane >> 1) - base) + r - 24 * plane
    target = jnp.where((((plane + 1) & 1) == c) & (i < cblock), target, -1)
    pct = hot(target == rows_of((LANES, cbp)))
    x1h = dot(pct, high).astype(BF16)
    x1l = dot(pct, low).astype(BF16)
    i = rows_of((LANES, 1))
    r = 48 * k - 48 + i
    r = jnp.where((i < 120) & (r < ncoarse), r, -1)
    sel = hot(r == cols_of((LANES, ncp)))
    dall[b] = dot_nt(sel, x1h) + dot_nt(sel, x1l)
    for j in range(1, ncrs):
        remote(dall.at[b], dall.at[b], csend.at[j], crecv.at[j], (a, lax.rem(b + j, ncrs))).start()

    bch = dot_nt(bmat[...], chi).astype(BF16)
    bcl = dot_nt(bmat[...], clo).astype(BF16)
    l = rows_of((32, 1))
    da = div(l, 12)
    rem12 = l - 12 * da
    db = div(rem12, 6)
    where_l = 24 * (1 + da) + 6 * lax.rem(b + db, ncrs) + rem12 - 6 * db
    where_l = jnp.where(l < 24, where_l, -1000)
    lanes = cols_of((32, LANES))
    emaps = [hot(where_l + off == lanes) for off in (0, 24, -24)]
    wo[...] = dot(bch, emaps[0]) + dot(bcl, emaps[0])
    ws[0:2 * FACE, :] = wo[0:2 * FACE, :]
    for pos in (2, 3):
        band = slice(pos * FACE, (pos + 1) * FACE)
        ws[band, :] = dot(bch[band], emaps[pos - 1]) + dot(bcl[band], emaps[pos - 1])
    wcopies = [remote(ws.at[pl.ds(pos * FACE, FACE)], wr.at[pl.ds((pos ^ 1) * FACE, FACE)],
                      wsend.at[pos], wrecv.at[pos ^ 1], dests[pos]) for pos in range(4)]
    for copy in wcopies:
        copy.start()

    in_copies[3].wait()

    def split_k(i, carry):
        at = pl.multiple_of(i * step, step)
        high, low = split(kv[pl.ds(at, step), :])
        khi[pl.ds(at, step), 0:nrows] = high
        klo[pl.ds(at, step), 0:nrows] = low
        return carry

    lax.fori_loop(0, whole // step, split_k, 0)
    tail[0:left_rows, 0:nrows] = kv[whole:nrows, :]
    high, low = split(tail[...])
    khi[whole:whole + 16, :] = high
    klo[whole:whole + 16, :] = low

    def face_rows(lo, hi):
        def tile(i, carry):
            at = pl.ds(pl.multiple_of(i * 256, 256), 256)
            a0hi[NC + lo:NC + hi, at] = dot(bmat[lo:hi, :], khi[:, at]).astype(BF16)
            a0lo[NC + lo:NC + hi, at] = dot(bmat[lo:hi, :], klo[:, at]).astype(BF16)
            return carry

        lax.fori_loop(0, nrp // 256, tile, 0)

    half = 2 * FACE
    face_rows(0, half)
    tb[0, 0:half, :] = apply_loads(NC, NC + half)
    copies = faces_start(0, (0, 1))
    face_rows(half, NX)
    coarse_gather(0, (0, 1))
    tb[0, half:NX, :] = apply_loads(NC + half, NC + NX)
    copies += faces_start(0, (2, 3))

    for j in range(1, ncrs):
        copy = remote(dall.at[b], dall.at[b], csend.at[j], crecv.at[j], (a, lax.rem(b + j, ncrs)))
        copy.wait()
    total_hi = total_lo = None
    for blk_b in range(ncrs):
        j = rows_of((LANES, 1))
        pair = div(j, 24)
        rem = j - 24 * pair
        pair = pair + (cblock * blk_b // 24) // 2
        r = 24 * (2 * pair + 1 - c) + rem
        target = jnp.where((j < 120) & (r >= cblock * blk_b) & (r < cblock * (blk_b + 1)),
                           24 * (pair + 1 - c) + rem, -1)
        perm = hot(target == cols_of((LANES, chips * 24)))
        high, low = split(dall[blk_b])
        ph, plo = dot(high, perm), dot(low, perm)
        total_hi = ph if total_hi is None else total_hi + ph
        total_lo = plo if total_lo is None else total_lo + plo
    dphi[...] = total_hi.astype(BF16)
    dplo[...] = total_lo.astype(BF16)

    def between(i, carry):
        at = pl.ds(pl.multiple_of(i * half, half), half)
        src = pl.ds(pl.multiple_of(NC + i * half, 16), half)
        high = dot(a0hi[src, :], bmt[...]).astype(BF16)
        a3[at, 0:NX] = high
        a3[at, NX:2 * NX] = high
        a3[at, 2 * NX:] = dot(a0lo[src, :], bmt[...]).astype(BF16)
        return carry

    coarse_copy = coarse_solve(0)

    nface = sv.shape[2]
    for pos in range(4):
        in_copies[4 + pos].wait()
        sp[pos * FACE:pos * FACE + fdof, 0:nface] = sv[pos] * (0.5 if pos % 2 else -0.5)
    high, low = split(sp[...])
    khi[0:NX, 0:NX] = high
    klo[0:NX, 0:NX] = low
    pos_l = jnp.where(lane >= FACE, 1, 0) + jnp.where(lane >= 2 * FACE, 1, 0) + jnp.where(lane >= 3 * FACE, 1, 0)
    j = lane - FACE * pos_l
    target = jnp.where(j < fdof, j + fdof * ((pos_l + 2) & 3), -1)
    kept = jnp.where(pos_l == 2, jnp.where(a > 0, 0.5, 0.0), jnp.where(pos_l == 3, jnp.where(a < nsub - 1, 0.5, 0.0), 0.5))
    tmt[...] = jnp.where(target == rows_of((NX, NX)), signs * kept, 0.0).astype(BF16)

    def precond_rows(i, carry):
        at = pl.ds(pl.multiple_of(i * FACE, FACE), FACE)
        high = dot(khi[at, 0:NX], tmt[...]).astype(BF16)
        low = klo[at, 0:NX]
        to = pl.ds(pl.multiple_of(NW + i * FACE, 16), FACE)
        m3[to, 0:NX] = high
        m3[to, NX:2 * NX] = high
        m3[to, 2 * NX:] = dot(low, tmt[...]).astype(BF16)
        return carry

    coarse_spread(0, coarse_copy)
    lax.fori_loop(0, 4, precond_rows, 0)

    for copy in wcopies:
        copy.wait()
    for pos in range(4):
        band = slice(pos * FACE, (pos + 1) * FACE)
        value = wo[band, :] + wr[band, :]
        if keeps[pos] is not None:
            value = jnp.where(keeps[pos], value, 0.0)
        wo[band, :] = value
    high, low = split(wo[...])
    w3[:, 0:LANES] = high
    w3[:, LANES:2 * LANES] = high
    w3[:, 2 * LANES:] = low
    high, low = split(jnp.transpose(wo[...]))
    mhi, mlo = m3[NW:, 0:NX], m3[NW:, 2 * NX:]
    both = dot(jnp.concatenate([high[0:NW], low[0:NW]], axis=0), mhi)
    high, low = split(both[0:NW] + both[NW:] + dot(high[0:NW], mlo))
    m3[0:NW, 0:NX] = high
    m3[0:NW, NX:2 * NX] = high
    m3[0:NW, 2 * NX:] = low

    def operator_end(n, f, copies, use, scale=None):
        coarse_end(f, scale)
        faces_wait(copies)
        for pos in range(4):
            use(pos, jumped(n, pos, dot(w3[pos * FACE:(pos + 1) * FACE, :], h3[...])))

    def first_use(pos, value):
        rv[pos * FACE:(pos + 1) * FACE, :] = value
        put_x(pos, value)

    operator_end(0, 0, copies, first_use)

    around = (-1, 0, 1, 2)

    def precond(n, f, total, idle):
        block = dot(m3[0:NW + half, :], x3[...])
        pbuf[f] = block[0:NW]
        coarse_begin(f, around)
        tb[n % 2, 0:half, :] = block[NW:]
        copies = []
        if total is None:
            copies += faces_start(n, (0, 1))
        tb[n % 2, half:, :] = dot(m3[NW + half:, :], x3[...])
        if total is None:
            copies += faces_start(n, (2, 3))
        rz_part = packed(jnp.sum(rv[...] * tb[n % 2], axis=0, keepdims=True))
        if total is not None:
            sum_begin(total, rz_part, jnp.zeros((ncrs, LANES), F32))
            copies += faces_start(n, (0, 1, 2, 3))
            sum_gather(total)
        coarse_gather(f, around)
        idle()
        faces_wait(copies)
        return rz_part

    def operator(n, f, rz_part, scale):
        tb[n % 2, 0:half, :] = dot(a3[0:half, :], x3[...])
        copies = faces_start(n, (0, 1))
        tb[n % 2, half:, :] = dot(a3[half:, :], x3[...])
        copies += faces_start(n, (2, 3))
        energy = packed(jnp.sum(dv[...] * tb[n % 2], axis=0, keepdims=True))
        coarse_spread(f, coarse_solve(f))
        energy = energy + jnp.where(rows_of((ncrs, LANES)) == b, coarse_energy(f, scale), 0.0)
        late_begin(f, rz_part, energy)
        late_spread(f)
        return copies

    def keep_image(n):
        def use(pos, value):
            tb[n % 2, pos * FACE:(pos + 1) * FACE, :] = value
        return use

    rz_part = precond(1, 1, None, lambda: lax.fori_loop(0, 2, between, 0))
    for pos in range(4):
        value = jumped(1, pos)
        dv[pos * FACE:(pos + 1) * FACE, :] = value
        put_x(pos, value)

    copies = operator(2, 1, rz_part, None)
    operator_end(2, 1, copies, keep_image(2))
    rz_now, energy = late_end(1)
    alpha = unpacked(rz_now / energy)
    for pos in range(4):
        band = slice(pos * FACE, (pos + 1) * FACE)
        value = rv[band, :] - alpha * tb[0, band, :]
        rv[band, :] = value
        put_x(pos, value)

    def first_multipliers():
        for pos in range(4):
            band = slice(pos * FACE, (pos + 1) * FACE)
            mv[band, :] = alpha * dv[band, :]

    rz_part = precond(3, 2, 0, first_multipliers)
    rz_next, _ = sum_end(0)
    beta = unpacked(rz_next / rz_now)
    co[0:1, :] = beta
    for pos in range(4):
        band = slice(pos * FACE, (pos + 1) * FACE)
        value = jumped(3, pos) + beta * dv[band, :]
        dv[band, :] = value
        put_x(pos, value)

    copies = operator(4, 2, rz_next, co)
    operator_end(4, 2, copies, keep_image(4), co)
    _, energy = late_end(2)
    alpha = unpacked(rz_next / energy)
    out_copies = []
    for pos in range(4):
        band = slice(pos * FACE, (pos + 1) * FACE)
        outs[pos] = (mv[band, :] + alpha * dv[band, :])[0:fdof]
        outs[4 + pos] = (rv[band, :] - alpha * tb[0, band, :])[0:fdof]
        for side, ref in enumerate((mo, ro)):
            copy = pltpu.make_async_copy(outs.at[4 * side + pos], ref.at[0, :, ORDER[pos]], osem.at[4 * side + pos])
            copy.start()
            out_copies.append(copy)
    for copy in out_copies:
        copy.wait()

    for drain in drains:
        drain()


def body(face_index, kinv, schur, corner, coarse_inverse, loads):
    nsub = lax.axis_size("sub")
    ncrs = lax.axis_size("crs")
    fdof = face_index.shape[2]
    nrows, cases = loads.shape[1:]
    ncoarse = coarse_inverse.shape[1]
    nface = schur.shape[1]
    ncl = corner.shape[2]
    chips = nsub // 2
    nrp = -(-nrows // 256) * 256
    cbp = -(-coarse_inverse.shape[0] // 16) * 16
    ncp = -(-ncoarse // LANES) * LANES
    vm = pltpu.VMEM
    dma = pltpu.SemaphoreType.DMA
    scratch = [
        vm((nrows, nrows), F32), vm((nrows, cases), F32), vm((ncl, nrows), F32), vm((4, fdof, nface), F32),
        vm(coarse_inverse.shape, F32),
        vm((nrp, nrp), BF16), vm((nrp, nrp), BF16), vm((16, nrp), F32),
        vm((8, NX), jnp.int32), vm((NX, 8), jnp.int32),
        vm((NX, nrp), BF16), vm((nrp, NX), BF16), vm((NA, nrp), BF16), vm((NA, nrp), BF16),
        vm((nrp, cases), BF16), vm((nrp, cases), BF16),
        vm((NX, 3 * NX), BF16), vm((NW + NX, 3 * NX), BF16), vm((NX, 3 * LANES), BF16), vm((3 * NX, cases), BF16),
        vm((32, nrp), F32), vm((cbp, ncp), F32),
        vm((NX, NX), F32), vm((NX, NX), BF16),
        vm((NX, LANES), F32), vm((NX, LANES), F32), vm((NX, LANES), F32),
        vm((ncrs, LANES, LANES), F32), vm((LANES, chips * 24), BF16), vm((LANES, chips * 24), BF16),
        vm((2, NX, cases), F32), vm((2, 4, FACE, cases), F32),
        vm((NX, cases), F32), vm((NX, cases), F32), vm((NX, cases), F32),
        vm((3, NW, cases), F32), vm((3, 4 * ncrs, 24, LANES), F32), vm((3, chips, 24, LANES), F32),
        vm((3, LANES + 24, LANES), F32), vm((3, LANES + 24, LANES), F32), vm((LANES, LANES), F32), vm((LANES, LANES), F32),
        vm((2, 24, LANES), F32), vm((3, LANES, cases), F32), vm((3 * LANES, cases), BF16),
        vm((3, 8, LANES), F32), vm((3, 2 * ncrs, 8, LANES), F32), vm((3, chips, 8, LANES), F32),
        vm((8, cases), F32), vm((8, fdof, cases), F32),
        dma((8,)), dma((8,)), dma((2, 4)), dma((2, 4)), dma((4,)), dma((4,)), dma((ncrs,)), dma((ncrs,)),
    ] + [dma((3,)) for _ in range(12)]
    out = jax.ShapeDtypeStruct((1, fdof, 4, cases), F32)
    anyspace = pl.BlockSpec(memory_space=pl.ANY)
    inside = pl.BlockSpec(memory_space=pltpu.VMEM)
    dims = (nsub, ncrs, nrows, fdof, cases, ncoarse)
    mult, resid = pl.pallas_call(
        functools.partial(kernel, dims),
        out_shape=(out, out),
        in_specs=[inside] + [anyspace] * 5,
        out_specs=(anyspace, anyspace),
        scratch_shapes=scratch,
        compiler_params=pltpu.CompilerParams(
            collective_id=0, has_side_effects=True, vmem_limit_bytes=63 * 2**20),
    )(face_index, jnp.swapaxes(kinv, 0, 1), jnp.swapaxes(schur, 0, 1),
      jnp.swapaxes(corner, 1, 2), coarse_inverse, jnp.swapaxes(loads, 0, 1))
    return jnp.swapaxes(mult, 1, 2), jnp.swapaxes(resid, 1, 2)


def solution(mesh):
    subs = P(("sub", "crs"), None, None)
    out = P(("sub", "crs"), None, None, None)
    return jax.shard_map(
        body, mesh=mesh, in_specs=(subs, subs, subs, subs, P("crs", None), subs), out_specs=(out, out),
        check_vma=False)
```

```python
import functools

import jax
import jax.numpy as jnp
from jax import lax
from jax.experimental import pallas as pl
from jax.experimental.pallas import tpu as pltpu
from jax.sharding import PartitionSpec as P

F32 = jnp.float32
BF16 = jnp.bfloat16
MESH = pl.DeviceIdType.MESH

FACE = 160
SENT = 152
NX = 4 * FACE
NC = 48
NW = 96
NA = NX + NC
ORDER = (2, 3, 0, 1)
LANES = 128


def dot(left, right):
    return jnp.dot(left, right, preferred_element_type=F32)


def dot_nt(left, right):
    return lax.dot_general(left, right, (((1,), (1,)), ((), ())), preferred_element_type=F32)


def split(value):
    high = value.astype(BF16)
    return high, (value - high.astype(F32)).astype(BF16)


def hot(cond, value=1.0):
    return jnp.where(cond, value, 0.0).astype(BF16)


def rows_of(shape):
    return lax.broadcasted_iota(jnp.int32, shape, 0)


def cols_of(shape):
    return lax.broadcasted_iota(jnp.int32, shape, 1)


def div(value, by):
    return (value * (65536 // by + 1)) >> 16


def kernel(dims, faces, kinv, schur, corner, cinv, loads, mo, ro,
           kv, lv, cv, sv, civ, khi, klo, tail, idxr, idxc, bmat, bmt, a0hi, a0lo, lhi, llo, a3, m3, w3, x3,
           cpad, cip, sp, tmt, ws, wo, wr, dall, dphi, dplo,
           tb, rb, rv, dv, mv, zv, tk, wv, pbuf, p0, gb, sibs, sibr, hs, hk, qk, hb, h3,
           qs, rr, er, co, outs,
           dsem, osem, fsend, frecv, wsend, wrecv, csend, crecv,
           s1s, s1r, s2s, s2r, bs, br, s3s, s3r, r1s, r1r, r2s, r2r, qsend, qrecv):
    nsub, ncrs, nrows, fdof, cases, ncoarse = dims
    chips = nsub // 2
    nrp = khi.shape[1]
    cblock = ncoarse // ncrs
    cbp, ncp = cip.shape
    a = lax.axis_index("sub")
    b = lax.axis_index("crs")
    k = lax.div(a, 2)
    c = lax.rem(a, 2)
    sib = 2 * k + 1 - c
    up = lax.rem(a + 1, nsub)
    down = lax.rem(a + nsub - 1, nsub)
    left = lax.rem(b + ncrs - 1, ncrs)
    right = lax.rem(b + 1, ncrs)
    dests = ((a, left), (a, right), (down, b), (up, b))
    keeps = (None, None, a > 0, a < nsub - 1)
    drains = []

    def local(src, dst, n):
        return pltpu.make_async_copy(src, dst, dsem.at[n])

    def remote(src, dst, ssem, rsem, dev):
        return pltpu.make_async_remote_copy(
            src_ref=src, dst_ref=dst, send_sem=ssem, recv_sem=rsem, device_id=dev, device_id_type=MESH)

    def settle(ref, sem):
        pltpu.make_async_copy(ref, ref, sem).wait()

    in_copies = [local(corner.at[0], cv, 0), local(cinv, civ, 1), local(loads.at[:, 0], lv, 2),
                 local(kinv.at[:, 0], kv, 3)]
    in_copies += [local(schur.at[pl.ds(ORDER[pos] * fdof, fdof), 0], sv.at[pos], 4 + pos) for pos in range(4)]
    for copy in in_copies:
        copy.start()

    barrier = pltpu.get_barrier_semaphore()
    for j in range(1, ncrs):
        pl.semaphore_signal(barrier, inc=1, device_id=(a, lax.rem(b + j, ncrs)), device_id_type=MESH)
    for j in range(ncrs):
        pl.semaphore_signal(barrier, inc=1, device_id=(up, j), device_id_type=MESH)
        pl.semaphore_signal(barrier, inc=1, device_id=(down, j), device_id_type=MESH)
    for j in range(1, ncrs):
        to = lax.rem(b + j, ncrs)
        pl.semaphore_signal(barrier, inc=1, device_id=(lax.rem(a + 2, nsub), to), device_id_type=MESH)
        pl.semaphore_signal(barrier, inc=1, device_id=(lax.rem(a + nsub - 2, nsub), to), device_id_type=MESH)

    def greet(j, carry):
        pl.semaphore_signal(barrier, inc=1, device_id=(2 * lax.rem(k + j, chips) + c, b), device_id_type=MESH)
        return carry

    lax.fori_loop(1, chips, greet, 0)

    greeted = ncrs - 1 + 2 * ncrs + 2 * (ncrs - 1) + chips - 1

    idxr[...] = jnp.full(idxr.shape, -1, jnp.int32)
    for pos in range(4):
        face = ORDER[pos]
        idxr[0:1, pos * FACE:pos * FACE + fdof] = faces[0, face:face + 1, :]
    idxc[...] = jnp.transpose(idxr[...])
    for pos in range(4):
        sign = 1.0 if pos % 2 else -1.0
        band = slice(pos * FACE, (pos + 1) * FACE)
        bmat[band, :] = hot(idxc[band, 0:1] == cols_of((FACE, nrp)), sign)
    lane = cols_of((1, NX))
    signs = jnp.where(((lane >= FACE) & (lane < 2 * FACE)) | (lane >= 3 * FACE), 1.0, -1.0)

    def build_bmt(i, carry):
        at = pl.multiple_of(i * LANES, LANES)
        rows = rows_of((LANES, NX)) + at
        bmt[pl.ds(at, LANES), :] = jnp.where(idxr[0:1, :] == rows, signs, 0.0).astype(BF16)
        return carry

    lax.fori_loop(0, nrp // LANES, build_bmt, 0)

    for n in range(2):
        for pos in range(4):
            rb[n, pos, SENT:FACE, :] = jnp.zeros((FACE - SENT, cases), F32)
    hb[:, 96:LANES, :] = jnp.zeros((3, 32, cases), F32)
    cpad[...] = jnp.zeros(cpad.shape, F32)
    cip[...] = jnp.zeros(cip.shape, F32)
    sp[...] = jnp.zeros(sp.shape, F32)
    edge = nrp - LANES
    khi[:, edge:] = jnp.zeros((nrp, LANES), BF16)
    klo[:, edge:] = jnp.zeros((nrp, LANES), BF16)
    whole = nrows // 16 * 16
    for ref in (khi, klo, lhi, llo):
        ref[whole:, :] = jnp.zeros((nrp - whole, ref.shape[1]), BF16)
    tail[...] = jnp.zeros(tail.shape, F32)

    in_copies[0].wait()
    ncl = cv.shape[0]
    cpad[0:ncl, 0:nrows] = cv[...]
    chi, clo = split(cpad[...])
    l = cols_of((1, 32))
    da = div(l, 12)
    rem12 = l - 12 * da
    db = div(rem12, 6)
    where_l = jnp.where(l < 24, 24 * da + 6 * lax.rem(b + db, ncrs) + rem12 - 6 * db, -1000)
    sel = hot(where_l == rows_of((NC, 32)))
    a0hi[0:NC, :] = dot(sel, chi).astype(BF16)
    a0lo[0:NC, :] = dot(sel, clo).astype(BF16)
    in_copies[2].wait()
    step = 16 * 5

    def split_loads(i, carry):
        at = pl.multiple_of(i * step, step)
        high, low = split(lv[pl.ds(at, step), :])
        lhi[pl.ds(at, step), :] = high
        llo[pl.ds(at, step), :] = low
        return carry

    lax.fori_loop(0, whole // step, split_loads, 0)
    left_rows = nrows - whole
    tail[0:left_rows, 0:cases] = lv[whole:nrows, :]
    high, low = split(tail[:, 0:cases])
    lhi[whole:whole + 16, :] = high
    llo[whole:whole + 16, :] = low

    def apply_loads(lo, hi):
        high, low = a0hi[lo:hi, :], a0lo[lo:hi, :]
        return dot(high, lhi[...]) + dot(high, llo[...]) + dot(low, lhi[...])

    def coarse_begin(f, offs):
        for i, off in enumerate(offs):
            owner = lax.rem(a + off + nsub, nsub)
            for j in range(ncrs):
                to = lax.rem(b + j, ncrs)
                at = pl.ds(pl.multiple_of(to * LANES, LANES), LANES)
                band = pl.ds(24 * i, 24)
                if off == 0 and j == 0:
                    p0[f, i * ncrs + b] = pbuf[f, band, at]
                    continue
                remote(pbuf.at[f, band, at], p0.at[f, i * ncrs + b], s1s.at[f], s1r.at[f], (owner, to)).start()
        drains.append(lambda: settle(p0.at[f, pl.ds(0, ncrs * len(offs) - 1)], s1s.at[f]))

    def coarse_gather(f, offs):
        count = ncrs * len(offs)
        settle(p0.at[f, pl.ds(0, count - 1)], s1r.at[f])
        gb[f, k] = jnp.sum(p0[f, 0:count], axis=0)

        def send(j, carry):
            to = 2 * lax.rem(k + j, chips) + c
            remote(gb.at[f, k], gb.at[f, k], s2s.at[f], s2r.at[f], (to, b)).start()
            return carry

        lax.fori_loop(1, chips, send, 0)
        other = remote(gb.at[f, k], qs.at[f], qsend.at[f], qrecv.at[f], (sib, b))
        other.start()
        drains.append(lambda: settle(gb.at[f, pl.ds(0, chips - 1)], s2s.at[f]))
        drains.append(other.wait_send)
        return other

    def coarse_solve(f):
        settle(gb.at[f, pl.ds(0, chips - 1)], s2r.at[f])
        high, low = split(gb[f].reshape(chips * 24, LANES))
        sibs[f] = dot(dphi[...], high) + dot(dphi[...], low) + dot(dplo[...], high)
        copy = remote(sibs.at[f], sibr.at[f], bs.at[f], br.at[f], (sib, b))
        copy.start()
        return copy

    def coarse_spread(f, copy):
        copy.wait()
        at = pl.ds(pl.multiple_of(b * LANES, LANES), LANES)
        hs[...] = sibs[f] + sibr[f]
        hb[f, 0:NW, at] = hs[pl.ds(pl.multiple_of(24 * c, 8), NW), :]
        for j in range(1, ncrs):
            remote(hb.at[f, pl.ds(0, NW), at], hb.at[f, pl.ds(0, NW), at], s3s.at[f], s3r.at[f],
                   (a, lax.rem(b + j, ncrs))).start()
        drains.append(lambda: settle(hb.at[f, pl.ds(0, NW), pl.ds(0, (ncrs - 1) * LANES)], s3s.at[f]))

    def coarse_energy(f, qcopy, scale=None):
        at = pl.ds(pl.multiple_of(b * LANES, LANES), LANES)
        qcopy.wait_recv()
        total, mine, other = sibs[f], gb[f, k], qs[f]
        if scale is not None:
            part = scale[0:1, at]
            total = total + part * hk[...]
            mine = mine + part * qk[0]
            other = other + part * qk[1]
        hk[...] = total
        qk[0] = mine
        qk[1] = other
        mine = hk[pl.ds(pl.multiple_of(24 + 24 * c, 8), 24), :] * mine
        other = hk[pl.ds(pl.multiple_of(48 - 24 * c, 8), 24), :] * other
        return jnp.sum(mine + other, axis=0, keepdims=True)

    def coarse_end(f):
        settle(hb.at[f, pl.ds(0, NW), pl.ds(0, (ncrs - 1) * LANES)], s3r.at[f])
        high, low = split(hb[f])
        h3[0:LANES, :] = high
        h3[LANES:2 * LANES, :] = low
        h3[2 * LANES:, :] = high

    row8 = rows_of((8, LANES))

    def packed(value):
        return jnp.concatenate([value[:, i * LANES:(i + 1) * LANES] for i in range(ncrs)], axis=0)

    def unpacked(value):
        return jnp.concatenate([value[i:i + 1] for i in range(ncrs)], axis=1)

    def late_begin(n, first, second):
        er[n, k] = jnp.concatenate([first, second], axis=0)

        def send(j, carry):
            to = 2 * lax.rem(k + j, chips) + c
            remote(er.at[n, k], er.at[n, k], r2s.at[n], r2r.at[n], (to, b)).start()
            return carry

        lax.fori_loop(1, chips, send, 0)
        drains.append(lambda: settle(er.at[n, pl.ds(0, chips - 1)], r2s.at[n]))

    def late_spread(n):
        settle(er.at[n, pl.ds(0, chips - 1)], r2r.at[n])
        mine = rr.at[n, c * ncrs + b]
        rr[n, c * ncrs + b] = jnp.sum(er[n], axis=0)
        for cc in range(2):
            for j in range(ncrs):
                if cc == 0 and j == 0:
                    continue
                dev = (a if cc == 0 else sib, lax.rem(b + j, ncrs))
                remote(mine, mine, r1s.at[n], r1r.at[n], dev).start()
        drains.append(lambda: settle(rr.at[n, pl.ds(0, 2 * ncrs - 1)], r1s.at[n]))

    def late_end(n):
        settle(rr.at[n, pl.ds(0, 2 * ncrs - 1)], r1r.at[n])
        total = jnp.sum(rr[n], axis=0)
        return total[0:ncrs], total[ncrs:]

    def faces_start(n, which, lanes=slice(0, cases), h=0):
        copies = []
        at = pl.ds(lanes.start, lanes.stop - lanes.start)
        for pos in which:
            copy = remote(tb.at[n % 2, pl.ds(pos * FACE, SENT), at], rb.at[n % 2, pos ^ 1, pl.ds(0, SENT), at],
                          fsend.at[2 * (n % 2) + h, pos], frecv.at[2 * (n % 2) + h, pos ^ 1], dests[pos])
            copy.start()
            copies.append(copy)
        return copies

    def faces_wait(copies):
        for copy in copies:
            copy.wait()

    def jumped(n, pos, extra=None, lanes=slice(0, cases)):
        band = slice(pos * FACE, (pos + 1) * FACE)
        value = tb[n % 2, band, lanes] + rb[n % 2, pos, :, lanes]
        if extra is not None:
            value = value + extra
        if keeps[pos] is not None:
            value = jnp.where(keeps[pos], value, 0.0)
        return value

    def put_x(pos, value, lanes=slice(0, cases)):
        high, low = split(value)
        lo = pos * FACE
        x3[lo:lo + FACE, lanes] = high
        x3[NX + lo:NX + lo + FACE, lanes] = low
        x3[2 * NX + lo:2 * NX + lo + FACE, lanes] = high

    both = dot(jnp.concatenate([a0hi[0:NC, :], a0lo[0:NC, :]], axis=0), lhi[...])
    pbuf[0, 0:NC] = both[0:NC] + both[NC:] + dot(a0hi[0:NC, :], llo[...])
    pl.semaphore_wait(barrier, greeted)
    coarse_begin(0, (0, 1))

    in_copies[1].wait()
    cip[0:cblock, 0:ncoarse] = civ[...]
    high, low = split(cip[...])
    i = cols_of((1, cbp))
    r = cblock * b + i
    plane = div(r, 24)
    base = lax.div(lax.div(cblock * b, 24), 2)
    target = 24 * ((plane >> 1) - base) + r - 24 * plane
    target = jnp.where((((plane + 1) & 1) == c) & (i < cblock), target, -1)
    pct = hot(target == rows_of((LANES, cbp)))
    x1h = dot(pct, high).astype(BF16)
    x1l = dot(pct, low).astype(BF16)
    i = rows_of((LANES, 1))
    r = 48 * k - 48 + i
    r = jnp.where((i < 120) & (r < ncoarse), r, -1)
    sel = hot(r == cols_of((LANES, ncp)))
    dall[b] = dot_nt(sel, x1h) + dot_nt(sel, x1l)
    for j in range(1, ncrs):
        remote(dall.at[b], dall.at[b], csend.at[j], crecv.at[j], (a, lax.rem(b + j, ncrs))).start()

    bch = dot_nt(bmat[...], chi).astype(BF16)
    bcl = dot_nt(bmat[...], clo).astype(BF16)
    l = rows_of((32, 1))
    da = div(l, 12)
    rem12 = l - 12 * da
    db = div(rem12, 6)
    where_l = 24 * (1 + da) + 6 * lax.rem(b + db, ncrs) + rem12 - 6 * db
    where_l = jnp.where(l < 24, where_l, -1000)
    lanes = cols_of((32, LANES))
    emaps = [hot(where_l + off == lanes) for off in (0, 24, -24)]
    wo[...] = dot(bch, emaps[0]) + dot(bcl, emaps[0])
    ws[0:2 * FACE, :] = wo[0:2 * FACE, :]
    for pos in (2, 3):
        band = slice(pos * FACE, (pos + 1) * FACE)
        ws[band, :] = dot(bch[band], emaps[pos - 1]) + dot(bcl[band], emaps[pos - 1])
    wcopies = [remote(ws.at[pl.ds(pos * FACE, FACE)], wr.at[pl.ds((pos ^ 1) * FACE, FACE)],
                      wsend.at[pos], wrecv.at[pos ^ 1], dests[pos]) for pos in range(4)]
    for copy in wcopies:
        copy.start()

    in_copies[3].wait()

    def split_k(i, carry):
        at = pl.multiple_of(i * step, step)
        high, low = split(kv[pl.ds(at, step), :])
        khi[pl.ds(at, step), 0:nrows] = high
        klo[pl.ds(at, step), 0:nrows] = low
        return carry

    lax.fori_loop(0, whole // step, split_k, 0)
    tail[0:left_rows, 0:nrows] = kv[whole:nrows, :]
    high, low = split(tail[...])
    khi[whole:whole + 16, :] = high
    klo[whole:whole + 16, :] = low

    def face_rows(lo, hi):
        def tile(i, carry):
            at = pl.ds(pl.multiple_of(i * 256, 256), 256)
            a0hi[NC + lo:NC + hi, at] = dot(bmat[lo:hi, :], khi[:, at]).astype(BF16)
            a0lo[NC + lo:NC + hi, at] = dot(bmat[lo:hi, :], klo[:, at]).astype(BF16)
            return carry

        lax.fori_loop(0, nrp // 256, tile, 0)

    half = 2 * FACE
    face_rows(0, half)
    tb[0, 0:half, :] = apply_loads(NC, NC + half)
    copies = faces_start(0, (0, 1))
    face_rows(half, NX)
    qcopy = coarse_gather(0, (0, 1))
    tb[0, half:NX, :] = apply_loads(NC + half, NC + NX)
    copies += faces_start(0, (2, 3))

    for j in range(1, ncrs):
        copy = remote(dall.at[b], dall.at[b], csend.at[j], crecv.at[j], (a, lax.rem(b + j, ncrs)))
        copy.wait()
    total_hi = total_lo = None
    for blk_b in range(ncrs):
        j = rows_of((LANES, 1))
        pair = div(j, 24)
        rem = j - 24 * pair
        pair = pair + (cblock * blk_b // 24) // 2
        r = 24 * (2 * pair + 1 - c) + rem
        target = jnp.where((j < 120) & (r >= cblock * blk_b) & (r < cblock * (blk_b + 1)),
                           24 * (pair + 1 - c) + rem, -1)
        perm = hot(target == cols_of((LANES, chips * 24)))
        high, low = split(dall[blk_b])
        ph, plo = dot(high, perm), dot(low, perm)
        total_hi = ph if total_hi is None else total_hi + ph
        total_lo = plo if total_lo is None else total_lo + plo
    dphi[...] = total_hi.astype(BF16)
    dplo[...] = total_lo.astype(BF16)

    def between(i, carry):
        at = pl.ds(pl.multiple_of(i * half, half), half)
        src = pl.ds(pl.multiple_of(NC + i * half, 16), half)
        high = dot(a0hi[src, :], bmt[...]).astype(BF16)
        a3[at, 0:NX] = high
        a3[at, NX:2 * NX] = high
        a3[at, 2 * NX:] = dot(a0lo[src, :], bmt[...]).astype(BF16)
        return carry

    coarse_copy = coarse_solve(0)

    nface = sv.shape[2]
    for pos in range(4):
        in_copies[4 + pos].wait()
        sp[pos * FACE:pos * FACE + fdof, 0:nface] = sv[pos] * (0.5 if pos % 2 else -0.5)
    high, low = split(sp[...])
    khi[0:NX, 0:NX] = high
    klo[0:NX, 0:NX] = low
    pos_l = jnp.where(lane >= FACE, 1, 0) + jnp.where(lane >= 2 * FACE, 1, 0) + jnp.where(lane >= 3 * FACE, 1, 0)
    j = lane - FACE * pos_l
    target = jnp.where(j < fdof, j + fdof * ((pos_l + 2) & 3), -1)
    kept = jnp.where(pos_l == 2, jnp.where(a > 0, 0.5, 0.0), jnp.where(pos_l == 3, jnp.where(a < nsub - 1, 0.5, 0.0), 0.5))
    tmt[...] = jnp.where(target == rows_of((NX, NX)), signs * kept, 0.0).astype(BF16)

    def precond_rows(i, carry):
        at = pl.ds(pl.multiple_of(i * FACE, FACE), FACE)
        high = dot(khi[at, 0:NX], tmt[...]).astype(BF16)
        low = klo[at, 0:NX]
        to = pl.ds(pl.multiple_of(NW + i * FACE, 16), FACE)
        m3[to, 0:NX] = high
        m3[to, NX:2 * NX] = high
        m3[to, 2 * NX:] = dot(low, tmt[...]).astype(BF16)
        return carry

    coarse_spread(0, coarse_copy)
    qcopy.wait_recv()
    lax.fori_loop(0, 4, precond_rows, 0)

    for copy in wcopies:
        copy.wait()
    for pos in range(4):
        band = slice(pos * FACE, (pos + 1) * FACE)
        value = wo[band, :] + wr[band, :]
        if keeps[pos] is not None:
            value = jnp.where(keeps[pos], value, 0.0)
        wo[band, :] = value
    high, low = split(wo[...])
    w3[:, 0:LANES] = high
    w3[:, LANES:2 * LANES] = high
    w3[:, 2 * LANES:] = low
    high, low = split(jnp.transpose(wo[...]))
    mhi, mlo = m3[NW:, 0:NX], m3[NW:, 2 * NX:]
    both = dot(jnp.concatenate([high[0:NW], low[0:NW]], axis=0), mhi)
    high, low = split(both[0:NW] + both[NW:] + dot(high[0:NW], mlo))
    m3[0:NW, 0:NX] = high
    m3[0:NW, NX:2 * NX] = high
    m3[0:NW, 2 * NX:] = low

    def operator_end(n, f, copies, use):
        coarse_end(f)
        faces_wait(copies)
        for pos in range(4):
            use(pos, jumped(n, pos, dot(w3[pos * FACE:(pos + 1) * FACE, :], h3[...])))

    def first_use(pos, value):
        rv[pos * FACE:(pos + 1) * FACE, :] = value
        put_x(pos, value)

    operator_end(0, 0, copies, first_use)

    around = (-1, 0, 1, 2)

    halves = (slice(0, cases // 2), slice(cases // 2, cases))
    every = (0, 1, 2, 3)

    def precond(n, f):
        block = dot(m3[0:NW + half, :], x3[...])
        pbuf[f] = block[0:NW]
        coarse_begin(f, around)
        tb[n % 2, 0:half, :] = block[NW:]
        tb[n % 2, half:, :] = dot(m3[NW + half:, :], x3[...])
        return [faces_start(n, every, lanes, h) for h, lanes in enumerate(halves)]

    def operator(n, copies, keep_z):
        out = []
        for h, lanes in enumerate(halves):
            faces_wait(copies[h])
            for pos in range(4):
                value = jumped(n - 1, pos, None, lanes)
                keep_z[pos * FACE:(pos + 1) * FACE, lanes] = value
                put_x(pos, value, lanes)
            tb[n % 2, 0:half, lanes] = dot(a3[0:half, :], x3[:, lanes])
            tb[n % 2, half:, lanes] = dot(a3[half:, :], x3[:, lanes])
            out += faces_start(n, every, lanes, h)
        return out

    def operator_sums(f, qcopy, rz_part, energy, scale):
        coarse_copy = coarse_solve(f)
        energy = energy + jnp.where(rows_of((ncrs, LANES)) == b, coarse_energy(f, qcopy, scale), 0.0)
        late_begin(f, rz_part, energy)
        coarse_spread(f, coarse_copy)
        late_spread(f)

    def total_rz(n):
        return packed(jnp.sum(rv[...] * tb[n % 2], axis=0, keepdims=True))

    copies = precond(1, 1)
    rz_part = total_rz(1)
    lax.fori_loop(0, 2, between, 0)
    qcopy = coarse_gather(1, around)

    copies = operator(2, copies, dv)
    tk[...] = tb[0]
    operator_sums(1, qcopy, rz_part, packed(jnp.sum(dv[...] * tk[...], axis=0, keepdims=True)), None)

    def keep_image(pos, value):
        wv[pos * FACE:(pos + 1) * FACE, :] = value

    operator_end(2, 1, copies, keep_image)
    rz_now, energy = late_end(1)
    alpha = unpacked(rz_now / energy)
    for pos in range(4):
        band = slice(pos * FACE, (pos + 1) * FACE)
        value = rv[band, :] - alpha * wv[band, :]
        rv[band, :] = value
        put_x(pos, value)

    copies = precond(3, 2)
    late_begin(0, total_rz(3), jnp.zeros((ncrs, LANES), F32))
    for pos in range(4):
        band = slice(pos * FACE, (pos + 1) * FACE)
        mv[band, :] = alpha * dv[band, :]
    qcopy = coarse_gather(2, around)
    late_spread(0)

    copies = operator(4, copies, zv)
    rz_next, _ = late_end(0)
    beta = unpacked(rz_next / rz_now)
    co[0:1, :] = beta
    parts = 0.0
    for pos in range(4):
        band = slice(pos * FACE, (pos + 1) * FACE)
        value = zv[band, :] + beta * dv[band, :]
        dv[band, :] = value
        parts = parts + jnp.sum(value * (tb[0, band, :] + beta * tk[band, :]), axis=0, keepdims=True)
    operator_sums(2, qcopy, jnp.zeros((ncrs, LANES), F32), packed(parts), co)

    def whole_image(pos, value):
        band = slice(pos * FACE, (pos + 1) * FACE)
        wv[band, :] = value + beta * wv[band, :]

    operator_end(4, 2, copies, whole_image)
    _, energy = late_end(2)
    alpha = unpacked(rz_next / energy)
    out_copies = []
    for pos in range(4):
        band = slice(pos * FACE, (pos + 1) * FACE)
        outs[pos] = (mv[band, :] + alpha * dv[band, :])[0:fdof]
        outs[4 + pos] = (rv[band, :] - alpha * wv[band, :])[0:fdof]
        for side, ref in enumerate((mo, ro)):
            copy = pltpu.make_async_copy(outs.at[4 * side + pos], ref.at[0, :, ORDER[pos]], osem.at[4 * side + pos])
            copy.start()
            out_copies.append(copy)
    for copy in out_copies:
        copy.wait()

    for drain in drains:
        drain()


def body(face_index, kinv, schur, corner, coarse_inverse, loads):
    nsub = lax.axis_size("sub")
    ncrs = lax.axis_size("crs")
    fdof = face_index.shape[2]
    nrows, cases = loads.shape[1:]
    ncoarse = coarse_inverse.shape[1]
    nface = schur.shape[1]
    ncl = corner.shape[2]
    chips = nsub // 2
    nrp = -(-nrows // 256) * 256
    cbp = -(-coarse_inverse.shape[0] // 16) * 16
    ncp = -(-ncoarse // LANES) * LANES
    vm = pltpu.VMEM
    dma = pltpu.SemaphoreType.DMA
    scratch = [
        vm((nrows, nrows), F32), vm((nrows, cases), F32), vm((ncl, nrows), F32), vm((4, fdof, nface), F32),
        vm(coarse_inverse.shape, F32),
        vm((nrp, nrp), BF16), vm((nrp, nrp), BF16), vm((16, nrp), F32),
        vm((8, NX), jnp.int32), vm((NX, 8), jnp.int32),
        vm((NX, nrp), BF16), vm((nrp, NX), BF16), vm((NA, nrp), BF16), vm((NA, nrp), BF16),
        vm((nrp, cases), BF16), vm((nrp, cases), BF16),
        vm((NX, 3 * NX), BF16), vm((NW + NX, 3 * NX), BF16), vm((NX, 3 * LANES), BF16), vm((3 * NX, cases), BF16),
        vm((32, nrp), F32), vm((cbp, ncp), F32),
        vm((NX, NX), F32), vm((NX, NX), BF16),
        vm((NX, LANES), F32), vm((NX, LANES), F32), vm((NX, LANES), F32),
        vm((ncrs, LANES, LANES), F32), vm((LANES, chips * 24), BF16), vm((LANES, chips * 24), BF16),
        vm((2, NX, cases), F32), vm((2, 4, FACE, cases), F32),
        vm((NX, cases), F32), vm((NX, cases), F32), vm((NX, cases), F32),
        vm((NX, cases), F32), vm((NX, cases), F32), vm((NX, cases), F32),
        vm((3, NW, cases), F32), vm((3, 4 * ncrs, 24, LANES), F32), vm((3, chips, 24, LANES), F32),
        vm((3, LANES, LANES), F32), vm((3, LANES, LANES), F32), vm((LANES, LANES), F32), vm((LANES, LANES), F32),
        vm((2, 24, LANES), F32), vm((3, LANES, cases), F32), vm((3 * LANES, cases), BF16),
        vm((3, 24, LANES), F32), vm((3, 2 * ncrs, 8, LANES), F32), vm((3, chips, 8, LANES), F32),
        vm((8, cases), F32), vm((8, fdof, cases), F32),
        dma((8,)), dma((8,)), dma((4, 4)), dma((4, 4)), dma((4,)), dma((4,)), dma((ncrs,)), dma((ncrs,)),
    ] + [dma((3,)) for _ in range(14)]
    out = jax.ShapeDtypeStruct((1, fdof, 4, cases), F32)
    anyspace = pl.BlockSpec(memory_space=pl.ANY)
    inside = pl.BlockSpec(memory_space=pltpu.VMEM)
    dims = (nsub, ncrs, nrows, fdof, cases, ncoarse)
    mult, resid = pl.pallas_call(
        functools.partial(kernel, dims),
        out_shape=(out, out),
        in_specs=[inside] + [anyspace] * 5,
        out_specs=(anyspace, anyspace),
        scratch_shapes=scratch,
        compiler_params=pltpu.CompilerParams(
            collective_id=0, has_side_effects=True, vmem_limit_bytes=63 * 2**20),
    )(face_index, jnp.swapaxes(kinv, 0, 1), jnp.swapaxes(schur, 0, 1),
      jnp.swapaxes(corner, 1, 2), coarse_inverse, jnp.swapaxes(loads, 0, 1))
    return jnp.swapaxes(mult, 1, 2), jnp.swapaxes(resid, 1, 2)


def solution(mesh):
    subs = P(("sub", "crs"), None, None)
    out = P(("sub", "crs"), None, None, None)
    return jax.shard_map(
        body, mesh=mesh, in_specs=(subs, subs, subs, subs, P("crs", None), subs), out_specs=(out, out),
        check_vma=False)
```

```python
import functools

import jax
import jax.numpy as jnp
from jax import lax
from jax.experimental import pallas as pl
from jax.experimental.pallas import tpu as pltpu
from jax.sharding import PartitionSpec as P

F32 = jnp.float32
BF16 = jnp.bfloat16
MESH = pl.DeviceIdType.MESH

FACE = 160
SENT = 152
NX = 4 * FACE
NC = 48
NW = 96
NA = NX + NC
ORDER = (2, 3, 0, 1)
LANES = 128


def dot(left, right):
    return jnp.dot(left, right, preferred_element_type=F32)


def dot_nt(left, right):
    return lax.dot_general(left, right, (((1,), (1,)), ((), ())), preferred_element_type=F32)


def split(value):
    high = value.astype(BF16)
    return high, (value - high.astype(F32)).astype(BF16)


def hot(cond, value=1.0):
    return jnp.where(cond, value, 0.0).astype(BF16)


def rows_of(shape):
    return lax.broadcasted_iota(jnp.int32, shape, 0)


def cols_of(shape):
    return lax.broadcasted_iota(jnp.int32, shape, 1)


def div(value, by):
    return (value * (65536 // by + 1)) >> 16


def kernel(dims, faces, kinv, schur, corner, cinv, loads, mo, do, ro, wo_out, alpha_out,
           kv, lv, cv, sv, civ, khi, klo, tail, idxr, idxc, bmat, bmt, a0hi, a0lo, lhi, llo, a3, m3, w3, x3,
           cpad, cip, sp, tmt, ws, wo, wr, dall, dphi, dplo,
           tb, rb, rv, dv, mv, zv, tk, wv, pbuf, p0, gb, sibs, sibr, hs, hk, qk, hb, h3,
           qs, rr, er, co,
           dsem, osem, fsend, frecv, wsend, wrecv, csend, crecv,
           s1s, s1r, s2s, s2r, bs, br, s3s, s3r, r1s, r1r, r2s, r2r, qsend, qrecv):
    nsub, ncrs, nrows, fdof, cases, ncoarse = dims
    chips = nsub // 2
    nrp = khi.shape[1]
    cblock = ncoarse // ncrs
    cbp, ncp = cip.shape
    a = lax.axis_index("sub")
    b = lax.axis_index("crs")
    k = lax.div(a, 2)
    c = lax.rem(a, 2)
    sib = 2 * k + 1 - c
    up = lax.rem(a + 1, nsub)
    down = lax.rem(a + nsub - 1, nsub)
    left = lax.rem(b + ncrs - 1, ncrs)
    right = lax.rem(b + 1, ncrs)
    dests = ((a, left), (a, right), (down, b), (up, b))
    keeps = (None, None, a > 0, a < nsub - 1)
    drains = []

    def local(src, dst, n):
        return pltpu.make_async_copy(src, dst, dsem.at[n])

    def remote(src, dst, ssem, rsem, dev):
        return pltpu.make_async_remote_copy(
            src_ref=src, dst_ref=dst, send_sem=ssem, recv_sem=rsem, device_id=dev, device_id_type=MESH)

    def settle(ref, sem):
        pltpu.make_async_copy(ref, ref, sem).wait()

    in_copies = [local(corner.at[0], cv, 0), local(cinv, civ, 1), local(loads.at[:, 0], lv, 2),
                 local(kinv.at[:, 0], kv, 3)]
    in_copies += [local(schur.at[pl.ds(ORDER[pos] * fdof, fdof), 0], sv.at[pos], 4 + pos) for pos in range(4)]
    for copy in in_copies:
        copy.start()

    barrier = pltpu.get_barrier_semaphore()
    for j in range(1, ncrs):
        pl.semaphore_signal(barrier, inc=1, device_id=(a, lax.rem(b + j, ncrs)), device_id_type=MESH)
    for j in range(ncrs):
        pl.semaphore_signal(barrier, inc=1, device_id=(up, j), device_id_type=MESH)
        pl.semaphore_signal(barrier, inc=1, device_id=(down, j), device_id_type=MESH)
    for j in range(1, ncrs):
        to = lax.rem(b + j, ncrs)
        pl.semaphore_signal(barrier, inc=1, device_id=(lax.rem(a + 2, nsub), to), device_id_type=MESH)
        pl.semaphore_signal(barrier, inc=1, device_id=(lax.rem(a + nsub - 2, nsub), to), device_id_type=MESH)

    def greet(j, carry):
        pl.semaphore_signal(barrier, inc=1, device_id=(2 * lax.rem(k + j, chips) + c, b), device_id_type=MESH)
        return carry

    lax.fori_loop(1, chips, greet, 0)

    greeted = ncrs - 1 + 2 * ncrs + 2 * (ncrs - 1) + chips - 1

    idxr[...] = jnp.full(idxr.shape, -1, jnp.int32)
    for pos in range(4):
        face = ORDER[pos]
        idxr[0:1, pos * FACE:pos * FACE + fdof] = faces[0, face:face + 1, :]
    idxc[...] = jnp.transpose(idxr[...])
    for pos in range(4):
        sign = 1.0 if pos % 2 else -1.0
        band = slice(pos * FACE, (pos + 1) * FACE)
        bmat[band, :] = hot(idxc[band, 0:1] == cols_of((FACE, nrp)), sign)
    lane = cols_of((1, NX))
    signs = jnp.where(((lane >= FACE) & (lane < 2 * FACE)) | (lane >= 3 * FACE), 1.0, -1.0)

    def build_bmt(i, carry):
        at = pl.multiple_of(i * LANES, LANES)
        rows = rows_of((LANES, NX)) + at
        bmt[pl.ds(at, LANES), :] = jnp.where(idxr[0:1, :] == rows, signs, 0.0).astype(BF16)
        return carry

    lax.fori_loop(0, nrp // LANES, build_bmt, 0)

    for n in range(2):
        for pos in range(4):
            rb[n, pos, SENT:FACE, :] = jnp.zeros((FACE - SENT, cases), F32)
    hb[:, 96:LANES, :] = jnp.zeros((3, 32, cases), F32)
    cpad[...] = jnp.zeros(cpad.shape, F32)
    cip[...] = jnp.zeros(cip.shape, F32)
    sp[...] = jnp.zeros(sp.shape, F32)
    edge = nrp - LANES
    khi[:, edge:] = jnp.zeros((nrp, LANES), BF16)
    klo[:, edge:] = jnp.zeros((nrp, LANES), BF16)
    whole = nrows // 16 * 16
    for ref in (khi, klo, lhi, llo):
        ref[whole:, :] = jnp.zeros((nrp - whole, ref.shape[1]), BF16)
    tail[...] = jnp.zeros(tail.shape, F32)

    in_copies[0].wait()
    ncl = cv.shape[0]
    cpad[0:ncl, 0:nrows] = cv[...]
    chi, clo = split(cpad[...])
    l = cols_of((1, 32))
    da = div(l, 12)
    rem12 = l - 12 * da
    db = div(rem12, 6)
    where_l = jnp.where(l < 24, 24 * da + 6 * lax.rem(b + db, ncrs) + rem12 - 6 * db, -1000)
    sel = hot(where_l == rows_of((NC, 32)))
    a0hi[0:NC, :] = dot(sel, chi).astype(BF16)
    a0lo[0:NC, :] = dot(sel, clo).astype(BF16)
    in_copies[2].wait()
    step = 16 * 5

    def split_loads(i, carry):
        at = pl.multiple_of(i * step, step)
        high, low = split(lv[pl.ds(at, step), :])
        lhi[pl.ds(at, step), :] = high
        llo[pl.ds(at, step), :] = low
        return carry

    lax.fori_loop(0, whole // step, split_loads, 0)
    left_rows = nrows - whole
    tail[0:left_rows, 0:cases] = lv[whole:nrows, :]
    high, low = split(tail[:, 0:cases])
    lhi[whole:whole + 16, :] = high
    llo[whole:whole + 16, :] = low

    def apply_loads(lo, hi):
        high, low = a0hi[lo:hi, :], a0lo[lo:hi, :]
        return dot(high, lhi[...]) + dot(high, llo[...]) + dot(low, lhi[...])

    def coarse_begin(f, offs):
        for i, off in enumerate(offs):
            owner = lax.rem(a + off + nsub, nsub)
            for j in range(ncrs):
                to = lax.rem(b + j, ncrs)
                at = pl.ds(pl.multiple_of(to * LANES, LANES), LANES)
                band = pl.ds(24 * i, 24)
                if off == 0 and j == 0:
                    p0[f, i * ncrs + b] = pbuf[f, band, at]
                    continue
                remote(pbuf.at[f, band, at], p0.at[f, i * ncrs + b], s1s.at[f], s1r.at[f], (owner, to)).start()
        drains.append(lambda: settle(p0.at[f, pl.ds(0, ncrs * len(offs) - 1)], s1s.at[f]))

    def coarse_gather(f, offs):
        count = ncrs * len(offs)
        settle(p0.at[f, pl.ds(0, count - 1)], s1r.at[f])
        gb[f, k] = jnp.sum(p0[f, 0:count], axis=0)

        def send(j, carry):
            to = 2 * lax.rem(k + j, chips) + c
            remote(gb.at[f, k], gb.at[f, k], s2s.at[f], s2r.at[f], (to, b)).start()
            return carry

        lax.fori_loop(1, chips, send, 0)
        other = remote(gb.at[f, k], qs.at[f], qsend.at[f], qrecv.at[f], (sib, b))
        other.start()
        drains.append(lambda: settle(gb.at[f, pl.ds(0, chips - 1)], s2s.at[f]))
        drains.append(other.wait_send)
        return other

    def coarse_solve(f):
        settle(gb.at[f, pl.ds(0, chips - 1)], s2r.at[f])
        high, low = split(gb[f].reshape(chips * 24, LANES))
        sibs[f] = dot(dphi[...], high) + dot(dphi[...], low) + dot(dplo[...], high)
        copy = remote(sibs.at[f], sibr.at[f], bs.at[f], br.at[f], (sib, b))
        copy.start()
        return copy

    def coarse_spread(f, copy):
        copy.wait()
        at = pl.ds(pl.multiple_of(b * LANES, LANES), LANES)
        hs[...] = sibs[f] + sibr[f]
        hb[f, 0:NW, at] = hs[pl.ds(pl.multiple_of(24 * c, 8), NW), :]
        for j in range(1, ncrs):
            remote(hb.at[f, pl.ds(0, NW), at], hb.at[f, pl.ds(0, NW), at], s3s.at[f], s3r.at[f],
                   (a, lax.rem(b + j, ncrs))).start()
        drains.append(lambda: settle(hb.at[f, pl.ds(0, NW), pl.ds(0, (ncrs - 1) * LANES)], s3s.at[f]))

    def coarse_energy(f, qcopy, scale=None):
        at = pl.ds(pl.multiple_of(b * LANES, LANES), LANES)
        qcopy.wait_recv()
        total, mine, other = sibs[f], gb[f, k], qs[f]
        if scale is not None:
            part = scale[0:1, at]
            total = total + part * hk[...]
            mine = mine + part * qk[0]
            other = other + part * qk[1]
        hk[...] = total
        qk[0] = mine
        qk[1] = other
        mine = hk[pl.ds(pl.multiple_of(24 + 24 * c, 8), 24), :] * mine
        other = hk[pl.ds(pl.multiple_of(48 - 24 * c, 8), 24), :] * other
        return jnp.sum(mine + other, axis=0, keepdims=True)

    def coarse_end(f):
        settle(hb.at[f, pl.ds(0, NW), pl.ds(0, (ncrs - 1) * LANES)], s3r.at[f])
        high, low = split(hb[f])
        h3[0:LANES, :] = high
        h3[LANES:2 * LANES, :] = low
        h3[2 * LANES:, :] = high

    row8 = rows_of((8, LANES))

    def packed(value):
        return jnp.concatenate([value[:, i * LANES:(i + 1) * LANES] for i in range(ncrs)], axis=0)

    def unpacked(value):
        return jnp.concatenate([value[i:i + 1] for i in range(ncrs)], axis=1)

    def late_begin(n, first, second):
        er[n, k] = jnp.concatenate([first, second], axis=0)

        def send(j, carry):
            to = 2 * lax.rem(k + j, chips) + c
            remote(er.at[n, k], er.at[n, k], r2s.at[n], r2r.at[n], (to, b)).start()
            return carry

        lax.fori_loop(1, chips, send, 0)
        drains.append(lambda: settle(er.at[n, pl.ds(0, chips - 1)], r2s.at[n]))

    def late_spread(n):
        settle(er.at[n, pl.ds(0, chips - 1)], r2r.at[n])
        mine = rr.at[n, c * ncrs + b]
        rr[n, c * ncrs + b] = jnp.sum(er[n], axis=0)
        for cc in range(2):
            for j in range(ncrs):
                if cc == 0 and j == 0:
                    continue
                dev = (a if cc == 0 else sib, lax.rem(b + j, ncrs))
                remote(mine, mine, r1s.at[n], r1r.at[n], dev).start()
        drains.append(lambda: settle(rr.at[n, pl.ds(0, 2 * ncrs - 1)], r1s.at[n]))

    def late_end(n):
        settle(rr.at[n, pl.ds(0, 2 * ncrs - 1)], r1r.at[n])
        total = jnp.sum(rr[n], axis=0)
        return total[0:ncrs], total[ncrs:]

    def faces_start(n, which, lanes=slice(0, cases), h=0):
        copies = []
        at = pl.ds(lanes.start, lanes.stop - lanes.start)
        for pos in which:
            copy = remote(tb.at[n % 2, pl.ds(pos * FACE, SENT), at], rb.at[n % 2, pos ^ 1, pl.ds(0, SENT), at],
                          fsend.at[2 * (n % 2) + h, pos], frecv.at[2 * (n % 2) + h, pos ^ 1], dests[pos])
            copy.start()
            copies.append(copy)
        return copies

    def faces_wait(copies):
        for copy in copies:
            copy.wait()

    def jumped(n, pos, extra=None, lanes=slice(0, cases)):
        band = slice(pos * FACE, (pos + 1) * FACE)
        value = tb[n % 2, band, lanes] + rb[n % 2, pos, :, lanes]
        if extra is not None:
            value = value + extra
        if keeps[pos] is not None:
            value = jnp.where(keeps[pos], value, 0.0)
        return value

    def put_x(pos, value, lanes=slice(0, cases)):
        high, low = split(value)
        lo = pos * FACE
        x3[lo:lo + FACE, lanes] = high
        x3[NX + lo:NX + lo + FACE, lanes] = low
        x3[2 * NX + lo:2 * NX + lo + FACE, lanes] = high

    both = dot(jnp.concatenate([a0hi[0:NC, :], a0lo[0:NC, :]], axis=0), lhi[...])
    pbuf[0, 0:NC] = both[0:NC] + both[NC:] + dot(a0hi[0:NC, :], llo[...])
    pl.semaphore_wait(barrier, greeted)
    coarse_begin(0, (0, 1))

    in_copies[1].wait()
    cip[0:cblock, 0:ncoarse] = civ[...]
    high, low = split(cip[...])
    i = cols_of((1, cbp))
    r = cblock * b + i
    plane = div(r, 24)
    base = lax.div(lax.div(cblock * b, 24), 2)
    target = 24 * ((plane >> 1) - base) + r - 24 * plane
    target = jnp.where((((plane + 1) & 1) == c) & (i < cblock), target, -1)
    pct = hot(target == rows_of((LANES, cbp)))
    x1h = dot(pct, high).astype(BF16)
    x1l = dot(pct, low).astype(BF16)
    i = rows_of((LANES, 1))
    r = 48 * k - 48 + i
    r = jnp.where((i < 120) & (r < ncoarse), r, -1)
    sel = hot(r == cols_of((LANES, ncp)))
    dall[b] = dot_nt(sel, x1h) + dot_nt(sel, x1l)
    for j in range(1, ncrs):
        remote(dall.at[b], dall.at[b], csend.at[j], crecv.at[j], (a, lax.rem(b + j, ncrs))).start()

    bch = dot_nt(bmat[...], chi).astype(BF16)
    bcl = dot_nt(bmat[...], clo).astype(BF16)
    l = rows_of((32, 1))
    da = div(l, 12)
    rem12 = l - 12 * da
    db = div(rem12, 6)
    where_l = 24 * (1 + da) + 6 * lax.rem(b + db, ncrs) + rem12 - 6 * db
    where_l = jnp.where(l < 24, where_l, -1000)
    lanes = cols_of((32, LANES))
    emaps = [hot(where_l + off == lanes) for off in (0, 24, -24)]
    wo[...] = dot(bch, emaps[0]) + dot(bcl, emaps[0])
    ws[0:2 * FACE, :] = wo[0:2 * FACE, :]
    for pos in (2, 3):
        band = slice(pos * FACE, (pos + 1) * FACE)
        ws[band, :] = dot(bch[band], emaps[pos - 1]) + dot(bcl[band], emaps[pos - 1])
    wcopies = [remote(ws.at[pl.ds(pos * FACE, FACE)], wr.at[pl.ds((pos ^ 1) * FACE, FACE)],
                      wsend.at[pos], wrecv.at[pos ^ 1], dests[pos]) for pos in range(4)]
    for copy in wcopies:
        copy.start()

    in_copies[3].wait()

    def split_k(i, carry):
        at = pl.multiple_of(i * step, step)
        high, low = split(kv[pl.ds(at, step), :])
        khi[pl.ds(at, step), 0:nrows] = high
        klo[pl.ds(at, step), 0:nrows] = low
        return carry

    lax.fori_loop(0, whole // step, split_k, 0)
    tail[0:left_rows, 0:nrows] = kv[whole:nrows, :]
    high, low = split(tail[...])
    khi[whole:whole + 16, :] = high
    klo[whole:whole + 16, :] = low

    def face_rows(lo, hi):
        def tile(i, carry):
            at = pl.ds(pl.multiple_of(i * 256, 256), 256)
            a0hi[NC + lo:NC + hi, at] = dot(bmat[lo:hi, :], khi[:, at]).astype(BF16)
            a0lo[NC + lo:NC + hi, at] = dot(bmat[lo:hi, :], klo[:, at]).astype(BF16)
            return carry

        lax.fori_loop(0, nrp // 256, tile, 0)

    half = 2 * FACE
    face_rows(0, half)
    tb[0, 0:half, :] = apply_loads(NC, NC + half)
    copies = faces_start(0, (0, 1))
    qcopy = coarse_gather(0, (0, 1))
    face_rows(half, NX)
    tb[0, half:NX, :] = apply_loads(NC + half, NC + NX)
    copies += faces_start(0, (2, 3))

    for j in range(1, ncrs):
        copy = remote(dall.at[b], dall.at[b], csend.at[j], crecv.at[j], (a, lax.rem(b + j, ncrs)))
        copy.wait()
    total_hi = total_lo = None
    for blk_b in range(ncrs):
        j = rows_of((LANES, 1))
        pair = div(j, 24)
        rem = j - 24 * pair
        pair = pair + (cblock * blk_b // 24) // 2
        r = 24 * (2 * pair + 1 - c) + rem
        target = jnp.where((j < 120) & (r >= cblock * blk_b) & (r < cblock * (blk_b + 1)),
                           24 * (pair + 1 - c) + rem, -1)
        perm = hot(target == cols_of((LANES, chips * 24)))
        high, low = split(dall[blk_b])
        ph, plo = dot(high, perm), dot(low, perm)
        total_hi = ph if total_hi is None else total_hi + ph
        total_lo = plo if total_lo is None else total_lo + plo
    dphi[...] = total_hi.astype(BF16)
    dplo[...] = total_lo.astype(BF16)

    def between(i, carry):
        at = pl.ds(pl.multiple_of(i * half, half), half)
        src = pl.ds(pl.multiple_of(NC + i * half, 16), half)
        high = dot(a0hi[src, :], bmt[...]).astype(BF16)
        a3[at, 0:NX] = high
        a3[at, NX:2 * NX] = high
        a3[at, 2 * NX:] = dot(a0lo[src, :], bmt[...]).astype(BF16)
        return carry

    coarse_copy = coarse_solve(0)

    nface = sv.shape[2]
    for pos in range(4):
        in_copies[4 + pos].wait()
        sp[pos * FACE:pos * FACE + fdof, 0:nface] = sv[pos] * (0.5 if pos % 2 else -0.5)
    high, low = split(sp[...])
    khi[0:NX, 0:NX] = high
    klo[0:NX, 0:NX] = low
    pos_l = jnp.where(lane >= FACE, 1, 0) + jnp.where(lane >= 2 * FACE, 1, 0) + jnp.where(lane >= 3 * FACE, 1, 0)
    j = lane - FACE * pos_l
    target = jnp.where(j < fdof, j + fdof * ((pos_l + 2) & 3), -1)
    kept = jnp.where(pos_l == 2, jnp.where(a > 0, 0.5, 0.0), jnp.where(pos_l == 3, jnp.where(a < nsub - 1, 0.5, 0.0), 0.5))
    tmt[...] = jnp.where(target == rows_of((NX, NX)), signs * kept, 0.0).astype(BF16)

    def precond_rows(i, carry):
        at = pl.ds(pl.multiple_of(i * FACE, FACE), FACE)
        high = dot(khi[at, 0:NX], tmt[...]).astype(BF16)
        low = klo[at, 0:NX]
        to = pl.ds(pl.multiple_of(NW + i * FACE, 16), FACE)
        m3[to, 0:NX] = high
        m3[to, NX:2 * NX] = high
        m3[to, 2 * NX:] = dot(low, tmt[...]).astype(BF16)
        return carry

    coarse_spread(0, coarse_copy)
    qcopy.wait_recv()
    lax.fori_loop(0, 4, precond_rows, 0)

    for copy in wcopies:
        copy.wait()
    for pos in range(4):
        band = slice(pos * FACE, (pos + 1) * FACE)
        value = wo[band, :] + wr[band, :]
        if keeps[pos] is not None:
            value = jnp.where(keeps[pos], value, 0.0)
        wo[band, :] = value
    high, low = split(wo[...])
    w3[:, 0:LANES] = high
    w3[:, LANES:2 * LANES] = high
    w3[:, 2 * LANES:] = low
    high, low = split(jnp.transpose(wo[...]))
    mhi, mlo = m3[NW:, 0:NX], m3[NW:, 2 * NX:]
    both = dot(jnp.concatenate([high[0:NW], low[0:NW]], axis=0), mhi)
    high, low = split(both[0:NW] + both[NW:] + dot(high[0:NW], mlo))
    m3[0:NW, 0:NX] = high
    m3[0:NW, NX:2 * NX] = high
    m3[0:NW, 2 * NX:] = low

    def operator_end(n, f, copies, use):
        coarse_end(f)
        faces_wait(copies)
        for pos in range(4):
            use(pos, jumped(n, pos, dot(w3[pos * FACE:(pos + 1) * FACE, :], h3[...])))

    def first_use(pos, value):
        rv[pos * FACE:(pos + 1) * FACE, :] = value
        put_x(pos, value)

    operator_end(0, 0, copies, first_use)

    around = (-1, 0, 1, 2)

    halves = (slice(0, cases // 2), slice(cases // 2, cases))
    every = (0, 1, 2, 3)

    def precond(n, f):
        block = dot(m3[0:NW + half, :], x3[...])
        pbuf[f] = block[0:NW]
        coarse_begin(f, around)
        tb[n % 2, 0:half, :] = block[NW:]
        tb[n % 2, half:, :] = dot(m3[NW + half:, :], x3[...])
        return [faces_start(n, every, lanes, h) for h, lanes in enumerate(halves)]

    def operator(n, copies, keep_z):
        out = []
        for h, lanes in enumerate(halves):
            faces_wait(copies[h])
            for pos in range(4):
                value = jumped(n - 1, pos, None, lanes)
                keep_z[pos * FACE:(pos + 1) * FACE, lanes] = value
                put_x(pos, value, lanes)
            tb[n % 2, 0:half, lanes] = dot(a3[0:half, :], x3[:, lanes])
            tb[n % 2, half:, lanes] = dot(a3[half:, :], x3[:, lanes])
            out += faces_start(n, every, lanes, h)
        return out

    def operator_sums(f, qcopy, rz_part, energy, scale):
        coarse_copy = coarse_solve(f)
        energy = energy + jnp.where(rows_of((ncrs, LANES)) == b, coarse_energy(f, qcopy, scale), 0.0)
        late_begin(f, rz_part, energy)
        coarse_spread(f, coarse_copy)
        late_spread(f)

    def total_rz(n):
        return packed(jnp.sum(rv[...] * tb[n % 2], axis=0, keepdims=True))

    def leave(src, dst, n):
        for pos in range(4):
            copy = pltpu.make_async_copy(src.at[pl.ds(pos * FACE, SENT)], dst.at[0, :, ORDER[pos]], osem.at[4 * n + pos])
            copy.start()
            drains.append(copy.wait)

    copies = precond(1, 1)
    rz_part = total_rz(1)
    lax.fori_loop(0, 2, between, 0)
    qcopy = coarse_gather(1, around)

    copies = operator(2, copies, dv)
    tk[...] = tb[0]
    operator_sums(1, qcopy, rz_part, packed(jnp.sum(dv[...] * tk[...], axis=0, keepdims=True)), None)

    def keep_image(pos, value):
        wv[pos * FACE:(pos + 1) * FACE, :] = value

    operator_end(2, 1, copies, keep_image)
    rz_now, energy = late_end(1)
    alpha = unpacked(rz_now / energy)
    for pos in range(4):
        band = slice(pos * FACE, (pos + 1) * FACE)
        value = rv[band, :] - alpha * wv[band, :]
        rv[band, :] = value
        put_x(pos, value)

    copies = precond(3, 2)
    late_begin(0, total_rz(3), jnp.zeros((ncrs, LANES), F32))
    for pos in range(4):
        band = slice(pos * FACE, (pos + 1) * FACE)
        mv[band, :] = alpha * dv[band, :]
    leave(rv, ro, 0)
    leave(mv, mo, 1)
    qcopy = coarse_gather(2, around)
    late_spread(0)

    copies = operator(4, copies, zv)
    rz_next, _ = late_end(0)
    beta = unpacked(rz_next / rz_now)
    co[0:1, :] = beta
    parts = 0.0
    for pos in range(4):
        band = slice(pos * FACE, (pos + 1) * FACE)
        value = zv[band, :] + beta * dv[band, :]
        dv[band, :] = value
        parts = parts + jnp.sum(value * (tb[0, band, :] + beta * tk[band, :]), axis=0, keepdims=True)
    leave(dv, do, 2)
    operator_sums(2, qcopy, jnp.zeros((ncrs, LANES), F32), packed(parts), co)

    def whole_image(pos, value):
        band = slice(pos * FACE, (pos + 1) * FACE)
        wv[band, :] = value + beta * wv[band, :]

    operator_end(4, 2, copies, whole_image)
    leave(wv, wo_out, 3)
    _, energy = late_end(2)
    alpha_out[...] = unpacked(rz_next / energy)

    for drain in drains:
        drain()


def body(face_index, kinv, schur, corner, coarse_inverse, loads):
    nsub = lax.axis_size("sub")
    ncrs = lax.axis_size("crs")
    fdof = face_index.shape[2]
    nrows, cases = loads.shape[1:]
    ncoarse = coarse_inverse.shape[1]
    nface = schur.shape[1]
    ncl = corner.shape[2]
    chips = nsub // 2
    nrp = -(-nrows // 256) * 256
    cbp = -(-coarse_inverse.shape[0] // 16) * 16
    ncp = -(-ncoarse // LANES) * LANES
    vm = pltpu.VMEM
    dma = pltpu.SemaphoreType.DMA
    scratch = [
        vm((nrows, nrows), F32), vm((nrows, cases), F32), vm((ncl, nrows), F32), vm((4, fdof, nface), F32),
        vm(coarse_inverse.shape, F32),
        vm((nrp, nrp), BF16), vm((nrp, nrp), BF16), vm((16, nrp), F32),
        vm((8, NX), jnp.int32), vm((NX, 8), jnp.int32),
        vm((NX, nrp), BF16), vm((nrp, NX), BF16), vm((NA, nrp), BF16), vm((NA, nrp), BF16),
        vm((nrp, cases), BF16), vm((nrp, cases), BF16),
        vm((NX, 3 * NX), BF16), vm((NW + NX, 3 * NX), BF16), vm((NX, 3 * LANES), BF16), vm((3 * NX, cases), BF16),
        vm((32, nrp), F32), vm((cbp, ncp), F32),
        vm((NX, NX), F32), vm((NX, NX), BF16),
        vm((NX, LANES), F32), vm((NX, LANES), F32), vm((NX, LANES), F32),
        vm((ncrs, LANES, LANES), F32), vm((LANES, chips * 24), BF16), vm((LANES, chips * 24), BF16),
        vm((2, NX, cases), F32), vm((2, 4, FACE, cases), F32),
        vm((NX, cases), F32), vm((NX, cases), F32), vm((NX, cases), F32),
        vm((NX, cases), F32), vm((NX, cases), F32), vm((NX, cases), F32),
        vm((3, NW, cases), F32), vm((3, 4 * ncrs, 24, LANES), F32), vm((3, chips, 24, LANES), F32),
        vm((3, LANES, LANES), F32), vm((3, LANES, LANES), F32), vm((LANES, LANES), F32), vm((LANES, LANES), F32),
        vm((2, 24, LANES), F32), vm((3, LANES, cases), F32), vm((3 * LANES, cases), BF16),
        vm((3, 24, LANES), F32), vm((3, 2 * ncrs, 8, LANES), F32), vm((3, chips, 8, LANES), F32),
        vm((8, cases), F32),
        dma((8,)), dma((16,)), dma((4, 4)), dma((4, 4)), dma((4,)), dma((4,)), dma((ncrs,)), dma((ncrs,)),
    ] + [dma((3,)) for _ in range(14)]
    out = jax.ShapeDtypeStruct((1, SENT, 4, cases), F32)
    anyspace = pl.BlockSpec(memory_space=pl.ANY)
    inside = pl.BlockSpec(memory_space=pltpu.VMEM)
    dims = (nsub, ncrs, nrows, fdof, cases, ncoarse)
    first, last, resid, image, alpha = pl.pallas_call(
        functools.partial(kernel, dims),
        out_shape=(out, out, out, out, jax.ShapeDtypeStruct((1, cases), F32)),
        in_specs=[inside] + [anyspace] * 5,
        out_specs=(anyspace, anyspace, anyspace, anyspace, inside),
        scratch_shapes=scratch,
        compiler_params=pltpu.CompilerParams(
            collective_id=0, has_side_effects=True, vmem_limit_bytes=63 * 2**20),
    )(face_index, jnp.swapaxes(kinv, 0, 1), jnp.swapaxes(schur, 0, 1),
      jnp.swapaxes(corner, 1, 2), coarse_inverse, jnp.swapaxes(loads, 0, 1))
    alpha = alpha[:, None, None, :]
    first, last, resid, image = (value[:, 0:fdof] for value in (first, last, resid, image))
    return jnp.swapaxes(first + alpha * last, 1, 2), jnp.swapaxes(resid - alpha * image, 1, 2)


def solution(mesh):
    subs = P(("sub", "crs"), None, None)
    out = P(("sub", "crs"), None, None, None)
    return jax.shard_map(
        body, mesh=mesh, in_specs=(subs, subs, subs, subs, P("crs", None), subs), out_specs=(out, out),
        check_vma=False)
```

```python
import functools

import jax
import jax.numpy as jnp
from jax import lax
from jax.experimental import pallas as pl
from jax.experimental.pallas import tpu as pltpu
from jax.sharding import PartitionSpec as P

F32 = jnp.float32
BF16 = jnp.bfloat16
MESH = pl.DeviceIdType.MESH

FACE = 160
SENT = 152
NX = 4 * FACE
NC = 48
NW = 96
NA = NX + NC
ORDER = (2, 3, 0, 1)
LANES = 128


def dot(left, right):
    return jnp.dot(left, right, preferred_element_type=F32)


def dot_nt(left, right):
    return lax.dot_general(left, right, (((1,), (1,)), ((), ())), preferred_element_type=F32)


def split(value):
    high = value.astype(BF16)
    return high, (value - high.astype(F32)).astype(BF16)


def hot(cond, value=1.0):
    return jnp.where(cond, value, 0.0).astype(BF16)


def rows_of(shape):
    return lax.broadcasted_iota(jnp.int32, shape, 0)


def cols_of(shape):
    return lax.broadcasted_iota(jnp.int32, shape, 1)


def div(value, by):
    return (value * (65536 // by + 1)) >> 16


def kernel(dims, faces, kinv, schur, corner, cinv, loads, mo, do, ro, wo_out, alpha_out,
           kv, lv, cv, sv, civ, khi, klo, tail, idxr, idxc, bmat, bmt, a0hi, a0lo, lhi, llo, a3, m3, w3, x3,
           cpad, cip, sp, tmt, ws, wo, wr, dall, dphi, dplo,
           tb, rb, rv, dv, mv, zv, tk, wv, pbuf, p0, gb, sibs, sibr, hs, hk, qk, hb, h3,
           qs, rr, er, co,
           dsem, osem, fsend, frecv, wsend, wrecv, csend, crecv,
           s1s, s1r, s2s, s2r, bs, br, s3s, s3r, r1s, r1r, r2s, r2r, qsend, qrecv):
    nsub, ncrs, nrows, fdof, cases, ncoarse = dims
    chips = nsub // 2
    nrp = khi.shape[1]
    cblock = ncoarse // ncrs
    cbp, ncp = cip.shape
    a = lax.axis_index("sub")
    b = lax.axis_index("crs")
    k = a >> 1
    c = a & 1
    sib = 2 * k + 1 - c
    up = (a + 1) & (nsub - 1)
    down = (a + nsub - 1) & (nsub - 1)
    left = (b + ncrs - 1) & (ncrs - 1)
    right = (b + 1) & (ncrs - 1)
    dests = ((a, left), (a, right), (down, b), (up, b))
    keeps = (None, None, a > 0, a < nsub - 1)
    drains = []

    def local(src, dst, n):
        return pltpu.make_async_copy(src, dst, dsem.at[n])

    def remote(src, dst, ssem, rsem, dev):
        return pltpu.make_async_remote_copy(
            src_ref=src, dst_ref=dst, send_sem=ssem, recv_sem=rsem, device_id=dev, device_id_type=MESH)

    def settle(ref, sem):
        pltpu.make_async_copy(ref, ref, sem).wait()

    in_copies = [local(corner.at[0], cv, 0), local(cinv, civ, 1), local(loads.at[:, 0], lv, 2),
                 local(kinv.at[:, 0], kv, 3)]
    in_copies += [local(schur.at[pl.ds(ORDER[pos] * fdof, fdof), 0], sv.at[pos], 4 + pos) for pos in range(4)]
    for copy in in_copies:
        copy.start()

    barrier = pltpu.get_barrier_semaphore()
    for j in range(1, ncrs):
        pl.semaphore_signal(barrier, inc=1, device_id=(a, (b + j) & (ncrs - 1)), device_id_type=MESH)
    for j in range(ncrs):
        pl.semaphore_signal(barrier, inc=1, device_id=(up, j), device_id_type=MESH)
        pl.semaphore_signal(barrier, inc=1, device_id=(down, j), device_id_type=MESH)
    for j in range(1, ncrs):
        to = (b + j) & (ncrs - 1)
        pl.semaphore_signal(barrier, inc=1, device_id=((a + 2) & (nsub - 1), to), device_id_type=MESH)
        pl.semaphore_signal(barrier, inc=1, device_id=((a + nsub - 2) & (nsub - 1), to), device_id_type=MESH)

    def greet(j, carry):
        pl.semaphore_signal(barrier, inc=1, device_id=(2 * ((k + j) & (chips - 1)) + c, b), device_id_type=MESH)
        return carry

    lax.fori_loop(1, chips, greet, 0)

    greeted = ncrs - 1 + 2 * ncrs + 2 * (ncrs - 1) + chips - 1

    idxr[...] = jnp.full(idxr.shape, -1, jnp.int32)
    for pos in range(4):
        face = ORDER[pos]
        idxr[0:1, pos * FACE:pos * FACE + fdof] = faces[0, face:face + 1, :]
    idxc[...] = jnp.transpose(idxr[...])
    for pos in range(4):
        sign = 1.0 if pos % 2 else -1.0
        band = slice(pos * FACE, (pos + 1) * FACE)
        bmat[band, :] = hot(idxc[band, 0:1] == cols_of((FACE, nrp)), sign)
    lane = cols_of((1, NX))
    signs = jnp.where(((lane >= FACE) & (lane < 2 * FACE)) | (lane >= 3 * FACE), 1.0, -1.0)

    def build_bmt(i, carry):
        at = pl.multiple_of(i * LANES, LANES)
        rows = rows_of((LANES, NX)) + at
        bmt[pl.ds(at, LANES), :] = jnp.where(idxr[0:1, :] == rows, signs, 0.0).astype(BF16)
        return carry

    lax.fori_loop(0, nrp // LANES, build_bmt, 0)

    for n in range(2):
        for pos in range(4):
            rb[n, pos, SENT:FACE, :] = jnp.zeros((FACE - SENT, cases), F32)
    hb[:, 96:LANES, :] = jnp.zeros((3, 32, cases), F32)
    cpad[...] = jnp.zeros(cpad.shape, F32)
    cip[...] = jnp.zeros(cip.shape, F32)
    sp[...] = jnp.zeros(sp.shape, F32)
    edge = nrp - LANES
    khi[:, edge:] = jnp.zeros((nrp, LANES), BF16)
    klo[:, edge:] = jnp.zeros((nrp, LANES), BF16)
    whole = nrows // 16 * 16
    for ref in (khi, klo, lhi, llo):
        ref[whole:, :] = jnp.zeros((nrp - whole, ref.shape[1]), BF16)
    tail[...] = jnp.zeros(tail.shape, F32)

    in_copies[0].wait()
    ncl = cv.shape[0]
    cpad[0:ncl, 0:nrows] = cv[...]
    chi, clo = split(cpad[...])
    l = cols_of((1, 32))
    da = div(l, 12)
    rem12 = l - 12 * da
    db = div(rem12, 6)
    where_l = jnp.where(l < 24, 24 * da + 6 * ((b + db) & (ncrs - 1)) + rem12 - 6 * db, -1000)
    sel = hot(where_l == rows_of((NC, 32)))
    a0hi[0:NC, :] = dot(sel, chi).astype(BF16)
    a0lo[0:NC, :] = dot(sel, clo).astype(BF16)
    in_copies[2].wait()
    step = 16 * 5

    def split_loads(i, carry):
        at = pl.multiple_of(i * step, step)
        high, low = split(lv[pl.ds(at, step), :])
        lhi[pl.ds(at, step), :] = high
        llo[pl.ds(at, step), :] = low
        return carry

    lax.fori_loop(0, whole // step, split_loads, 0)
    left_rows = nrows - whole
    tail[0:left_rows, 0:cases] = lv[whole:nrows, :]
    high, low = split(tail[:, 0:cases])
    lhi[whole:whole + 16, :] = high
    llo[whole:whole + 16, :] = low

    def apply_loads(lo, hi):
        high, low = a0hi[lo:hi, :], a0lo[lo:hi, :]
        return dot(high, lhi[...]) + dot(high, llo[...]) + dot(low, lhi[...])

    def coarse_begin(f, offs):
        for i, off in enumerate(offs):
            owner = (a + off + nsub) & (nsub - 1)
            for j in range(ncrs):
                to = (b + j) & (ncrs - 1)
                at = pl.ds(pl.multiple_of(to * LANES, LANES), LANES)
                band = pl.ds(24 * i, 24)
                if off == 0 and j == 0:
                    p0[f, i * ncrs + b] = pbuf[f, band, at]
                    continue
                remote(pbuf.at[f, band, at], p0.at[f, i * ncrs + b], s1s.at[f], s1r.at[f], (owner, to)).start()
        drains.append(lambda: settle(p0.at[f, pl.ds(0, ncrs * len(offs) - 1)], s1s.at[f]))

    def coarse_gather(f, offs):
        count = ncrs * len(offs)
        settle(p0.at[f, pl.ds(0, count - 1)], s1r.at[f])
        gb[f, k] = jnp.sum(p0[f, 0:count], axis=0)

        def send(j, carry):
            to = 2 * ((k + j) & (chips - 1)) + c
            remote(gb.at[f, k], gb.at[f, k], s2s.at[f], s2r.at[f], (to, b)).start()
            return carry

        lax.fori_loop(1, chips, send, 0)
        other = remote(gb.at[f, k], qs.at[f], qsend.at[f], qrecv.at[f], (sib, b))
        other.start()
        drains.append(lambda: settle(gb.at[f, pl.ds(0, chips - 1)], s2s.at[f]))
        drains.append(other.wait_send)
        return other

    def coarse_solve(f):
        settle(gb.at[f, pl.ds(0, chips - 1)], s2r.at[f])
        high, low = split(gb[f].reshape(chips * 24, LANES))
        sibs[f] = dot(dphi[...], high) + dot(dphi[...], low) + dot(dplo[...], high)
        copy = remote(sibs.at[f], sibr.at[f], bs.at[f], br.at[f], (sib, b))
        copy.start()
        return copy

    def coarse_spread(f, copy):
        copy.wait()
        at = pl.ds(pl.multiple_of(b * LANES, LANES), LANES)
        hs[...] = sibs[f] + sibr[f]
        hb[f, 0:NW, at] = hs[pl.ds(pl.multiple_of(24 * c, 8), NW), :]
        for j in range(1, ncrs):
            remote(hb.at[f, pl.ds(0, NW), at], hb.at[f, pl.ds(0, NW), at], s3s.at[f], s3r.at[f],
                   (a, (b + j) & (ncrs - 1))).start()
        drains.append(lambda: settle(hb.at[f, pl.ds(0, NW), pl.ds(0, (ncrs - 1) * LANES)], s3s.at[f]))

    def coarse_energy(f, qcopy, scale=None):
        at = pl.ds(pl.multiple_of(b * LANES, LANES), LANES)
        qcopy.wait_recv()
        total, mine, other = sibs[f], gb[f, k], qs[f]
        if scale is not None:
            part = scale[0:1, at]
            total = total + part * hk[...]
            mine = mine + part * qk[0]
            other = other + part * qk[1]
        hk[...] = total
        qk[0] = mine
        qk[1] = other
        mine = hk[pl.ds(pl.multiple_of(24 + 24 * c, 8), 24), :] * mine
        other = hk[pl.ds(pl.multiple_of(48 - 24 * c, 8), 24), :] * other
        return jnp.sum(mine + other, axis=0, keepdims=True)

    def coarse_end(f):
        settle(hb.at[f, pl.ds(0, NW), pl.ds(0, (ncrs - 1) * LANES)], s3r.at[f])
        high, low = split(hb[f])
        h3[0:LANES, :] = high
        h3[LANES:2 * LANES, :] = low
        h3[2 * LANES:, :] = high

    row8 = rows_of((8, LANES))

    def packed(value):
        return jnp.concatenate([value[:, i * LANES:(i + 1) * LANES] for i in range(ncrs)], axis=0)

    def unpacked(value):
        return jnp.concatenate([value[i:i + 1] for i in range(ncrs)], axis=1)

    def late_begin(n, first, second):
        er[n, k] = jnp.concatenate([first, second], axis=0)

        def send(j, carry):
            to = 2 * ((k + j) & (chips - 1)) + c
            remote(er.at[n, k], er.at[n, k], r2s.at[n], r2r.at[n], (to, b)).start()
            return carry

        lax.fori_loop(1, chips, send, 0)
        drains.append(lambda: settle(er.at[n, pl.ds(0, chips - 1)], r2s.at[n]))

    def late_spread(n):
        settle(er.at[n, pl.ds(0, chips - 1)], r2r.at[n])
        mine = rr.at[n, c * ncrs + b]
        rr[n, c * ncrs + b] = jnp.sum(er[n], axis=0)
        for cc in range(2):
            for j in range(ncrs):
                if cc == 0 and j == 0:
                    continue
                dev = (a if cc == 0 else sib, (b + j) & (ncrs - 1))
                remote(mine, mine, r1s.at[n], r1r.at[n], dev).start()
        drains.append(lambda: settle(rr.at[n, pl.ds(0, 2 * ncrs - 1)], r1s.at[n]))

    def late_end(n):
        settle(rr.at[n, pl.ds(0, 2 * ncrs - 1)], r1r.at[n])
        total = jnp.sum(rr[n], axis=0)
        return total[0:ncrs], total[ncrs:]

    def faces_start(n, which, lanes=slice(0, cases), h=0):
        copies = []
        at = pl.ds(lanes.start, lanes.stop - lanes.start)
        for pos in which:
            copy = remote(tb.at[n % 2, pl.ds(pos * FACE, SENT), at], rb.at[n % 2, pos ^ 1, pl.ds(0, SENT), at],
                          fsend.at[2 * (n % 2) + h, pos], frecv.at[2 * (n % 2) + h, pos ^ 1], dests[pos])
            copy.start()
            copies.append(copy)
        return copies

    def faces_wait(copies):
        for copy in copies:
            copy.wait()

    def jumped(n, pos, extra=None, lanes=slice(0, cases)):
        band = slice(pos * FACE, (pos + 1) * FACE)
        value = tb[n % 2, band, lanes] + rb[n % 2, pos, :, lanes]
        if extra is not None:
            value = value + extra
        if keeps[pos] is not None:
            value = jnp.where(keeps[pos], value, 0.0)
        return value

    def put_x(pos, value, lanes=slice(0, cases)):
        high, low = split(value)
        lo = pos * FACE
        x3[lo:lo + FACE, lanes] = high
        x3[NX + lo:NX + lo + FACE, lanes] = low
        x3[2 * NX + lo:2 * NX + lo + FACE, lanes] = high

    both = dot(jnp.concatenate([a0hi[0:NC, :], a0lo[0:NC, :]], axis=0), lhi[...])
    pbuf[0, 0:NC] = both[0:NC] + both[NC:] + dot(a0hi[0:NC, :], llo[...])
    pl.semaphore_wait(barrier, greeted)
    coarse_begin(0, (0, 1))

    in_copies[1].wait()
    cip[0:cblock, 0:ncoarse] = civ[...]
    high, low = split(cip[...])
    i = cols_of((1, cbp))
    r = cblock * b + i
    plane = div(r, 24)
    base = lax.div(lax.div(cblock * b, 24), 2)
    target = 24 * ((plane >> 1) - base) + r - 24 * plane
    target = jnp.where((((plane + 1) & 1) == c) & (i < cblock), target, -1)
    pct = hot(target == rows_of((LANES, cbp)))
    x1h = dot(pct, high).astype(BF16)
    x1l = dot(pct, low).astype(BF16)
    i = rows_of((LANES, 1))
    r = 48 * k - 48 + i
    r = jnp.where((i < 120) & (r < ncoarse), r, -1)
    sel = hot(r == cols_of((LANES, ncp)))
    dall[b] = dot_nt(sel, x1h) + dot_nt(sel, x1l)
    for j in range(1, ncrs):
        remote(dall.at[b], dall.at[b], csend.at[j], crecv.at[j], (a, (b + j) & (ncrs - 1))).start()

    bch = dot_nt(bmat[...], chi).astype(BF16)
    bcl = dot_nt(bmat[...], clo).astype(BF16)
    l = rows_of((32, 1))
    da = div(l, 12)
    rem12 = l - 12 * da
    db = div(rem12, 6)
    where_l = 24 * (1 + da) + 6 * ((b + db) & (ncrs - 1)) + rem12 - 6 * db
    where_l = jnp.where(l < 24, where_l, -1000)
    lanes = cols_of((32, LANES))
    emaps = [hot(where_l + off == lanes) for off in (0, 24, -24)]
    wo[...] = dot(bch, emaps[0]) + dot(bcl, emaps[0])
    ws[0:2 * FACE, :] = wo[0:2 * FACE, :]
    for pos in (2, 3):
        band = slice(pos * FACE, (pos + 1) * FACE)
        ws[band, :] = dot(bch[band], emaps[pos - 1]) + dot(bcl[band], emaps[pos - 1])
    wcopies = [remote(ws.at[pl.ds(pos * FACE, FACE)], wr.at[pl.ds((pos ^ 1) * FACE, FACE)],
                      wsend.at[pos], wrecv.at[pos ^ 1], dests[pos]) for pos in range(4)]
    for copy in wcopies:
        copy.start()

    in_copies[3].wait()

    tail[0:left_rows, 0:nrows] = kv[whole:nrows, :]

    def face_rows(lo, hi):
        def tile(i, carry):
            at = pl.ds(pl.multiple_of(i * 256, 256), 256)
            a0hi[NC + lo:NC + hi, at] = dot(bmat[lo:hi, :], khi[:, at]).astype(BF16)
            a0lo[NC + lo:NC + hi, at] = dot(bmat[lo:hi, :], klo[:, at]).astype(BF16)
            return carry

        lax.fori_loop(0, nrp // 256, tile, 0)

    half = 2 * FACE
    for i in range(nrp // 256):
        at = slice(i * 256, (i + 1) * 256)
        filled = slice(i * 256, min((i + 1) * 256, nrows))
        high, low = split(kv[0:whole, filled])
        khi[0:whole, filled] = high
        klo[0:whole, filled] = low
        high, low = split(tail[:, at])
        khi[whole:whole + 16, at] = high
        klo[whole:whole + 16, at] = low
        a0hi[NC:NC + half, at] = dot(bmat[0:half, :], khi[:, at]).astype(BF16)
        a0lo[NC:NC + half, at] = dot(bmat[0:half, :], klo[:, at]).astype(BF16)
    tb[0, 0:half, :] = apply_loads(NC, NC + half)
    copies = faces_start(0, (0, 1))
    qcopy = coarse_gather(0, (0, 1))
    face_rows(half, NX)
    tb[0, half:NX, :] = apply_loads(NC + half, NC + NX)
    copies += faces_start(0, (2, 3))

    for j in range(1, ncrs):
        copy = remote(dall.at[b], dall.at[b], csend.at[j], crecv.at[j], (a, (b + j) & (ncrs - 1)))
        copy.wait()
    total_hi = total_lo = None
    for blk_b in range(ncrs):
        j = rows_of((LANES, 1))
        pair = div(j, 24)
        rem = j - 24 * pair
        pair = pair + (cblock * blk_b // 24) // 2
        r = 24 * (2 * pair + 1 - c) + rem
        target = jnp.where((j < 120) & (r >= cblock * blk_b) & (r < cblock * (blk_b + 1)),
                           24 * (pair + 1 - c) + rem, -1)
        perm = hot(target == cols_of((LANES, chips * 24)))
        high, low = split(dall[blk_b])
        ph, plo = dot(high, perm), dot(low, perm)
        total_hi = ph if total_hi is None else total_hi + ph
        total_lo = plo if total_lo is None else total_lo + plo
    dphi[...] = total_hi.astype(BF16)
    dplo[...] = total_lo.astype(BF16)

    def between(i, carry):
        at = pl.ds(pl.multiple_of(i * half, half), half)
        src = pl.ds(pl.multiple_of(NC + i * half, 16), half)
        high = dot(a0hi[src, :], bmt[...]).astype(BF16)
        a3[at, 0:NX] = high
        a3[at, NX:2 * NX] = high
        a3[at, 2 * NX:] = dot(a0lo[src, :], bmt[...]).astype(BF16)
        return carry

    coarse_copy = coarse_solve(0)

    nface = sv.shape[2]
    for pos in range(4):
        in_copies[4 + pos].wait()
        sp[pos * FACE:pos * FACE + fdof, 0:nface] = sv[pos] * (0.5 if pos % 2 else -0.5)
    high, low = split(sp[...])
    khi[0:NX, 0:NX] = high
    klo[0:NX, 0:NX] = low
    pos_l = jnp.where(lane >= FACE, 1, 0) + jnp.where(lane >= 2 * FACE, 1, 0) + jnp.where(lane >= 3 * FACE, 1, 0)
    j = lane - FACE * pos_l
    target = jnp.where(j < fdof, j + fdof * ((pos_l + 2) & 3), -1)
    kept = jnp.where(pos_l == 2, jnp.where(a > 0, 0.5, 0.0), jnp.where(pos_l == 3, jnp.where(a < nsub - 1, 0.5, 0.0), 0.5))
    tmt[...] = jnp.where(target == rows_of((NX, NX)), signs * kept, 0.0).astype(BF16)

    def precond_rows(i, carry):
        at = pl.ds(pl.multiple_of(i * FACE, FACE), FACE)
        high = dot(khi[at, 0:NX], tmt[...]).astype(BF16)
        low = klo[at, 0:NX]
        to = pl.ds(pl.multiple_of(NW + i * FACE, 16), FACE)
        m3[to, 0:NX] = high
        m3[to, NX:2 * NX] = high
        m3[to, 2 * NX:] = dot(low, tmt[...]).astype(BF16)
        return carry

    coarse_spread(0, coarse_copy)
    qcopy.wait_recv()
    lax.fori_loop(0, 4, precond_rows, 0)

    for copy in wcopies:
        copy.wait()
    for pos in range(4):
        band = slice(pos * FACE, (pos + 1) * FACE)
        value = wo[band, :] + wr[band, :]
        if keeps[pos] is not None:
            value = jnp.where(keeps[pos], value, 0.0)
        wo[band, :] = value
    high, low = split(wo[...])
    w3[:, 0:LANES] = high
    w3[:, LANES:2 * LANES] = high
    w3[:, 2 * LANES:] = low
    high, low = split(jnp.transpose(wo[...]))
    mhi, mlo = m3[NW:, 0:NX], m3[NW:, 2 * NX:]
    both = dot(jnp.concatenate([high[0:NW], low[0:NW]], axis=0), mhi)
    high, low = split(both[0:NW] + both[NW:] + dot(high[0:NW], mlo))
    m3[0:NW, 0:NX] = high
    m3[0:NW, NX:2 * NX] = high
    m3[0:NW, 2 * NX:] = low

    def operator_end(n, f, copies, use):
        coarse_end(f)
        faces_wait(copies)
        for pos in range(4):
            use(pos, jumped(n, pos, dot(w3[pos * FACE:(pos + 1) * FACE, :], h3[...])))

    def first_use(pos, value):
        rv[pos * FACE:(pos + 1) * FACE, :] = value
        put_x(pos, value)

    operator_end(0, 0, copies, first_use)

    around = (-1, 0, 1, 2)

    halves = (slice(0, cases // 2), slice(cases // 2, cases))

    def precond(n, f):
        block = dot(m3[0:NW + half, :], x3[...])
        pbuf[f] = block[0:NW]
        coarse_begin(f, around)
        tb[n % 2, 0:half, :] = block[NW:]
        copies = [faces_start(n, (0, 1), lanes, h) for h, lanes in enumerate(halves)]
        tb[n % 2, half:, :] = dot(m3[NW + half:, :], x3[...])
        for h, lanes in enumerate(halves):
            copies[h] += faces_start(n, (2, 3), lanes, h)
        return copies

    def operator(n, copies, keep_z):
        out = []
        for h, lanes in enumerate(halves):
            faces_wait(copies[h])
            for pos in range(4):
                value = jumped(n - 1, pos, None, lanes)
                keep_z[pos * FACE:(pos + 1) * FACE, lanes] = value
                put_x(pos, value, lanes)
            tb[n % 2, 0:half, lanes] = dot(a3[0:half, :], x3[:, lanes])
            out += faces_start(n, (0, 1), lanes, h)
            tb[n % 2, half:, lanes] = dot(a3[half:, :], x3[:, lanes])
            out += faces_start(n, (2, 3), lanes, h)
        return out

    def operator_sums(f, qcopy, rz_part, energy, scale):
        coarse_copy = coarse_solve(f)
        energy = energy + jnp.where(rows_of((ncrs, LANES)) == b, coarse_energy(f, qcopy, scale), 0.0)
        late_begin(f, rz_part, energy)
        coarse_spread(f, coarse_copy)
        late_spread(f)

    def total_rz(n):
        return packed(jnp.sum(rv[...] * tb[n % 2], axis=0, keepdims=True))

    def leave(src, dst, n):
        for pos in range(4):
            copy = pltpu.make_async_copy(src.at[pl.ds(pos * FACE, SENT)], dst.at[0, :, ORDER[pos]], osem.at[4 * n + pos])
            copy.start()
            drains.append(copy.wait)

    copies = precond(1, 1)
    rz_part = total_rz(1)
    lax.fori_loop(0, 2, between, 0)
    qcopy = coarse_gather(1, around)

    copies = operator(2, copies, dv)
    tk[...] = tb[0]
    operator_sums(1, qcopy, rz_part, packed(jnp.sum(dv[...] * tk[...], axis=0, keepdims=True)), None)

    def keep_image(pos, value):
        wv[pos * FACE:(pos + 1) * FACE, :] = value

    operator_end(2, 1, copies, keep_image)
    rz_now, energy = late_end(1)
    alpha = unpacked(rz_now / energy)
    for pos in range(4):
        band = slice(pos * FACE, (pos + 1) * FACE)
        value = rv[band, :] - alpha * wv[band, :]
        rv[band, :] = value
        put_x(pos, value)

    copies = precond(3, 2)
    late_begin(0, total_rz(3), jnp.zeros((ncrs, LANES), F32))
    for pos in range(4):
        band = slice(pos * FACE, (pos + 1) * FACE)
        mv[band, :] = alpha * dv[band, :]
    leave(rv, ro, 0)
    leave(mv, mo, 1)
    qcopy = coarse_gather(2, around)
    late_spread(0)

    copies = operator(4, copies, zv)
    rz_next, _ = late_end(0)
    beta = unpacked(rz_next / rz_now)
    co[0:1, :] = beta
    parts = 0.0
    for pos in range(4):
        band = slice(pos * FACE, (pos + 1) * FACE)
        value = zv[band, :] + beta * dv[band, :]
        dv[band, :] = value
        parts = parts + jnp.sum(value * (tb[0, band, :] + beta * tk[band, :]), axis=0, keepdims=True)
    leave(dv, do, 2)
    operator_sums(2, qcopy, jnp.zeros((ncrs, LANES), F32), packed(parts), co)

    def whole_image(pos, value):
        band = slice(pos * FACE, (pos + 1) * FACE)
        wv[band, :] = value + beta * wv[band, :]

    operator_end(4, 2, copies, whole_image)
    leave(wv, wo_out, 3)
    _, energy = late_end(2)
    alpha_out[...] = unpacked(rz_next / energy)

    for drain in drains:
        drain()


def body(face_index, kinv, schur, corner, coarse_inverse, loads):
    nsub = lax.axis_size("sub")
    ncrs = lax.axis_size("crs")
    fdof = face_index.shape[2]
    nrows, cases = loads.shape[1:]
    ncoarse = coarse_inverse.shape[1]
    nface = schur.shape[1]
    ncl = corner.shape[2]
    chips = nsub // 2
    nrp = -(-nrows // 256) * 256
    cbp = -(-coarse_inverse.shape[0] // 16) * 16
    ncp = -(-ncoarse // LANES) * LANES
    vm = pltpu.VMEM
    dma = pltpu.SemaphoreType.DMA
    scratch = [
        vm((nrows, nrows), F32), vm((nrows, cases), F32), vm((ncl, nrows), F32), vm((4, fdof, nface), F32),
        vm(coarse_inverse.shape, F32),
        vm((nrp, nrp), BF16), vm((nrp, nrp), BF16), vm((16, nrp), F32),
        vm((8, NX), jnp.int32), vm((NX, 8), jnp.int32),
        vm((NX, nrp), BF16), vm((nrp, NX), BF16), vm((NA, nrp), BF16), vm((NA, nrp), BF16),
        vm((nrp, cases), BF16), vm((nrp, cases), BF16),
        vm((NX, 3 * NX), BF16), vm((NW + NX, 3 * NX), BF16), vm((NX, 3 * LANES), BF16), vm((3 * NX, cases), BF16),
        vm((32, nrp), F32), vm((cbp, ncp), F32),
        vm((NX, NX), F32), vm((NX, NX), BF16),
        vm((NX, LANES), F32), vm((NX, LANES), F32), vm((NX, LANES), F32),
        vm((ncrs, LANES, LANES), F32), vm((LANES, chips * 24), BF16), vm((LANES, chips * 24), BF16),
        vm((2, NX, cases), F32), vm((2, 4, FACE, cases), F32),
        vm((NX, cases), F32), vm((NX, cases), F32), vm((NX, cases), F32),
        vm((NX, cases), F32), vm((NX, cases), F32), vm((NX, cases), F32),
        vm((3, NW, cases), F32), vm((3, 4 * ncrs, 24, LANES), F32), vm((3, chips, 24, LANES), F32),
        vm((3, LANES, LANES), F32), vm((3, LANES, LANES), F32), vm((LANES, LANES), F32), vm((LANES, LANES), F32),
        vm((2, 24, LANES), F32), vm((3, LANES, cases), F32), vm((3 * LANES, cases), BF16),
        vm((3, 24, LANES), F32), vm((3, 2 * ncrs, 8, LANES), F32), vm((3, chips, 8, LANES), F32),
        vm((8, cases), F32),
        dma((8,)), dma((16,)), dma((4, 4)), dma((4, 4)), dma((4,)), dma((4,)), dma((ncrs,)), dma((ncrs,)),
    ] + [dma((3,)) for _ in range(14)]
    out = jax.ShapeDtypeStruct((1, SENT, 4, cases), F32)
    anyspace = pl.BlockSpec(memory_space=pl.ANY)
    inside = pl.BlockSpec(memory_space=pltpu.VMEM)
    dims = (nsub, ncrs, nrows, fdof, cases, ncoarse)
    first, last, resid, image, alpha = pl.pallas_call(
        functools.partial(kernel, dims),
        out_shape=(out, out, out, out, jax.ShapeDtypeStruct((1, cases), F32)),
        in_specs=[inside] + [anyspace] * 5,
        out_specs=(anyspace, anyspace, anyspace, anyspace, inside),
        scratch_shapes=scratch,
        compiler_params=pltpu.CompilerParams(
            collective_id=0, has_side_effects=True, vmem_limit_bytes=63 * 2**20),
    )(face_index, jnp.swapaxes(kinv, 0, 1), jnp.swapaxes(schur, 0, 1),
      jnp.swapaxes(corner, 1, 2), coarse_inverse, jnp.swapaxes(loads, 0, 1))
    alpha = alpha[:, None, None, :]
    first, last, resid, image = (value[:, 0:fdof] for value in (first, last, resid, image))
    return jnp.swapaxes(first + alpha * last, 1, 2), jnp.swapaxes(resid - alpha * image, 1, 2)


def solution(mesh):
    subs = P(("sub", "crs"), None, None)
    out = P(("sub", "crs"), None, None, None)
    return jax.shard_map(
        body, mesh=mesh, in_specs=(subs, subs, subs, subs, P("crs", None), subs), out_specs=(out, out),
        check_vma=False)
```

```python
import functools

import jax
import jax.numpy as jnp
from jax import lax
from jax.experimental import pallas as pl
from jax.experimental.pallas import tpu as pltpu
from jax.sharding import PartitionSpec as P

F32 = jnp.float32
BF16 = jnp.bfloat16
MESH = pl.DeviceIdType.MESH

FACE = 160
SENT = 152
NX = 4 * FACE
NC = 48
NW = 96
NA = NX + NC
ORDER = (2, 3, 0, 1)
LANES = 128


def dot(left, right):
    return jnp.dot(left, right, preferred_element_type=F32)


def dot_nt(left, right):
    return lax.dot_general(left, right, (((1,), (1,)), ((), ())), preferred_element_type=F32)


def split(value):
    high = value.astype(BF16)
    return high, (value - high.astype(F32)).astype(BF16)


def hot(cond, value=1.0):
    return jnp.where(cond, value, 0.0).astype(BF16)


def rows_of(shape):
    return lax.broadcasted_iota(jnp.int32, shape, 0)


def cols_of(shape):
    return lax.broadcasted_iota(jnp.int32, shape, 1)


def div(value, by):
    return (value * (65536 // by + 1)) >> 16


def kernel(dims, faces, kinv, schur, corner, cinv, loads, mo, do, ro, wo_out, alpha_out,
           kv, lv, cv, sv, civ, khi, klo, tail, idxr, idxc, bmat, bmt, a0hi, a0lo, lhi, llo, a3, m3, w3, x3,
           cpad, cip, sp, tmt, ws, wo, wr, dall, dphi, dplo,
           tb, rb, rv, dv, mv, zv, tk, wv, pw, pbuf, p0, gb, sibs, sibr, hs, hk, qk, hb, h3,
           qs, rr, er, co,
           dsem, osem, fsend, frecv, wsend, wrecv, csend, crecv,
           s1s, s1r, s2s, s2r, bs, br, s3s, s3r, r1s, r1r, r2s, r2r, qsend, qrecv):
    nsub, ncrs, nrows, fdof, cases, ncoarse = dims
    chips = nsub // 2
    nrp = khi.shape[1]
    cblock = ncoarse // ncrs
    cbp, ncp = cip.shape
    a = lax.axis_index("sub")
    b = lax.axis_index("crs")
    k = a >> 1
    c = a & 1
    sib = 2 * k + 1 - c
    up = (a + 1) & (nsub - 1)
    down = (a + nsub - 1) & (nsub - 1)
    left = (b + ncrs - 1) & (ncrs - 1)
    right = (b + 1) & (ncrs - 1)
    dests = ((a, left), (a, right), (down, b), (up, b))
    keeps = (None, None, a > 0, a < nsub - 1)
    drains = []

    def local(src, dst, n):
        return pltpu.make_async_copy(src, dst, dsem.at[n])

    def remote(src, dst, ssem, rsem, dev):
        return pltpu.make_async_remote_copy(
            src_ref=src, dst_ref=dst, send_sem=ssem, recv_sem=rsem, device_id=dev, device_id_type=MESH)

    def settle(ref, sem):
        pltpu.make_async_copy(ref, ref, sem).wait()

    in_copies = [local(corner.at[0], cv, 0), local(cinv, civ, 1), local(loads.at[:, 0], lv, 2),
                 local(kinv.at[:, 0], kv, 3)]
    in_copies += [local(schur.at[pl.ds(ORDER[pos] * fdof, fdof), 0], sv.at[pos], 4 + pos) for pos in range(4)]
    for copy in in_copies:
        copy.start()

    barrier = pltpu.get_barrier_semaphore()
    for j in range(1, ncrs):
        pl.semaphore_signal(barrier, inc=1, device_id=(a, (b + j) & (ncrs - 1)), device_id_type=MESH)
    for j in range(ncrs):
        pl.semaphore_signal(barrier, inc=1, device_id=(up, j), device_id_type=MESH)
        pl.semaphore_signal(barrier, inc=1, device_id=(down, j), device_id_type=MESH)
    for j in range(1, ncrs):
        to = (b + j) & (ncrs - 1)
        pl.semaphore_signal(barrier, inc=1, device_id=((a + 2) & (nsub - 1), to), device_id_type=MESH)
        pl.semaphore_signal(barrier, inc=1, device_id=((a + nsub - 2) & (nsub - 1), to), device_id_type=MESH)

    def greet(j, carry):
        pl.semaphore_signal(barrier, inc=1, device_id=(2 * ((k + j) & (chips - 1)) + c, b), device_id_type=MESH)
        return carry

    lax.fori_loop(1, chips, greet, 0)

    greeted = ncrs - 1 + 2 * ncrs + 2 * (ncrs - 1) + chips - 1

    idxr[...] = jnp.full(idxr.shape, -1, jnp.int32)
    for pos in range(4):
        face = ORDER[pos]
        idxr[0:1, pos * FACE:pos * FACE + fdof] = faces[0, face:face + 1, :]
    idxc[...] = jnp.transpose(idxr[...])
    for pos in range(4):
        sign = 1.0 if pos % 2 else -1.0
        band = slice(pos * FACE, (pos + 1) * FACE)
        bmat[band, :] = hot(idxc[band, 0:1] == cols_of((FACE, nrp)), sign)
    lane = cols_of((1, NX))
    signs = jnp.where(((lane >= FACE) & (lane < 2 * FACE)) | (lane >= 3 * FACE), 1.0, -1.0)

    def build_bmt(i, carry):
        at = pl.multiple_of(i * LANES, LANES)
        rows = rows_of((LANES, NX)) + at
        bmt[pl.ds(at, LANES), :] = jnp.where(idxr[0:1, :] == rows, signs, 0.0).astype(BF16)
        return carry

    lax.fori_loop(0, nrp // LANES, build_bmt, 0)

    for n in range(2):
        for pos in range(4):
            rb[n, pos, SENT:FACE, :] = jnp.zeros((FACE - SENT, cases), F32)
    hb[:, 96:LANES, :] = jnp.zeros((3, 32, cases), F32)
    cpad[...] = jnp.zeros(cpad.shape, F32)
    cip[...] = jnp.zeros(cip.shape, F32)
    sp[...] = jnp.zeros(sp.shape, F32)
    edge = nrp - LANES
    khi[:, edge:] = jnp.zeros((nrp, LANES), BF16)
    klo[:, edge:] = jnp.zeros((nrp, LANES), BF16)
    whole = nrows // 16 * 16
    for ref in (khi, klo, lhi, llo):
        ref[whole:, :] = jnp.zeros((nrp - whole, ref.shape[1]), BF16)
    tail[...] = jnp.zeros(tail.shape, F32)

    in_copies[0].wait()
    ncl = cv.shape[0]
    cpad[0:ncl, 0:nrows] = cv[...]
    chi, clo = split(cpad[...])
    l = cols_of((1, 32))
    da = div(l, 12)
    rem12 = l - 12 * da
    db = div(rem12, 6)
    where_l = jnp.where(l < 24, 24 * da + 6 * ((b + db) & (ncrs - 1)) + rem12 - 6 * db, -1000)
    sel = hot(where_l == rows_of((NC, 32)))
    a0hi[0:NC, :] = dot(sel, chi).astype(BF16)
    a0lo[0:NC, :] = dot(sel, clo).astype(BF16)
    in_copies[2].wait()
    step = 16 * 5

    def split_loads(i, carry):
        at = pl.multiple_of(i * step, step)
        high, low = split(lv[pl.ds(at, step), :])
        lhi[pl.ds(at, step), :] = high
        llo[pl.ds(at, step), :] = low
        return carry

    lax.fori_loop(0, whole // step, split_loads, 0)
    left_rows = nrows - whole
    tail[0:left_rows, 0:cases] = lv[whole:nrows, :]
    high, low = split(tail[:, 0:cases])
    lhi[whole:whole + 16, :] = high
    llo[whole:whole + 16, :] = low

    def apply_loads(lo, hi):
        high, low = a0hi[lo:hi, :], a0lo[lo:hi, :]
        return dot(high, lhi[...]) + dot(high, llo[...]) + dot(low, lhi[...])

    def coarse_begin(f, offs):
        for i, off in enumerate(offs):
            owner = (a + off + nsub) & (nsub - 1)
            for j in range(ncrs):
                to = (b + j) & (ncrs - 1)
                at = pl.ds(pl.multiple_of(to * LANES, LANES), LANES)
                band = pl.ds(24 * i, 24)
                if off == 0 and j == 0:
                    p0[f, i * ncrs + b] = pbuf[f, band, at]
                    continue
                remote(pbuf.at[f, band, at], p0.at[f, i * ncrs + b], s1s.at[f], s1r.at[f], (owner, to)).start()
        drains.append(lambda: settle(p0.at[f, pl.ds(0, ncrs * len(offs) - 1)], s1s.at[f]))

    def coarse_gather(f, offs):
        count = ncrs * len(offs)
        settle(p0.at[f, pl.ds(0, count - 1)], s1r.at[f])
        gb[f, k] = jnp.sum(p0[f, 0:count], axis=0)

        def send(j, carry):
            to = 2 * ((k + j) & (chips - 1)) + c
            remote(gb.at[f, k], gb.at[f, k], s2s.at[f], s2r.at[f], (to, b)).start()
            return carry

        lax.fori_loop(1, chips, send, 0)
        other = remote(gb.at[f, k], qs.at[f], qsend.at[f], qrecv.at[f], (sib, b))
        other.start()
        drains.append(lambda: settle(gb.at[f, pl.ds(0, chips - 1)], s2s.at[f]))
        drains.append(other.wait_send)
        return other

    def coarse_solve(f):
        settle(gb.at[f, pl.ds(0, chips - 1)], s2r.at[f])
        high, low = split(gb[f].reshape(chips * 24, LANES))
        sibs[f] = dot(dphi[...], high) + dot(dphi[...], low) + dot(dplo[...], high)
        copy = remote(sibs.at[f], sibr.at[f], bs.at[f], br.at[f], (sib, b))
        copy.start()
        return copy

    def coarse_spread(f, copy):
        copy.wait()
        at = pl.ds(pl.multiple_of(b * LANES, LANES), LANES)
        hs[...] = sibs[f] + sibr[f]
        hb[f, 0:NW, at] = hs[pl.ds(pl.multiple_of(24 * c, 8), NW), :]
        for j in range(1, ncrs):
            remote(hb.at[f, pl.ds(0, NW), at], hb.at[f, pl.ds(0, NW), at], s3s.at[f], s3r.at[f],
                   (a, (b + j) & (ncrs - 1))).start()
        drains.append(lambda: settle(hb.at[f, pl.ds(0, NW), pl.ds(0, (ncrs - 1) * LANES)], s3s.at[f]))

    def coarse_energy(f, qcopy, scale=None):
        at = pl.ds(pl.multiple_of(b * LANES, LANES), LANES)
        qcopy.wait_recv()
        total, mine, other = sibs[f], gb[f, k], qs[f]
        if scale is not None:
            part = scale[0:1, at]
            total = total + part * hk[...]
            mine = mine + part * qk[0]
            other = other + part * qk[1]
        hk[...] = total
        qk[0] = mine
        qk[1] = other
        mine = hk[pl.ds(pl.multiple_of(24 + 24 * c, 8), 24), :] * mine
        other = hk[pl.ds(pl.multiple_of(48 - 24 * c, 8), 24), :] * other
        return jnp.sum(mine + other, axis=0, keepdims=True)

    def coarse_end(f):
        settle(hb.at[f, pl.ds(0, NW), pl.ds(0, (ncrs - 1) * LANES)], s3r.at[f])
        high, low = split(hb[f])
        h3[0:LANES, :] = high
        h3[LANES:2 * LANES, :] = low
        h3[2 * LANES:, :] = high

    row8 = rows_of((8, LANES))

    def packed(value):
        return jnp.concatenate([value[:, i * LANES:(i + 1) * LANES] for i in range(ncrs)], axis=0)

    def unpacked(value):
        return jnp.concatenate([value[i:i + 1] for i in range(ncrs)], axis=1)

    def late_begin(n, first, second):
        er[n, k] = jnp.concatenate([first, second], axis=0)

        def send(j, carry):
            to = 2 * ((k + j) & (chips - 1)) + c
            remote(er.at[n, k], er.at[n, k], r2s.at[n], r2r.at[n], (to, b)).start()
            return carry

        lax.fori_loop(1, chips, send, 0)
        drains.append(lambda: settle(er.at[n, pl.ds(0, chips - 1)], r2s.at[n]))

    def late_spread(n):
        settle(er.at[n, pl.ds(0, chips - 1)], r2r.at[n])
        mine = rr.at[n, c * ncrs + b]
        rr[n, c * ncrs + b] = jnp.sum(er[n], axis=0)
        for cc in range(2):
            for j in range(ncrs):
                if cc == 0 and j == 0:
                    continue
                dev = (a if cc == 0 else sib, (b + j) & (ncrs - 1))
                remote(mine, mine, r1s.at[n], r1r.at[n], dev).start()
        drains.append(lambda: settle(rr.at[n, pl.ds(0, 2 * ncrs - 1)], r1s.at[n]))

    def late_end(n):
        settle(rr.at[n, pl.ds(0, 2 * ncrs - 1)], r1r.at[n])
        total = jnp.sum(rr[n], axis=0)
        return total[0:ncrs], total[ncrs:]

    def faces_start(n, which, lanes=slice(0, cases), h=0):
        copies = []
        at = pl.ds(lanes.start, lanes.stop - lanes.start)
        for pos in which:
            copy = remote(tb.at[n % 2, pl.ds(pos * FACE, SENT), at], rb.at[n % 2, pos ^ 1, pl.ds(0, SENT), at],
                          fsend.at[2 * (n % 2) + h, pos], frecv.at[2 * (n % 2) + h, pos ^ 1], dests[pos])
            copy.start()
            copies.append(copy)
        return copies

    def faces_wait(copies):
        for copy in copies:
            copy.wait()

    def jumped(n, pos, extra=None, lanes=slice(0, cases)):
        band = slice(pos * FACE, (pos + 1) * FACE)
        value = tb[n % 2, band, lanes] + rb[n % 2, pos, :, lanes]
        if extra is not None:
            value = value + extra
        if keeps[pos] is not None:
            value = jnp.where(keeps[pos], value, 0.0)
        return value

    def put_x(pos, value, lanes=slice(0, cases)):
        high, low = split(value)
        lo = pos * FACE
        x3[lo:lo + FACE, lanes] = high
        x3[NX + lo:NX + lo + FACE, lanes] = low
        x3[2 * NX + lo:2 * NX + lo + FACE, lanes] = high

    both = dot(jnp.concatenate([a0hi[0:NC, :], a0lo[0:NC, :]], axis=0), lhi[...])
    pbuf[0, 0:NC] = both[0:NC] + both[NC:] + dot(a0hi[0:NC, :], llo[...])
    pl.semaphore_wait(barrier, greeted)
    coarse_begin(0, (0, 1))

    in_copies[1].wait()
    cip[0:cblock, 0:ncoarse] = civ[...]
    high, low = split(cip[...])
    i = cols_of((1, cbp))
    r = cblock * b + i
    plane = div(r, 24)
    base = lax.div(lax.div(cblock * b, 24), 2)
    target = 24 * ((plane >> 1) - base) + r - 24 * plane
    target = jnp.where((((plane + 1) & 1) == c) & (i < cblock), target, -1)
    pct = hot(target == rows_of((LANES, cbp)))
    x1h = dot(pct, high).astype(BF16)
    x1l = dot(pct, low).astype(BF16)
    i = rows_of((LANES, 1))
    r = 48 * k - 48 + i
    r = jnp.where((i < 120) & (r < ncoarse), r, -1)
    sel = hot(r == cols_of((LANES, ncp)))
    dall[b] = dot_nt(sel, x1h) + dot_nt(sel, x1l)
    for j in range(1, ncrs):
        remote(dall.at[b], dall.at[b], csend.at[j], crecv.at[j], (a, (b + j) & (ncrs - 1))).start()

    bch = dot_nt(bmat[...], chi).astype(BF16)
    bcl = dot_nt(bmat[...], clo).astype(BF16)
    l = rows_of((32, 1))
    da = div(l, 12)
    rem12 = l - 12 * da
    db = div(rem12, 6)
    where_l = 24 * (1 + da) + 6 * ((b + db) & (ncrs - 1)) + rem12 - 6 * db
    where_l = jnp.where(l < 24, where_l, -1000)
    lanes = cols_of((32, LANES))
    emaps = [hot(where_l + off == lanes) for off in (0, 24, -24)]
    wo[...] = dot(bch, emaps[0]) + dot(bcl, emaps[0])
    ws[0:2 * FACE, :] = wo[0:2 * FACE, :]
    for pos in (2, 3):
        band = slice(pos * FACE, (pos + 1) * FACE)
        ws[band, :] = dot(bch[band], emaps[pos - 1]) + dot(bcl[band], emaps[pos - 1])
    wcopies = [remote(ws.at[pl.ds(pos * FACE, FACE)], wr.at[pl.ds((pos ^ 1) * FACE, FACE)],
                      wsend.at[pos], wrecv.at[pos ^ 1], dests[pos]) for pos in range(4)]
    for copy in wcopies:
        copy.start()

    in_copies[3].wait()

    tail[0:left_rows, 0:nrows] = kv[whole:nrows, :]

    def face_rows(lo, hi):
        def tile(i, carry):
            at = pl.ds(pl.multiple_of(i * 256, 256), 256)
            a0hi[NC + lo:NC + hi, at] = dot(bmat[lo:hi, :], khi[:, at]).astype(BF16)
            a0lo[NC + lo:NC + hi, at] = dot(bmat[lo:hi, :], klo[:, at]).astype(BF16)
            return carry

        lax.fori_loop(0, nrp // 256, tile, 0)

    half = 2 * FACE
    for i in range(nrp // 256):
        at = slice(i * 256, (i + 1) * 256)
        filled = slice(i * 256, min((i + 1) * 256, nrows))
        high, low = split(kv[0:whole, filled])
        khi[0:whole, filled] = high
        klo[0:whole, filled] = low
        high, low = split(tail[:, at])
        khi[whole:whole + 16, at] = high
        klo[whole:whole + 16, at] = low
        a0hi[NC:NC + half, at] = dot(bmat[0:half, :], khi[:, at]).astype(BF16)
        a0lo[NC:NC + half, at] = dot(bmat[0:half, :], klo[:, at]).astype(BF16)
    tb[0, 0:half, :] = apply_loads(NC, NC + half)
    copies = faces_start(0, (0, 1))
    qcopy = coarse_gather(0, (0, 1))
    face_rows(half, NX)
    tb[0, half:NX, :] = apply_loads(NC + half, NC + NX)
    copies += faces_start(0, (2, 3))

    for j in range(1, ncrs):
        copy = remote(dall.at[b], dall.at[b], csend.at[j], crecv.at[j], (a, (b + j) & (ncrs - 1)))
        copy.wait()
    total_hi = total_lo = None
    for blk_b in range(ncrs):
        j = rows_of((LANES, 1))
        pair = div(j, 24)
        rem = j - 24 * pair
        pair = pair + (cblock * blk_b // 24) // 2
        r = 24 * (2 * pair + 1 - c) + rem
        target = jnp.where((j < 120) & (r >= cblock * blk_b) & (r < cblock * (blk_b + 1)),
                           24 * (pair + 1 - c) + rem, -1)
        perm = hot(target == cols_of((LANES, chips * 24)))
        high, low = split(dall[blk_b])
        ph, plo = dot(high, perm), dot(low, perm)
        total_hi = ph if total_hi is None else total_hi + ph
        total_lo = plo if total_lo is None else total_lo + plo
    dphi[...] = total_hi.astype(BF16)
    dplo[...] = total_lo.astype(BF16)

    def between(i, carry):
        at = pl.ds(pl.multiple_of(i * half, half), half)
        src = pl.ds(pl.multiple_of(NC + i * half, 16), half)
        high = dot(a0hi[src, :], bmt[...]).astype(BF16)
        a3[at, 0:NX] = high
        a3[at, NX:2 * NX] = high
        a3[at, 2 * NX:] = dot(a0lo[src, :], bmt[...]).astype(BF16)
        return carry

    coarse_copy = coarse_solve(0)

    nface = sv.shape[2]
    for pos in range(4):
        in_copies[4 + pos].wait()
        sp[pos * FACE:pos * FACE + fdof, 0:nface] = sv[pos] * (0.5 if pos % 2 else -0.5)
    high, low = split(sp[...])
    khi[0:NX, 0:NX] = high
    klo[0:NX, 0:NX] = low
    pos_l = jnp.where(lane >= FACE, 1, 0) + jnp.where(lane >= 2 * FACE, 1, 0) + jnp.where(lane >= 3 * FACE, 1, 0)
    j = lane - FACE * pos_l
    target = jnp.where(j < fdof, j + fdof * ((pos_l + 2) & 3), -1)
    kept = jnp.where(pos_l == 2, jnp.where(a > 0, 0.5, 0.0), jnp.where(pos_l == 3, jnp.where(a < nsub - 1, 0.5, 0.0), 0.5))
    tmt[...] = jnp.where(target == rows_of((NX, NX)), signs * kept, 0.0).astype(BF16)

    def precond_rows(i, carry):
        at = pl.ds(pl.multiple_of(i * FACE, FACE), FACE)
        high = dot(khi[at, 0:NX], tmt[...]).astype(BF16)
        low = klo[at, 0:NX]
        to = pl.ds(pl.multiple_of(NW + i * FACE, 16), FACE)
        m3[to, 0:NX] = high
        m3[to, NX:2 * NX] = high
        m3[to, 2 * NX:] = dot(low, tmt[...]).astype(BF16)
        return carry

    coarse_spread(0, coarse_copy)
    qcopy.wait_recv()
    lax.fori_loop(0, 4, precond_rows, 0)

    for copy in wcopies:
        copy.wait()
    for pos in range(4):
        band = slice(pos * FACE, (pos + 1) * FACE)
        value = wo[band, :] + wr[band, :]
        if keeps[pos] is not None:
            value = jnp.where(keeps[pos], value, 0.0)
        wo[band, :] = value
    high, low = split(wo[...])
    w3[:, 0:LANES] = high
    w3[:, LANES:2 * LANES] = high
    w3[:, 2 * LANES:] = low
    high, low = split(jnp.transpose(wo[...]))
    mhi, mlo = m3[NW:, 0:NX], m3[NW:, 2 * NX:]
    both = dot(jnp.concatenate([high[0:NW], low[0:NW]], axis=0), mhi)
    high, low = split(both[0:NW] + both[NW:] + dot(high[0:NW], mlo))
    m3[0:NW, 0:NX] = high
    m3[0:NW, NX:2 * NX] = high
    m3[0:NW, 2 * NX:] = low

    def operator_end(n, f, copies, use):
        coarse_end(f)
        faces_wait(copies)
        for pos in range(4):
            use(pos, jumped(n, pos, dot(w3[pos * FACE:(pos + 1) * FACE, :], h3[...])))

    def first_use(pos, value):
        rv[pos * FACE:(pos + 1) * FACE, :] = value
        put_x(pos, value)

    operator_end(0, 0, copies, first_use)

    around = (-1, 0, 1, 2)

    halves = (slice(0, cases // 2), slice(cases // 2, cases))

    def precond(n, f):
        block = dot(m3[0:NW + half, :], x3[...])
        pbuf[f] = block[0:NW]
        coarse_begin(f, around)
        tb[n % 2, 0:half, :] = block[NW:]
        copies = [faces_start(n, (0, 1), lanes, h) for h, lanes in enumerate(halves)]
        tb[n % 2, half:, :] = dot(m3[NW + half:, :], x3[...])
        for h, lanes in enumerate(halves):
            copies[h] += faces_start(n, (2, 3), lanes, h)
        return copies

    def operator(n, copies, keep_z):
        out = []
        for h, lanes in enumerate(halves):
            faces_wait(copies[h])
            for pos in range(4):
                value = jumped(n - 1, pos, None, lanes)
                keep_z[pos * FACE:(pos + 1) * FACE, lanes] = value
                put_x(pos, value, lanes)
            tb[n % 2, 0:half, lanes] = dot(a3[0:half, :], x3[:, lanes])
            out += faces_start(n, (0, 1), lanes, h)
            tb[n % 2, half:, lanes] = dot(a3[half:, :], x3[:, lanes])
            out += faces_start(n, (2, 3), lanes, h)
        return out

    def operator_sums(f, qcopy, rz_part, energy, scale):
        coarse_copy = coarse_solve(f)
        energy = energy + jnp.where(rows_of((ncrs, LANES)) == b, coarse_energy(f, qcopy, scale), 0.0)
        late_begin(f, rz_part, energy)
        coarse_spread(f, coarse_copy)
        late_spread(f)

    def total_rz(n):
        return packed(jnp.sum(rv[...] * tb[n % 2], axis=0, keepdims=True))

    def leave(src, dst, n):
        for pos in range(4):
            copy = pltpu.make_async_copy(src.at[pl.ds(pos * FACE, SENT)], dst.at[0, :, ORDER[pos]], osem.at[4 * n + pos])
            copy.start()
            drains.append(copy.wait)

    copies = precond(1, 1)
    rz_part = total_rz(1)
    lax.fori_loop(0, 2, between, 0)
    qcopy = coarse_gather(1, around)

    copies = operator(2, copies, dv)
    tk[...] = tb[0]
    operator_sums(1, qcopy, rz_part, packed(jnp.sum(dv[...] * tk[...], axis=0, keepdims=True)), None)

    def keep_image(pos, value):
        wv[pos * FACE:(pos + 1) * FACE, :] = value

    operator_end(2, 1, copies, keep_image)
    largest = jnp.max(jnp.abs(wv[...]), axis=0, keepdims=True)
    largest = jnp.where(largest > 0.0, largest, 1.0)
    for pos in range(4):
        put_x(pos, wv[pos * FACE:(pos + 1) * FACE, :] / largest)
    block = dot(m3[0:NW + half, :], x3[...])
    pw[...] = block[0:NW]
    zv[0:half, :] = block[NW:]
    zv[half:, :] = dot(m3[NW + half:, :], x3[...])
    rz_now, energy = late_end(1)
    alpha = unpacked(rz_now / energy)

    moved = alpha * largest
    pbuf[2] = pbuf[1] - moved * pw[...]
    coarse_begin(2, around)
    tb[1, 0:half, :] = tb[1, 0:half, :] - moved * zv[0:half, :]
    copies = [faces_start(3, (0, 1), lanes, h) for h, lanes in enumerate(halves)]
    tb[1, half:, :] = tb[1, half:, :] - moved * zv[half:, :]
    for h, lanes in enumerate(halves):
        copies[h] += faces_start(3, (2, 3), lanes, h)
    rv[...] = rv[...] - alpha * wv[...]
    late_begin(0, total_rz(3), jnp.zeros((ncrs, LANES), F32))
    for pos in range(4):
        band = slice(pos * FACE, (pos + 1) * FACE)
        mv[band, :] = alpha * dv[band, :]
    leave(rv, ro, 0)
    leave(mv, mo, 1)
    qcopy = coarse_gather(2, around)
    late_spread(0)

    copies = operator(4, copies, zv)
    rz_next, _ = late_end(0)
    beta = unpacked(rz_next / rz_now)
    co[0:1, :] = beta
    parts = 0.0
    for pos in range(4):
        band = slice(pos * FACE, (pos + 1) * FACE)
        value = zv[band, :] + beta * dv[band, :]
        dv[band, :] = value
        parts = parts + jnp.sum(value * (tb[0, band, :] + beta * tk[band, :]), axis=0, keepdims=True)
    leave(dv, do, 2)
    operator_sums(2, qcopy, jnp.zeros((ncrs, LANES), F32), packed(parts), co)

    def whole_image(pos, value):
        band = slice(pos * FACE, (pos + 1) * FACE)
        wv[band, :] = value + beta * wv[band, :]

    operator_end(4, 2, copies, whole_image)
    leave(wv, wo_out, 3)
    _, energy = late_end(2)
    alpha_out[...] = unpacked(rz_next / energy)

    for drain in drains:
        drain()


def body(face_index, kinv, schur, corner, coarse_inverse, loads):
    nsub = lax.axis_size("sub")
    ncrs = lax.axis_size("crs")
    fdof = face_index.shape[2]
    nrows, cases = loads.shape[1:]
    ncoarse = coarse_inverse.shape[1]
    nface = schur.shape[1]
    ncl = corner.shape[2]
    chips = nsub // 2
    nrp = -(-nrows // 256) * 256
    cbp = -(-coarse_inverse.shape[0] // 16) * 16
    ncp = -(-ncoarse // LANES) * LANES
    vm = pltpu.VMEM
    dma = pltpu.SemaphoreType.DMA
    scratch = [
        vm((nrows, nrows), F32), vm((nrows, cases), F32), vm((ncl, nrows), F32), vm((4, fdof, nface), F32),
        vm(coarse_inverse.shape, F32),
        vm((nrp, nrp), BF16), vm((nrp, nrp), BF16), vm((16, nrp), F32),
        vm((8, NX), jnp.int32), vm((NX, 8), jnp.int32),
        vm((NX, nrp), BF16), vm((nrp, NX), BF16), vm((NA, nrp), BF16), vm((NA, nrp), BF16),
        vm((nrp, cases), BF16), vm((nrp, cases), BF16),
        vm((NX, 3 * NX), BF16), vm((NW + NX, 3 * NX), BF16), vm((NX, 3 * LANES), BF16), vm((3 * NX, cases), BF16),
        vm((32, nrp), F32), vm((cbp, ncp), F32),
        vm((NX, NX), F32), vm((NX, NX), BF16),
        vm((NX, LANES), F32), vm((NX, LANES), F32), vm((NX, LANES), F32),
        vm((ncrs, LANES, LANES), F32), vm((LANES, chips * 24), BF16), vm((LANES, chips * 24), BF16),
        vm((2, NX, cases), F32), vm((2, 4, FACE, cases), F32),
        vm((NX, cases), F32), vm((NX, cases), F32), vm((NX, cases), F32),
        vm((NX, cases), F32), vm((NX, cases), F32), vm((NX, cases), F32),
        vm((NW, cases), F32), vm((3, NW, cases), F32), vm((3, 4 * ncrs, 24, LANES), F32), vm((3, chips, 24, LANES), F32),
        vm((3, LANES, LANES), F32), vm((3, LANES, LANES), F32), vm((LANES, LANES), F32), vm((LANES, LANES), F32),
        vm((2, 24, LANES), F32), vm((3, LANES, cases), F32), vm((3 * LANES, cases), BF16),
        vm((3, 24, LANES), F32), vm((3, 2 * ncrs, 8, LANES), F32), vm((3, chips, 8, LANES), F32),
        vm((8, cases), F32),
        dma((8,)), dma((16,)), dma((4, 4)), dma((4, 4)), dma((4,)), dma((4,)), dma((ncrs,)), dma((ncrs,)),
    ] + [dma((3,)) for _ in range(14)]
    out = jax.ShapeDtypeStruct((1, SENT, 4, cases), F32)
    anyspace = pl.BlockSpec(memory_space=pl.ANY)
    inside = pl.BlockSpec(memory_space=pltpu.VMEM)
    dims = (nsub, ncrs, nrows, fdof, cases, ncoarse)
    first, last, resid, image, alpha = pl.pallas_call(
        functools.partial(kernel, dims),
        out_shape=(out, out, out, out, jax.ShapeDtypeStruct((1, cases), F32)),
        in_specs=[inside] + [anyspace] * 5,
        out_specs=(anyspace, anyspace, anyspace, anyspace, inside),
        scratch_shapes=scratch,
        compiler_params=pltpu.CompilerParams(
            collective_id=0, has_side_effects=True, vmem_limit_bytes=63 * 2**20),
    )(face_index, jnp.swapaxes(kinv, 0, 1), jnp.swapaxes(schur, 0, 1),
      jnp.swapaxes(corner, 1, 2), coarse_inverse, jnp.swapaxes(loads, 0, 1))
    alpha = alpha[:, None, None, :]
    first, last, resid, image = (value[:, 0:fdof] for value in (first, last, resid, image))
    return jnp.swapaxes(first + alpha * last, 1, 2), jnp.swapaxes(resid - alpha * image, 1, 2)


def solution(mesh):
    subs = P(("sub", "crs"), None, None)
    out = P(("sub", "crs"), None, None, None)
    return jax.shard_map(
        body, mesh=mesh, in_specs=(subs, subs, subs, subs, P("crs", None), subs), out_specs=(out, out),
        check_vma=False)
```
